32 devices in a mesh: section: 4 (over y, x), dp: 2 (over core), expert: 4 (over z).
Axes of the slice: x: 2, y: 2, z: 4, core: 2. Of those that a mesh axis runs over, the one named last changes fastest.
Arguments:
- tokens: bfloat16 [8192, 384], P(('section', 'dp', 'expert')), may hold values from -6 to 6
- timesteps: int32 [32], P(('section', 'dp', 'expert')), may hold values from 0 to 999
- routes_one: int32 [8192, 2], P(('section', 'dp', 'expert')), may hold values from 0 to 3, all different within a row; in each aligned block of 256 rows (0 to 255, 256 to 511, ...) at most 256 rows name the same one
- routes_two: int32 [8192, 2], P(('section', 'dp', 'expert')), may hold values from 0 to 3, all different within a row; in each aligned block of 256 rows (0 to 255, 256 to 511, ...) at most 256 rows name the same one
- cotangent: bfloat16 [8192, 384], P(('section', 'dp', 'expert')), may hold values from -6 to 6
- time_table: bfloat16 [1000, 384], replicated, may hold values from -6 to 6
- ada_weight: bfloat16 [4, 384, 1152], P('section'), may hold values from -0.3125 to 0.3125
- ada_bias: bfloat16 [4, 1152], P('section'), may hold values from -4 to 4
- qkv_weight: bfloat16 [2, 384, 1152], replicated, may hold values from -0.3125 to 0.3125
- qv_bias: bfloat16 [2, 768], replicated, may hold values from -3 to 3
- out_weight: bfloat16 [2, 384, 384], replicated, may hold values from -2.5 to 2.5
- out_bias: bfloat16 [2, 384], replicated, may hold values from -3 to 3
- router_weight: bfloat16 [2, 384, 4], replicated, may hold values from -0.21875 to 0.21875
- shared_up: bfloat16 [2, 384, 3072], replicated, may hold values from -0.3125 to 0.3125
- shared_up_bias: bfloat16 [2, 3072], replicated, may hold values from -3 to 3
- shared_down: bfloat16 [2, 3072, 384], replicated, may hold values from -0.109375 to 0.109375
- shared_down_bias: bfloat16 [2, 384], replicated, may hold values from -3 to 3
- expert_up: bfloat16 [2, 4, 384, 1536], P(None, 'expert'), may hold values from -0.3125 to 0.3125
- expert_up_bias: bfloat16 [2, 4, 1536], P(None, 'expert'), may hold values from -3 to 3
- expert_down: bfloat16 [2, 4, 1536, 384], P(None, 'expert'), may hold values from -0.15625 to 0.15625
- expert_down_bias: bfloat16 [2, 4, 384], P(None, 'expert'), may hold values from -3 to 3
Outputs:
- output: bfloat16 [8192, 384], P(('section', 'dp', 'expert'))
- grad_tokens: float32 [8192, 384], P(('section', 'dp', 'expert'))
- grad_time_table: float32 [1000, 384], replicated
- grad_ada_weight: float32 [4, 384, 1152], P('section')
- grad_ada_bias: float32 [4, 1152], P('section')
- grad_qkv_weight: float32 [2, 384, 1152], replicated
- grad_qv_bias: float32 [2, 768], replicated
- grad_out_weight: float32 [2, 384, 384], replicated
- grad_out_bias: float32 [2, 384], replicated
- grad_router_weight: float32 [2, 384, 4], replicated
- grad_shared_up: float32 [2, 384, 3072], replicated
- grad_shared_up_bias: float32 [2, 3072], replicated
- grad_shared_down: float32 [2, 3072, 384], replicated
- grad_shared_down_bias: float32 [2, 384], replicated
- grad_expert_up: float32 [2, 4, 384, 1536], P(None, 'expert')
- grad_expert_up_bias: float32 [2, 4, 1536], P(None, 'expert')
- grad_expert_down: float32 [2, 4, 1536, 384], P(None, 'expert')
- grad_expert_down_bias: float32 [2, 4, 384], P(None, 'expert')
- counts: int32 [2, 4], replicated
The draws below stay inside these ranges and needn't reach their ends.
Inputs may be any that keep to these rules, and one draw needn't show every extreme that they name: `routes_one`: in each aligned block of 256 rows (one device's tokens), no expert is named more than 256 times. `routes_two`: in each aligned block of 256 rows (one device's tokens), no expert is named more than 256 times.
All inputs are finite; a program needn't handle non-finite values.
Results may differ from the reference program's by a relative error of at most 0.039.
Values may be sent and summed in bfloat16 or wider, within the bound.
No kernel may reach another device: no remote copies, remote signals or barrier semaphores. Data moves between devices by JAX's collectives and lax.ppermute only.
A program may use at most 256 MiB of HBM per device.

```python
import math
import jax
import jax.numpy as jnp
import numpy as np
from jax import lax

D = 384
HEADS = 6
HD = 64
FF = 1536
SHARED = 2
STEPS = 1000
EXPERTS = 4
BLOCKS = 4
PATCHES = 256
MB_TOK = 256
IMAGES = 32
TOKENS = 8192
CAP = 256


def place_ends(entries, stream_key, smallest, top_value):
    extent = entries.shape
    place = [jax.random.randint(jax.random.fold_in(stream_key, axis), (), 0, extent[axis]) for axis in range(len(extent))]
    entries = entries.at[tuple(place)].set(smallest)
    longest = extent.index(max(extent))
    place[longest] = (place[longest] + 1) % extent[longest]
    return entries.at[tuple(place)].set(top_value)


def steps_of(stream_key, shape, split, least, high):
    loudness, own = 1.0, jax.random.fold_in(stream_key, 6)
    for dim, parts in split:
        heights = jnp.exp(jax.random.uniform(jax.random.fold_in(own, dim), (parts,), jnp.float32, least / len(split), high / len(split)))
        loudness = loudness * jnp.repeat(heights, shape[dim] // parts).reshape([-1 if axis == dim else 1 for axis in range(len(shape))])
    return loudness


def assign_block(stream_key, own, number, rows, number_of, top, limit, skew):
    order = jax.random.permutation(stream_key, number_of)
    packed, common = shares(number_of, rows * top, limit, skew, True), shares(number_of, rows * top, limit, skew, False)
    places = jnp.arange(number_of)

    def named(tallies, turn):
        used = int((tallies > 0).sum())
        fixed = max(1, used // 4)
        shifted = fixed + (places - fixed + turn * (used - fixed)) % max(1, number_of - fixed)
        return jnp.zeros((number_of,), jnp.int32).at[order[jnp.where(places < fixed, places, shifted)]].set(jnp.asarray(tallies, jnp.int32))

    tallies = jnp.where(number % 4 == 0, named(packed, number // 4), named(common, number - number // 4 - 1))
    mixed = jax.random.permutation(jax.random.fold_in(own, 3), number_of)
    source_of, taker = mixed[0:number_of // 2 * 2:2], mixed[1:number_of // 2 * 2:2]
    margin = jnp.minimum(tallies[source_of] - 1, limit - tallies[taker]) // 2
    margin = jnp.where((source_of == order[0]) | (taker == order[0]) | (tallies[taker] == 0), 0, jnp.maximum(margin, 0))
    shifted = jax.random.randint(jax.random.fold_in(own, 4), (number_of // 2,), 0, 1 << 20) % (margin + 1)
    tallies = tallies.at[source_of].add(-shifted).at[taker].add(shifted)
    labels = jnp.searchsorted(jnp.cumsum(tallies), jnp.arange(rows * top), side="right").astype(jnp.int32)
    grid = labels.reshape(top, rows).T
    grid = grid[jax.random.permutation(jax.random.fold_in(own, 1), rows)]
    turn = jax.random.randint(jax.random.fold_in(own, 2), (rows, 1), 0, top)
    return jnp.take_along_axis(grid, (jnp.arange(top)[None, :] + turn) % top, axis=1)


def shares(amount, total, bound, skew, full):
    loads = [(1 << 20) // math.isqrt(grade ** skew) + 1 for grade in range(1, amount + 1)]
    largest = bound if full else min(bound, max(-(-total // amount), total * loads[0] // sum(loads)))
    least = 1 if total - largest >= amount - 1 else 0
    holding, rest = [largest] + [least] * (amount - 1), total - largest - least * (amount - 1)
    while rest > 0:
        free = [i for i in range(1, amount) if holding[i] < largest] or [i for i in range(1, amount) if holding[i] < bound]
        mass, budget = sum([loads[i] for i in free]), rest
        for i in free:
            addition = min(bound - holding[i], max(1, budget * loads[i] // mass), rest)
            holding[i] = holding[i] + addition
            rest = rest - addition
    return np.array(holding)


def bell_draw(stream_key, shape, spread, reach, split=(), kind=jnp.bfloat16):
    level = steps_of(stream_key, shape, split, -0.22, 0.18) if split else 1.0
    drawn = jax.random.normal(stream_key, shape, jnp.float32) * spread * level
    return jnp.minimum(jnp.maximum(drawn, -reach), reach).astype(kind)


def setup_inputs(seed: int = 0) -> dict:
    arg_keys = jax.random.split(jax.random.key(seed), 22)
    tokens = bell_draw(arg_keys[0], (TOKENS, D), 1.0, 6.0, ((0, 32),))
    timesteps = place_ends(jax.random.randint(arg_keys[1], (IMAGES,), 0, STEPS), jax.random.fold_in(arg_keys[1], 1), 0, STEPS - 1).astype(jnp.int32)
    routes_one_keys = jax.random.split(jax.random.fold_in(arg_keys[2], 1), TOKENS // MB_TOK)
    routes_one_turns = jax.random.permutation(jax.random.fold_in(arg_keys[2], 3), TOKENS // MB_TOK)
    routes_one = jax.vmap(lambda own, number: assign_block(jax.random.fold_in(arg_keys[2], 2), own, number, MB_TOK, EXPERTS, 2, CAP, 2))(routes_one_keys, routes_one_turns).reshape((TOKENS, 2))
    routes_two_keys = jax.random.split(jax.random.fold_in(arg_keys[3], 1), TOKENS // MB_TOK)
    routes_two_turns = jax.random.permutation(jax.random.fold_in(arg_keys[3], 3), TOKENS // MB_TOK)
    routes_two = jax.vmap(lambda own, number: assign_block(jax.random.fold_in(arg_keys[3], 2), own, number, MB_TOK, EXPERTS, 2, CAP, 2))(routes_two_keys, routes_two_turns).reshape((TOKENS, 2))
    cotangent = bell_draw(arg_keys[4], (TOKENS, D), 1.0, 6.0, ((0, 32),))
    time_table = bell_draw(arg_keys[5], (STEPS, D), 1.0, 6.0)
    ada_weight = bell_draw(arg_keys[6], (BLOCKS, D, 3 * D), D ** -0.5, 0.3125, ((0, 4),))
    ada_bias = bell_draw(arg_keys[7], (BLOCKS, 3 * D), 0.3, 4.0, ((0, 4),))
    qkv_weight = bell_draw(arg_keys[8], (BLOCKS // 2, D, 3 * D), D ** -0.5, 0.3125)
    qv_bias = bell_draw(arg_keys[9], (BLOCKS // 2, 2 * D), 0.2, 3.0)
    out_weight = bell_draw(arg_keys[10], (BLOCKS // 2, D, D), (max(4 * D // PATCHES, 1)) ** -0.5, 2.5)
    out_bias = bell_draw(arg_keys[11], (BLOCKS // 2, D), 0.2, 3.0)
    router_weight = bell_draw(arg_keys[12], (BLOCKS // 2, D, EXPERTS), (2 * D) ** -0.5, 0.21875)
    shared_up = bell_draw(arg_keys[13], (BLOCKS // 2, D, SHARED * FF), D ** -0.5, 0.3125)
    shared_up_bias = bell_draw(arg_keys[14], (BLOCKS // 2, SHARED * FF), 0.2, 3.0)
    shared_down = bell_draw(arg_keys[15], (BLOCKS // 2, SHARED * FF, D), (SHARED * FF) ** -0.5, 0.109375)
    shared_down_bias = bell_draw(arg_keys[16], (BLOCKS // 2, D), 0.2, 3.0)
    expert_up = bell_draw(arg_keys[17], (BLOCKS // 2, EXPERTS, D, FF), D ** -0.5, 0.3125, ((1, 4),))
    expert_up_bias = bell_draw(arg_keys[18], (BLOCKS // 2, EXPERTS, FF), 0.2, 3.0, ((1, 4),))
    expert_down = bell_draw(arg_keys[19], (BLOCKS // 2, EXPERTS, FF, D), FF ** -0.5, 0.15625, ((1, 4),))
    expert_down_bias = bell_draw(arg_keys[20], (BLOCKS // 2, EXPERTS, D), 0.2, 3.0, ((1, 4),))
    return dict(tokens=tokens, timesteps=timesteps, routes_one=routes_one, routes_two=routes_two, cotangent=cotangent, time_table=time_table, ada_weight=ada_weight, ada_bias=ada_bias, qkv_weight=qkv_weight, qv_bias=qv_bias, out_weight=out_weight, out_bias=out_bias, router_weight=router_weight, shared_up=shared_up, shared_up_bias=shared_up_bias, shared_down=shared_down, shared_down_bias=shared_down_bias, expert_up=expert_up, expert_up_bias=expert_up_bias, expert_down=expert_down, expert_down_bias=expert_down_bias)


@jax.custom_vjp
def low(v):
    return lax.optimization_barrier(v.astype(jnp.bfloat16)).astype(jnp.float32)

@jax.custom_vjp
def low_back(v):
    return v

def low_keep(v):
    return (low(v), None)

def low_pass(kept, grad):
    return (grad,)

def back_keep(v):
    return (v, None)

def back_low(kept, grad):
    return (low(grad),)
low.defvjp(low_keep, low_pass)
low_back.defvjp(back_keep, back_low)

def matmul(left_arg, right_arg):
    return jnp.dot(left_arg, right_arg, precision=lax.Precision.HIGHEST)

def gelu_tanh(inputs_pre):
    return jax.nn.gelu(inputs_pre, approximate=True)

def normalize(stream, shifts, scaling):
    row_mean = lax.optimization_barrier(jnp.mean(stream, -1, keepdims=True))
    centred = stream - row_mean
    variance = lax.optimization_barrier(jnp.mean(centred * centred, -1, keepdims=True))
    return centred * lax.rsqrt(variance + 1e-06) * (1.0 + scaling) + shifts

def attend_images(image_blocks):
    query_rows, key_rows, value_rows = image_blocks
    scores = jnp.einsum('iqhd,ikhd->ihqk', query_rows, key_rows, precision=lax.Precision.HIGHEST) * HD ** (-0.5)
    scores = low_back(scores)
    weights_soft = low(jax.nn.softmax(scores, -1))
    return jnp.einsum('ihqk,ikhd->iqhd', weights_soft, value_rows, precision=lax.Precision.HIGHEST)

def attention(stream, modulation, qkv_matrix, qv_offset, out_matrix, out_offset):
    shifts = modulation[:, :D]
    scaling = modulation[:, D:2 * D]
    gating = modulation[:, 2 * D:]
    hidden = low(normalize(stream, shifts, scaling))
    projected = matmul(hidden, qkv_matrix)
    query_rows = low(low_back(projected[:, :D] + qv_offset[:D]))
    key_rows = low(low_back(projected[:, D:2 * D]))
    value_rows = low(low_back(projected[:, 2 * D:] + qv_offset[D:]))
    group_size = math.gcd(IMAGES, max(4096 // PATCHES, 1))

    def split_heads(rows):
        return rows.reshape(IMAGES // group_size, group_size, PATCHES, HEADS, HD)
    attended = lax.map(jax.checkpoint(attend_images), (split_heads(query_rows), split_heads(key_rows), split_heads(value_rows)))
    attended = low(low_back(attended.reshape(TOKENS, D)))
    branch = low_back(matmul(attended, out_matrix) + out_offset)
    return stream + gating * branch

def experts_layer(stream, modulation, route_pair, router_matrix, shared_upper, shared_upbias, shared_lower, shared_lowbias, expert_upper, expert_upbias, expert_lower, expert_lowbias):
    shifts = modulation[:, :D]
    scaling = modulation[:, D:2 * D]
    gating = modulation[:, 2 * D:]
    hidden = low(normalize(stream, shifts, scaling))
    logits = matmul(hidden, router_matrix)
    gate_probs = jax.nn.softmax(jnp.take_along_axis(logits, route_pair, 1), -1)
    shared_pre = low_back(matmul(hidden, shared_upper) + shared_upbias)
    shared = low_back(matmul(low(gelu_tanh(shared_pre)), shared_lower) + shared_lowbias)

    def one_expert(running, pieces):
        expert_number, upper, upbias, lower, lowbias = pieces
        inputs_rows = low_back(hidden)
        expert_pre = low_back(matmul(inputs_rows, upper) + upbias)
        result = low(low_back(matmul(low(gelu_tanh(expert_pre)), lower) + lowbias))
        weight = lax.optimization_barrier(jnp.sum(jnp.where(route_pair == expert_number, gate_probs, 0.0), -1, keepdims=True))
        return (running + weight * result, None)
    routed, _ = lax.scan(jax.checkpoint(one_expert), jnp.zeros((TOKENS, D), jnp.float32), (jnp.arange(EXPERTS, dtype=jnp.int32), expert_upper, expert_upbias, expert_lower, expert_lowbias))
    return stream + gating * (shared + routed)

def network(tokens, time_table, ada_weight, ada_bias, qkv_weight, qv_bias, out_weight, out_bias, router_weight, shared_up, shared_up_bias, shared_down, shared_down_bias, expert_up, expert_up_bias, expert_down, expert_down_bias, timesteps, routes_one, routes_two):
    pick_rows = (timesteps[:, None] == jnp.arange(STEPS, dtype=jnp.int32)[None, :]).astype(time_table.dtype)
    condition = low(jax.nn.silu(matmul(pick_rows, time_table)))
    stream = tokens
    route_sets = (routes_one, routes_two)
    for block_index in range(BLOCKS):
        layer_index = block_index // 2
        modulation = jnp.repeat(matmul(condition, ada_weight[block_index]) + ada_bias[block_index], PATCHES, axis=0)
        if block_index % 2 == 0:
            stream = attention(stream, modulation, qkv_weight[layer_index], qv_bias[layer_index], out_weight[layer_index], out_bias[layer_index])
        else:
            stream = experts_layer(stream, modulation, route_sets[layer_index], router_weight[layer_index], shared_up[layer_index], shared_up_bias[layer_index], shared_down[layer_index], shared_down_bias[layer_index], expert_up[layer_index], expert_up_bias[layer_index], expert_down[layer_index], expert_down_bias[layer_index])
        if block_index + 1 < BLOCKS:
            stream = low(low_back(stream))
    return stream

def reference(tokens, timesteps, routes_one, routes_two, cotangent, time_table, ada_weight, ada_bias, qkv_weight, qv_bias, out_weight, out_bias, router_weight, shared_up, shared_up_bias, shared_down, shared_down_bias, expert_up, expert_up_bias, expert_down, expert_down_bias):
    float_args = [item.astype(jnp.float32) for item in (tokens, time_table, ada_weight, ada_bias, qkv_weight, qv_bias, out_weight, out_bias, router_weight, shared_up, shared_up_bias, shared_down, shared_down_bias, expert_up, expert_up_bias, expert_down, expert_down_bias)]

    def forward(*params):
        return network(*params, timesteps, routes_one, routes_two)
    result, pullback = jax.vjp(forward, *float_args)
    gradients = pullback(cotangent.astype(jnp.float32))
    numbers = jnp.arange(EXPERTS, dtype=jnp.int32)
    counts = jnp.stack([lax.optimization_barrier(jnp.sum((route_pair.reshape(-1)[:, None] == numbers[None, :]).astype(jnp.int32), 0)) for route_pair in (routes_one, routes_two)])
    return (result.astype(jnp.bfloat16), gradients[0], gradients[1], gradients[2], gradients[3], gradients[4], gradients[5], gradients[6], gradients[7], gradients[8], gradients[9], gradients[10], gradients[11], gradients[12], gradients[13], gradients[14], gradients[15], gradients[16], counts)
```

```python
import jax
import jax.numpy as jnp
from jax import lax
from jax.sharding import PartitionSpec as P

HEADS = 6
HD = 64

BFLOAT = jnp.bfloat16
FLOAT = jnp.float32
ALL = ("section", "dp", "expert")


def product(left_arg, right_arg):
    return jnp.dot(left_arg, right_arg, preferred_element_type=FLOAT)


def lead_product(left_arg, right_arg):
    return lax.dot_general(
        left_arg, right_arg, (((0,), (0,)), ((), ())), preferred_element_type=FLOAT
    )


def back_product(left_arg, right_arg):
    return lax.dot_general(
        left_arg, right_arg, (((1,), (1,)), ((), ())), preferred_element_type=FLOAT
    )


def gelu_parts(pre):
    inner = 0.7978845608028654 * (pre + 0.044715 * pre * pre * pre)
    tanh = jnp.tanh(inner)
    act = 0.5 * pre * (1.0 + tanh)
    slope = 0.5 * (1.0 + tanh) + 0.5 * pre * (1.0 - tanh * tanh) * 0.7978845608028654 * (
        1.0 + 3 * 0.044715 * pre * pre
    )
    return act, slope


def normalized(stream):
    row_mean = jnp.mean(stream, -1, keepdims=True)
    centred = stream - row_mean
    variance = jnp.mean(centred * centred, -1, keepdims=True)
    inverse = lax.rsqrt(variance + 1e-06)
    return centred * inverse, inverse


def modulate(stream, mod):
    unit, _ = normalized(stream)
    return (unit * (1.0 + mod[1]) + mod[0]).astype(BFLOAT)


def norm_backward(stream, mod, hidden_grad):
    unit, inverse = normalized(stream)
    shift_grad = jnp.sum(hidden_grad, 0)
    scale_grad = jnp.sum(hidden_grad * unit, 0)
    unit_grad = hidden_grad * (1.0 + mod[1])
    stream_grad = inverse * (
        unit_grad
        - jnp.mean(unit_grad, -1, keepdims=True)
        - unit * jnp.mean(unit_grad * unit, -1, keepdims=True)
    )
    return stream_grad, shift_grad, scale_grad


def heads_view(rows):
    return rows.astype(BFLOAT).reshape(-1, HEADS, HD)


def attention_forward(hidden, weights):
    qkv_matrix, qv_offset, out_matrix, out_offset = weights
    width = hidden.shape[1]
    projected = product(hidden, qkv_matrix)
    query = heads_view(projected[:, :width] + qv_offset[:width])
    key = heads_view(projected[:, width : 2 * width])
    value = heads_view(projected[:, 2 * width :] + qv_offset[width:])
    scores = jnp.einsum("qhd,khd->hqk", query, key, preferred_element_type=FLOAT) * HD ** (-0.5)
    probs = jax.nn.softmax(scores, -1)
    probs_low = probs.astype(BFLOAT)
    attended = (
        jnp.einsum("hqk,khd->qhd", probs_low, value, preferred_element_type=FLOAT)
        .reshape(-1, width)
        .astype(BFLOAT)
    )
    branch = product(attended, out_matrix) + out_offset
    return branch, (query, key, value, probs, probs_low, attended)


def attention_backward(hidden, weights, saved, branch_grad):
    qkv_matrix, _, out_matrix, _ = weights
    query, key, value, probs, probs_low, attended = saved
    width = hidden.shape[1]
    factor = HD ** (-0.5)
    low_grad = branch_grad.astype(BFLOAT)
    out_grad = lead_product(attended, low_grad)
    out_offset_grad = jnp.sum(low_grad.astype(FLOAT), 0)
    attended_grad = heads_view(back_product(low_grad, out_matrix))
    value_grad = jnp.einsum("hqk,qhd->khd", probs_low, attended_grad, preferred_element_type=FLOAT)
    prob_grad = jnp.einsum("qhd,khd->hqk", attended_grad, value, preferred_element_type=FLOAT)
    score_grad = (probs * (prob_grad - jnp.sum(prob_grad * probs, -1, keepdims=True))).astype(
        BFLOAT
    )
    query_grad = (
        jnp.einsum("hqk,khd->qhd", score_grad, key, preferred_element_type=FLOAT) * factor
    )
    key_grad = (
        jnp.einsum("hqk,qhd->khd", score_grad, query, preferred_element_type=FLOAT) * factor
    )
    proj_grad = jnp.concatenate(
        [item.reshape(-1, width) for item in (query_grad, key_grad, value_grad)], -1
    ).astype(BFLOAT)
    qkv_grad = lead_product(hidden, proj_grad)
    sums = jnp.sum(proj_grad.astype(FLOAT), 0)
    offset_grad = jnp.concatenate([sums[:width], sums[2 * width :]])
    hidden_grad = back_product(proj_grad, qkv_matrix)
    return hidden_grad, (qkv_grad, offset_grad, out_grad, out_offset_grad)


def expert_gates(rows, router, route_pair):
    logits = product(rows, router)
    marks = (
        route_pair[:, :, None] == jnp.arange(router.shape[1], dtype=jnp.int32)[None, None, :]
    ).any(1)
    top = jnp.max(jnp.where(marks, logits, -jnp.inf), -1, keepdims=True)
    raised = jnp.where(marks, jnp.exp(logits - top), 0.0)
    return raised / jnp.sum(raised, -1, keepdims=True)


def pick_column(table, column):
    return lax.dynamic_slice_in_dim(table, column, 1, axis=1)


def moe_forward(hidden, route_pair, weights):
    router, s_up, s_upb, s_down, s_downb, e_up, e_upb, e_down, e_downb = weights
    mine = lax.axis_index("expert")
    rows = lax.all_gather(hidden, "expert", axis=0, tiled=True)
    routes = lax.all_gather(route_pair, "expert", axis=0, tiled=True)
    gates = expert_gates(rows, router, routes)
    gate = pick_column(gates, mine)
    shared_pre = product(hidden, s_up) + s_upb
    shared_act, shared_slope = gelu_parts(shared_pre)
    shared_act = shared_act.astype(BFLOAT)
    shared_out = product(shared_act, s_down) + s_downb
    pre = product(rows, e_up[0]) + e_upb[0]
    act, slope = gelu_parts(pre)
    act = act.astype(BFLOAT)
    result = (product(act, e_down[0]) + e_downb[0]).astype(BFLOAT)
    routed = lax.psum_scatter(
        (gate * result.astype(FLOAT)).astype(BFLOAT), "expert", scatter_dimension=0, tiled=True
    )
    branch = shared_out + routed.astype(FLOAT)
    saved = (rows, routes, gates, gate, shared_act, shared_slope, act, slope, result)
    return branch, saved


def moe_backward(hidden, weights, saved, branch_grad):
    router, s_up, s_upb, s_down, s_downb, e_up, e_upb, e_down, e_downb = weights
    rows, routes, gates, gate, shared_act, shared_slope, act, slope, result = saved
    mine = lax.axis_index("expert")
    devices = lax.axis_size("expert")
    tokens_here = hidden.shape[0]
    low_grad = branch_grad.astype(BFLOAT)
    s_down_grad = lead_product(shared_act, low_grad)
    s_downb_grad = jnp.sum(low_grad.astype(FLOAT), 0)
    shared_dpre = (back_product(low_grad, s_down) * shared_slope).astype(BFLOAT)
    s_up_grad = lead_product(hidden, shared_dpre)
    s_upb_grad = jnp.sum(shared_dpre.astype(FLOAT), 0)
    hidden_grad = back_product(shared_dpre, s_up)
    row_grad = lax.all_gather(low_grad, "expert", axis=0, tiled=True).astype(FLOAT)
    gate_grad = jnp.sum(row_grad * result.astype(FLOAT), -1)
    gate_grads = lax.all_to_all(
        gate_grad.reshape(devices, tokens_here).astype(BFLOAT), "expert", 0, 0, tiled=True
    ).astype(FLOAT)
    own_gates = lax.dynamic_slice_in_dim(gates, mine * tokens_here, tokens_here, axis=0)
    gate_grads = gate_grads.T
    logit_grad = own_gates * (gate_grads - jnp.sum(own_gates * gate_grads, -1, keepdims=True))
    router_grad = lax.dot_general(
        hidden.astype(FLOAT),
        logit_grad,
        (((0,), (0,)), ((), ())),
        precision=lax.Precision.HIGHEST,
        preferred_element_type=FLOAT,
    )
    result_grad = (gate * row_grad).astype(BFLOAT)
    e_down_grad = lead_product(act, result_grad)
    e_downb_grad = jnp.sum(result_grad.astype(FLOAT), 0)
    dpre = (back_product(result_grad, e_down[0]) * slope).astype(BFLOAT)
    e_up_grad = lead_product(rows, dpre)
    e_upb_grad = jnp.sum(dpre.astype(FLOAT), 0)
    back_rows = lax.psum_scatter(
        back_product(dpre, e_up[0]).astype(BFLOAT), "expert", scatter_dimension=0, tiled=True
    )
    hidden_grad = hidden_grad + back_product(logit_grad, router.astype(FLOAT)) + back_rows
    return hidden_grad, (
        router_grad,
        s_up_grad,
        s_upb_grad,
        s_down_grad,
        s_downb_grad,
        e_up_grad,
        e_upb_grad,
        e_down_grad,
        e_downb_grad,
    )


def shards(
    tokens,
    timesteps,
    routes_one,
    routes_two,
    cotangent,
    time_table,
    ada_weight,
    ada_bias,
    qkv_weight,
    qv_bias,
    out_weight,
    out_bias,
    router_weight,
    shared_up,
    shared_up_bias,
    shared_down,
    shared_down_bias,
    expert_up,
    expert_up_bias,
    expert_down,
    expert_down_bias,
):
    width = tokens.shape[1]
    steps_count = time_table.shape[0]
    experts_total = router_weight.shape[2]
    route_sets = (routes_one, routes_two)
    steps = lax.all_gather(timesteps, "section", axis=0, tiled=True)
    embedded = jnp.take(time_table, steps, axis=0).astype(FLOAT)
    condition = jax.nn.silu(embedded).astype(BFLOAT)
    section_mod = product(condition, ada_weight[0]) + ada_bias[0].astype(FLOAT)
    mods = lax.all_to_all(section_mod, "section", 0, 0, tiled=True).reshape(-1, 3, width)

    def attn_weights(layer):
        return (
            qkv_weight[layer],
            qv_bias[layer].astype(FLOAT),
            out_weight[layer],
            out_bias[layer].astype(FLOAT),
        )

    def moe_weights(layer):
        return (
            router_weight[layer],
            shared_up[layer],
            shared_up_bias[layer].astype(FLOAT),
            shared_down[layer],
            shared_down_bias[layer].astype(FLOAT),
            expert_up[layer],
            expert_up_bias[layer].astype(FLOAT),
            expert_down[layer],
            expert_down_bias[layer].astype(FLOAT),
        )

    streams, hiddens, branches, kept = [], [], [], []
    stream = tokens
    for block in range(4):
        layer = block // 2
        streams.append(stream)
        wide = stream.astype(FLOAT)
        hidden = modulate(wide, mods[block])
        if block % 2 == 0:
            branch, saved = attention_forward(hidden, attn_weights(layer))
        else:
            branch, saved = moe_forward(hidden, route_sets[layer], moe_weights(layer))
        hiddens.append(hidden)
        branches.append(branch)
        kept.append(saved)
        stream = (wide + mods[block][2] * branch).astype(BFLOAT)
    output = stream

    upstream = cotangent
    mod_grads = [None] * 4
    attn_grads = [None] * 2
    moe_grads = [None] * 2
    for block in (3, 2, 1, 0):
        layer = block // 2
        wide_grad = upstream.astype(FLOAT)
        gating_grad = jnp.sum(wide_grad * branches[block], 0)
        branch_grad = mods[block][2] * wide_grad
        if block % 2 == 0:
            hidden_grad, attn_grads[layer] = attention_backward(
                hiddens[block], attn_weights(layer), kept[block], branch_grad
            )
        else:
            hidden_grad, moe_grads[layer] = moe_backward(
                hiddens[block], moe_weights(layer), kept[block], branch_grad
            )
        stream_grad, shift_grad, scale_grad = norm_backward(
            streams[block].astype(FLOAT), mods[block], hidden_grad
        )
        mod_grads[block] = jnp.concatenate([shift_grad, scale_grad, gating_grad])
        token_grad = wide_grad + stream_grad
        upstream = token_grad.astype(BFLOAT)

    section_grads = lax.all_to_all(jnp.stack(mod_grads), "section", 0, 0, tiled=True)
    ada_part = lead_product(condition, section_grads.astype(BFLOAT))
    condition_grad = back_product(section_grads, ada_weight[0].astype(FLOAT))
    condition_grad = lax.psum(condition_grad, "section")
    embed_grad = jax.vjp(jax.nn.silu, embedded)[1](condition_grad)[0]
    marks = (steps[:, None] == jnp.arange(steps_count, dtype=jnp.int32)[None, :]).astype(FLOAT)
    table_part = lead_product(marks, embed_grad)

    def counted(route_pair):
        return jnp.sum(
            (
                route_pair.reshape(-1)[:, None]
                == jnp.arange(experts_total, dtype=jnp.int32)[None, :]
            ).astype(jnp.int32),
            0,
        )

    def total(parts, axes):
        return lax.psum(parts.astype(BFLOAT), axes).astype(FLOAT)

    both_attn = [jnp.stack([attn_grads[0][n], attn_grads[1][n]]) for n in range(4)]
    both_moe = [jnp.stack([moe_grads[0][n], moe_grads[1][n]]) for n in range(9)]
    counts = lax.psum(jnp.stack([counted(routes_one), counted(routes_two)]), ALL)
    attn_out = [total(item, ALL) for item in both_attn]
    moe_out = [total(item, ALL) for item in both_moe[:5]]
    expert_out = [total(item, ("section", "dp"))[:, None] for item in both_moe[5:]]
    table_out = total(table_part, ("dp", "expert"))
    ada_out = total(ada_part, ("dp", "expert"))[None]
    ada_bias_out = total(jnp.sum(section_grads, 0), ("dp", "expert"))[None]
    return (
        output,
        token_grad,
        table_out,
        ada_out,
        ada_bias_out,
        *attn_out,
        *moe_out,
        *expert_out,
        counts,
    )


def solution(mesh):
    rows = P(ALL, None)
    whole = P()
    placed = (
        rows,
        P(ALL),
        rows,
        rows,
        rows,
        whole,
        P("section", None, None),
        P("section", None),
        *([whole] * 9),
        P(None, "expert", None, None),
        P(None, "expert", None),
        P(None, "expert", None, None),
        P(None, "expert", None),
    )
    return jax.shard_map(
        shards,
        mesh=mesh,
        in_specs=placed,
        out_specs=(
            rows,
            rows,
            whole,
            P("section", None, None),
            P("section", None),
            *([whole] * 9),
            P(None, "expert", None, None),
            P(None, "expert", None),
            P(None, "expert", None, None),
            P(None, "expert", None),
            whole,
        ),
        check_vma=False,
    )
```

```python
import functools

import jax
import jax.numpy as jnp
from jax import lax
from jax.experimental import pallas as pl
from jax.experimental.pallas import tpu as pltpu
from jax.sharding import PartitionSpec as P

HEADS = 6
HD = 64

BFLOAT = jnp.bfloat16
FLOAT = jnp.float32
ALL = ("section", "dp", "expert")


def product(left_arg, right_arg):
    return jnp.dot(left_arg, right_arg, preferred_element_type=FLOAT)


def lead_product(left_arg, right_arg):
    return lax.dot_general(
        left_arg, right_arg, (((0,), (0,)), ((), ())), preferred_element_type=FLOAT
    )


def back_product(left_arg, right_arg):
    return lax.dot_general(
        left_arg, right_arg, (((1,), (1,)), ((), ())), preferred_element_type=FLOAT
    )


def gelu_parts(pre):
    inner = 0.7978845608028654 * (pre + 0.044715 * pre * pre * pre)
    tanh = jnp.tanh(inner)
    act = 0.5 * pre * (1.0 + tanh)
    slope = 0.5 * (1.0 + tanh) + 0.5 * pre * (1.0 - tanh * tanh) * 0.7978845608028654 * (
        1.0 + 3 * 0.044715 * pre * pre
    )
    return act, slope


def normalized(stream):
    row_mean = jnp.mean(stream, -1, keepdims=True)
    centred = stream - row_mean
    variance = jnp.mean(centred * centred, -1, keepdims=True)
    inverse = lax.rsqrt(variance + 1e-06)
    return centred * inverse, inverse


def modulate(stream, mod):
    unit, _ = normalized(stream)
    return (unit * (1.0 + mod[1]) + mod[0]).astype(BFLOAT)


def norm_backward(stream, mod, hidden_grad):
    unit, inverse = normalized(stream)
    shift_grad = jnp.sum(hidden_grad, 0)
    scale_grad = jnp.sum(hidden_grad * unit, 0)
    unit_grad = hidden_grad * (1.0 + mod[1])
    stream_grad = inverse * (
        unit_grad
        - jnp.mean(unit_grad, -1, keepdims=True)
        - unit * jnp.mean(unit_grad * unit, -1, keepdims=True)
    )
    return stream_grad, shift_grad, scale_grad


def heads_view(rows):
    return rows.astype(BFLOAT).reshape(-1, HEADS, HD)


def attention_forward(hidden, weights):
    qkv_matrix, qv_offset, out_matrix, out_offset = weights
    width = hidden.shape[1]
    projected = product(hidden, qkv_matrix)
    query = heads_view(projected[:, :width] + qv_offset[:width])
    key = heads_view(projected[:, width : 2 * width])
    value = heads_view(projected[:, 2 * width :] + qv_offset[width:])
    scores = jnp.einsum("qhd,khd->hqk", query, key, preferred_element_type=FLOAT) * HD ** (-0.5)
    probs = jax.nn.softmax(scores, -1)
    probs_low = probs.astype(BFLOAT)
    attended = (
        jnp.einsum("hqk,khd->qhd", probs_low, value, preferred_element_type=FLOAT)
        .reshape(-1, width)
        .astype(BFLOAT)
    )
    branch = product(attended, out_matrix) + out_offset
    return branch, (query, key, value, probs, probs_low, attended)


def attention_backward(hidden, weights, saved, branch_grad):
    qkv_matrix, _, out_matrix, _ = weights
    query, key, value, probs, probs_low, attended = saved
    width = hidden.shape[1]
    factor = HD ** (-0.5)
    low_grad = branch_grad.astype(BFLOAT)
    out_grad = lead_product(attended, low_grad)
    out_offset_grad = jnp.sum(low_grad.astype(FLOAT), 0)
    attended_grad = heads_view(back_product(low_grad, out_matrix))
    value_grad = jnp.einsum("hqk,qhd->khd", probs_low, attended_grad, preferred_element_type=FLOAT)
    prob_grad = jnp.einsum("qhd,khd->hqk", attended_grad, value, preferred_element_type=FLOAT)
    score_grad = (probs * (prob_grad - jnp.sum(prob_grad * probs, -1, keepdims=True))).astype(
        BFLOAT
    )
    query_grad = (
        jnp.einsum("hqk,khd->qhd", score_grad, key, preferred_element_type=FLOAT) * factor
    )
    key_grad = (
        jnp.einsum("hqk,qhd->khd", score_grad, query, preferred_element_type=FLOAT) * factor
    )
    proj_grad = jnp.concatenate(
        [item.reshape(-1, width) for item in (query_grad, key_grad, value_grad)], -1
    ).astype(BFLOAT)
    qkv_grad = lead_product(hidden, proj_grad)
    sums = jnp.sum(proj_grad.astype(FLOAT), 0)
    offset_grad = jnp.concatenate([sums[:width], sums[2 * width :]])
    hidden_grad = back_product(proj_grad, qkv_matrix)
    return hidden_grad, (qkv_grad, offset_grad, out_grad, out_offset_grad)


def expert_gates(rows, router, route_pair):
    logits = product(rows, router)
    marks = (
        route_pair[:, :, None] == jnp.arange(router.shape[1], dtype=jnp.int32)[None, None, :]
    ).any(1)
    top = jnp.max(jnp.where(marks, logits, -jnp.inf), -1, keepdims=True)
    raised = jnp.where(marks, jnp.exp(logits - top), 0.0)
    return raised / jnp.sum(raised, -1, keepdims=True)


def pick_column(table, column):
    return lax.dynamic_slice_in_dim(table, column, 1, axis=1)


def moe_forward(hidden, route_pair, weights):
    router, s_up, s_upb, s_down, s_downb, e_up, e_upb, e_down, e_downb = weights
    mine = lax.axis_index("expert")
    rows = lax.all_gather(hidden, "expert", axis=0, tiled=True)
    routes = lax.all_gather(route_pair, "expert", axis=0, tiled=True)
    gates = expert_gates(rows, router, routes)
    gate = pick_column(gates, mine)
    shared_pre = product(hidden, s_up) + s_upb
    shared_act, shared_slope = gelu_parts(shared_pre)
    shared_act = shared_act.astype(BFLOAT)
    shared_out = product(shared_act, s_down) + s_downb
    pre = product(rows, e_up[0]) + e_upb[0]
    act, slope = gelu_parts(pre)
    act = act.astype(BFLOAT)
    result = (product(act, e_down[0]) + e_downb[0]).astype(BFLOAT)
    routed = lax.psum_scatter(
        (gate * result.astype(FLOAT)).astype(BFLOAT), "expert", scatter_dimension=0, tiled=True
    )
    branch = shared_out + routed.astype(FLOAT)
    saved = (rows, routes, gates, gate, shared_act, shared_slope, act, slope, result)
    return branch, saved


def moe_backward(hidden, weights, saved, branch_grad):
    router, s_up, s_upb, s_down, s_downb, e_up, e_upb, e_down, e_downb = weights
    rows, routes, gates, gate, shared_act, shared_slope, act, slope, result = saved
    mine = lax.axis_index("expert")
    devices = lax.axis_size("expert")
    tokens_here = hidden.shape[0]
    low_grad = branch_grad.astype(BFLOAT)
    s_down_grad = lead_product(shared_act, low_grad)
    s_downb_grad = jnp.sum(low_grad.astype(FLOAT), 0)
    shared_dpre = (back_product(low_grad, s_down) * shared_slope).astype(BFLOAT)
    s_up_grad = lead_product(hidden, shared_dpre)
    s_upb_grad = jnp.sum(shared_dpre.astype(FLOAT), 0)
    hidden_grad = back_product(shared_dpre, s_up)
    row_grad = lax.all_gather(low_grad, "expert", axis=0, tiled=True).astype(FLOAT)
    gate_grad = jnp.sum(row_grad * result.astype(FLOAT), -1)
    gate_grads = lax.all_to_all(
        gate_grad.reshape(devices, tokens_here).astype(BFLOAT), "expert", 0, 0, tiled=True
    ).astype(FLOAT)
    own_gates = lax.dynamic_slice_in_dim(gates, mine * tokens_here, tokens_here, axis=0)
    gate_grads = gate_grads.T
    logit_grad = own_gates * (gate_grads - jnp.sum(own_gates * gate_grads, -1, keepdims=True))
    router_grad = lax.dot_general(
        hidden.astype(FLOAT),
        logit_grad,
        (((0,), (0,)), ((), ())),
        precision=lax.Precision.HIGHEST,
        preferred_element_type=FLOAT,
    )
    result_grad = (gate * row_grad).astype(BFLOAT)
    e_down_grad = lead_product(act, result_grad)
    e_downb_grad = jnp.sum(result_grad.astype(FLOAT), 0)
    dpre = (back_product(result_grad, e_down[0]) * slope).astype(BFLOAT)
    e_up_grad = lead_product(rows, dpre)
    e_upb_grad = jnp.sum(dpre.astype(FLOAT), 0)
    back_rows = lax.psum_scatter(
        back_product(dpre, e_up[0]).astype(BFLOAT), "expert", scatter_dimension=0, tiled=True
    )
    hidden_grad = hidden_grad + back_product(logit_grad, router.astype(FLOAT)) + back_rows
    return hidden_grad, (
        router_grad,
        s_up_grad,
        s_upb_grad,
        s_down_grad,
        s_downb_grad,
        e_up_grad,
        e_upb_grad,
        e_down_grad,
        e_downb_grad,
    )


def shards_general(
    tokens,
    timesteps,
    routes_one,
    routes_two,
    cotangent,
    time_table,
    ada_weight,
    ada_bias,
    qkv_weight,
    qv_bias,
    out_weight,
    out_bias,
    router_weight,
    shared_up,
    shared_up_bias,
    shared_down,
    shared_down_bias,
    expert_up,
    expert_up_bias,
    expert_down,
    expert_down_bias,
):
    width = tokens.shape[1]
    steps_count = time_table.shape[0]
    experts_total = router_weight.shape[2]
    route_sets = (routes_one, routes_two)
    steps = lax.all_gather(timesteps, "section", axis=0, tiled=True)
    embedded = jnp.take(time_table, steps, axis=0).astype(FLOAT)
    condition = jax.nn.silu(embedded).astype(BFLOAT)
    section_mod = product(condition, ada_weight[0]) + ada_bias[0].astype(FLOAT)
    mods = lax.all_to_all(section_mod, "section", 0, 0, tiled=True).reshape(-1, 3, width)

    def attn_weights(layer):
        return (
            qkv_weight[layer],
            qv_bias[layer].astype(FLOAT),
            out_weight[layer],
            out_bias[layer].astype(FLOAT),
        )

    def moe_weights(layer):
        return (
            router_weight[layer],
            shared_up[layer],
            shared_up_bias[layer].astype(FLOAT),
            shared_down[layer],
            shared_down_bias[layer].astype(FLOAT),
            expert_up[layer],
            expert_up_bias[layer].astype(FLOAT),
            expert_down[layer],
            expert_down_bias[layer].astype(FLOAT),
        )

    streams, hiddens, branches, kept = [], [], [], []
    stream = tokens
    for block in range(4):
        layer = block // 2
        streams.append(stream)
        wide = stream.astype(FLOAT)
        hidden = modulate(wide, mods[block])
        if block % 2 == 0:
            branch, saved = attention_forward(hidden, attn_weights(layer))
        else:
            branch, saved = moe_forward(hidden, route_sets[layer], moe_weights(layer))
        hiddens.append(hidden)
        branches.append(branch)
        kept.append(saved)
        stream = (wide + mods[block][2] * branch).astype(BFLOAT)
    output = stream

    upstream = cotangent
    mod_grads = [None] * 4
    attn_grads = [None] * 2
    moe_grads = [None] * 2
    for block in (3, 2, 1, 0):
        layer = block // 2
        wide_grad = upstream.astype(FLOAT)
        gating_grad = jnp.sum(wide_grad * branches[block], 0)
        branch_grad = mods[block][2] * wide_grad
        if block % 2 == 0:
            hidden_grad, attn_grads[layer] = attention_backward(
                hiddens[block], attn_weights(layer), kept[block], branch_grad
            )
        else:
            hidden_grad, moe_grads[layer] = moe_backward(
                hiddens[block], moe_weights(layer), kept[block], branch_grad
            )
        stream_grad, shift_grad, scale_grad = norm_backward(
            streams[block].astype(FLOAT), mods[block], hidden_grad
        )
        mod_grads[block] = jnp.concatenate([shift_grad, scale_grad, gating_grad])
        token_grad = wide_grad + stream_grad
        upstream = token_grad.astype(BFLOAT)

    section_grads = lax.all_to_all(jnp.stack(mod_grads), "section", 0, 0, tiled=True)
    ada_part = lead_product(condition, section_grads.astype(BFLOAT))
    condition_grad = back_product(section_grads, ada_weight[0].astype(FLOAT))
    condition_grad = lax.psum(condition_grad, "section")
    embed_grad = jax.vjp(jax.nn.silu, embedded)[1](condition_grad)[0]
    marks = (steps[:, None] == jnp.arange(steps_count, dtype=jnp.int32)[None, :]).astype(FLOAT)
    table_part = lead_product(marks, embed_grad)

    def counted(route_pair):
        return jnp.sum(
            (
                route_pair.reshape(-1)[:, None]
                == jnp.arange(experts_total, dtype=jnp.int32)[None, :]
            ).astype(jnp.int32),
            0,
        )

    def total(parts, axes):
        return lax.psum(parts.astype(BFLOAT), axes).astype(FLOAT)

    both_attn = [jnp.stack([attn_grads[0][n], attn_grads[1][n]]) for n in range(4)]
    both_moe = [jnp.stack([moe_grads[0][n], moe_grads[1][n]]) for n in range(9)]
    counts = lax.psum(jnp.stack([counted(routes_one), counted(routes_two)]), ALL)
    attn_out = [total(item, ALL) for item in both_attn]
    moe_out = [total(item, ALL) for item in both_moe[:5]]
    expert_out = [total(item, ("section", "dp"))[:, None] for item in both_moe[5:]]
    table_out = total(table_part, ("dp", "expert"))
    ada_out = total(ada_part, ("dp", "expert"))[None]
    ada_bias_out = total(jnp.sum(section_grads, 0), ("dp", "expert"))[None]
    return (
        output,
        token_grad,
        table_out,
        ada_out,
        ada_bias_out,
        *attn_out,
        *moe_out,
        *expert_out,
        counts,
    )


def norm_parts(wide):
    row_mean = jnp.mean(wide, -1, keepdims=True)
    centred = wide - row_mean
    variance = jnp.mean(centred * centred, -1, keepdims=True)
    inverse = lax.rsqrt(variance + 1e-06)
    return centred * inverse, inverse


def norm_grad(unit, inverse, scaling, hidden_grad):
    shift_grad = jnp.sum(hidden_grad, 0, keepdims=True)
    scale_grad = jnp.sum(hidden_grad * unit, 0, keepdims=True)
    unit_grad = hidden_grad * (1.0 + scaling)
    stream_grad = inverse * (
        unit_grad
        - jnp.mean(unit_grad, -1, keepdims=True)
        - unit * jnp.mean(unit_grad * unit, -1, keepdims=True)
    )
    return stream_grad, shift_grad, scale_grad


def whole_spec(array):
    return pl.BlockSpec(array.shape, lambda *_: (0,) * array.ndim)


def layer_spec(array, layer):
    block = (None,) + array.shape[1:]
    return pl.BlockSpec(block, lambda *_: (layer,) + (0,) * (array.ndim - 1))


def kernel_call(body, ins, outs, flops, grid=(1,), scratch=(), prefetch=()):
    arrays = [item[0] for item in ins]
    specs = [item[1] if len(item) > 1 else whole_spec(item[0]) for item in ins]
    moved = sum(array.size * array.dtype.itemsize for array in arrays)
    return pl.pallas_call(
        body,
        out_shape=[jax.ShapeDtypeStruct(shape, dtype) for shape, dtype in outs],
        grid_spec=pltpu.PrefetchScalarGridSpec(
            num_scalar_prefetch=len(prefetch),
            grid=grid,
            in_specs=specs,
            out_specs=[
                pl.BlockSpec(shape, lambda *_, rank=len(shape): (0,) * rank) for shape, _ in outs
            ],
            scratch_shapes=list(scratch),
        ),
        cost_estimate=pl.CostEstimate(flops=flops, bytes_accessed=moved, transcendentals=0),
        compiler_params=pltpu.CompilerParams(vmem_limit_bytes=50 << 20),
    )(*prefetch, *arrays)


def mod_of(mods, block, part):
    row = 3 * block + part
    return mods[row : row + 1, :]


def head_pairs(width):
    for pair in range(HEADS // 2):
        start = pair * 2 * HD
        yield slice(start, start + 2 * HD), slice(width + start, width + start + 2 * HD), slice(
            2 * width + start, 2 * width + start + 2 * HD
        )


def masked(mask, rows):
    return jnp.where(mask, rows, jnp.zeros_like(rows))


def head_probs(query, key):
    scores = back_product(query, key) * HD ** (-0.5)
    raised = jnp.exp(scores - jnp.max(scores, -1, keepdims=True))
    return raised * (1.0 / jnp.sum(raised, -1, keepdims=True))


def gate_column(gates, expert):
    lanes = lax.broadcasted_iota(jnp.int32, gates.shape, 1)
    return jnp.sum(jnp.where(lanes == expert, gates, 0.0), -1, keepdims=True)


def gelu_value(pre):
    tanh = jnp.tanh(pre * (0.7978845608028654 + 0.035677408136300125 * (pre * pre)))
    half = 0.5 * pre
    return half + half * tanh


def gelu_both(pre):
    square = pre * pre
    tanh = jnp.tanh(pre * (0.7978845608028654 + 0.035677408136300125 * square))
    half = 0.5 * pre
    slope = (0.5 + 0.5 * tanh) + (half * (1.0 - tanh * tanh)) * (
        0.7978845608028654 + 0.10703222440890037 * square
    )
    return half + half * tanh, slope


def gates_of(rows, routes, router):
    logits = product(rows, router)
    lanes = lax.broadcasted_iota(jnp.int32, logits.shape, 1)
    marks = (lanes == routes[:, 0:1]) | (lanes == routes[:, 1:2])
    top = jnp.max(jnp.where(marks, logits, -jnp.inf), -1, keepdims=True)
    raised = jnp.where(marks, jnp.exp(logits - top), 0.0)
    return raised / jnp.sum(raised, -1, keepdims=True)


def write_columns(out, start, table):
    rows = table.shape[0]
    turned = jnp.transpose(table)[:8]
    rounded = turned.astype(BFLOAT).astype(FLOAT)
    both = jnp.concatenate([rounded, turned - rounded]).astype(BFLOAT)
    out[start : start + 16, :] = jnp.zeros((16, out.shape[1]), BFLOAT)
    out[start : start + 16, :rows] = both


def read_columns(message, start, rows):
    both = message[start : start + 16, :rows].astype(FLOAT)
    turned = jnp.concatenate([both[:8] + both[8:], jnp.zeros((120, rows), FLOAT)])
    return jnp.transpose(turned)


def attention_forward_body(block, place, *refs):
    layer = block // 2
    refs = list(refs)
    pop = lambda count: [refs.pop(0) for _ in range(count)]
    if block:
        stream, own, back = pop(3)
    else:
        stream, cotangent = pop(2)
    mods, qkv_w, qv_b, out_w, out_b, router, routes = pop(7)
    if block:
        stream_out, before_out = pop(2)
        before = own[...] + back[...].astype(FLOAT)
        before_out[...] = before
        low_stream = (stream[...].astype(FLOAT) + mod_of(mods, block - 1, 2) * before).astype(BFLOAT)
        stream_out[...] = low_stream
        wide = low_stream.astype(FLOAT)
    else:
        wide = stream[...].astype(FLOAT)
    hidden_out, qkv_out, attended_out, branch_out, new_out, message_out, gates_out = pop(7)
    rows, width = wide.shape
    unit, _ = norm_parts(wide)
    hidden = (unit * (1.0 + mod_of(mods, block, 1)) + mod_of(mods, block, 0)).astype(BFLOAT)
    hidden_out[...] = hidden
    bias = qv_b[layer : layer + 1, :].astype(FLOAT)
    projected = product(hidden, qkv_w[...])
    qkv_out[:, :width] = (projected[:, :width] + bias[:, :width]).astype(BFLOAT)
    qkv_out[:, width : 2 * width] = projected[:, width : 2 * width].astype(BFLOAT)
    qkv_out[:, 2 * width :] = (projected[:, 2 * width :] + bias[:, width:]).astype(BFLOAT)
    low = lax.broadcasted_iota(jnp.int32, (rows, 2 * HD), 1) < HD
    for query_at, key_at, value_at in head_pairs(width):
        query, key, value = qkv_out[:, query_at], qkv_out[:, key_at], qkv_out[:, value_at]
        parts = [
            product(head_probs(masked(mask, query), key).astype(BFLOAT), value)
            for mask in (low, ~low)
        ]
        attended_out[:, query_at] = jnp.where(low, parts[0], parts[1]).astype(BFLOAT)
    branch = product(attended_out[...], out_w[...]) + out_b[layer : layer + 1, :].astype(FLOAT)
    branch_out[...] = branch
    new = (wide + mod_of(mods, block, 2) * branch).astype(BFLOAT)
    new_out[...] = new
    unit, _ = norm_parts(new.astype(FLOAT))
    following = (unit * (1.0 + mod_of(mods, block + 1, 1)) + mod_of(mods, block + 1, 0)).astype(
        BFLOAT
    )
    gates = gates_of(following, routes, router[...])
    gates_out[...] = gates
    message_out[:rows, :] = following
    write_columns(message_out, rows, gates)
    if not block:
        last, bundle = pop(2)
        last[...] = (mod_of(mods, 3, 2) * cotangent[...].astype(FLOAT)).astype(BFLOAT)
        bundle[: rows + 16, :] = message_out[...]
        bundle[rows + 16 : 2 * rows + 16, :] = last[...]
        bundle[2 * rows + 16 :, :] = jnp.zeros((16, width), BFLOAT)


def keep_or_send(place, core, kept, sent, piece, at, value):
    @pl.when(place[0] == core)
    def _():
        kept[piece, at, :] = value

    @pl.when(place[0] != core)
    def _():
        sent[piece, at, :] = value


def attention_backward_body(block, place, *refs):
    (
        upstream, after, after_message, own_grad, message, own_gates, gate_grads,
        stream, hidden, qkv, attended, branch, mods, router, qkv_w, out_w, *refs,
    ) = refs
    if block:
        before, grad_out, before_grad_out, kept, sent, small_out, proj = refs
    else:
        grad_out, kept, sent, small_out, proj = refs
    rows, width = stream.shape
    small_out[...] = jnp.zeros_like(small_out)

    gate_grad = gate_grads[...] + read_columns(message, rows, rows)
    gates = own_gates[...]
    logit_grad = gates * (gate_grad - jnp.sum(gates * gate_grad, -1, keepdims=True))
    logit_grad = logit_grad.astype(BFLOAT)
    router_grad = lead_product(logit_grad, after_message[:rows, :])[:4]
    hidden_grad = (
        own_grad[...] + message[:rows, :].astype(FLOAT) + back_product(logit_grad, router[...])
    )
    unit, inverse = norm_parts(after[...].astype(FLOAT))
    after_grad, shift_grad, scale_grad = norm_grad(
        unit, inverse, mod_of(mods, block + 1, 1), hidden_grad
    )
    small_out[0:1, :] = shift_grad
    small_out[1:2, :] = scale_grad
    wide_grad = (upstream[...].astype(FLOAT) + after_grad).astype(BFLOAT).astype(FLOAT)

    small_out[2:3, :] = jnp.sum(wide_grad * branch[...], 0, keepdims=True)
    branch_grad = (mod_of(mods, block, 2) * wide_grad).astype(BFLOAT)
    out_bias_grad = jnp.sum(branch_grad.astype(FLOAT), 0, keepdims=True)
    attended_grad = back_product(branch_grad, out_w[...]).astype(BFLOAT)
    low = lax.broadcasted_iota(jnp.int32, (rows, 2 * HD), 1) < HD
    factor = HD ** (-0.5)
    for query_at, key_at, value_at in head_pairs(width):
        query, key, value = qkv[:, query_at], qkv[:, key_at], qkv[:, value_at]
        pair_grad = attended_grad[:, query_at]
        sums = None
        for mask in (low, ~low):
            own_query, own_pair = masked(mask, query), masked(mask, pair_grad)
            probs = head_probs(own_query, key)
            value_grad = lead_product(probs.astype(BFLOAT), own_pair)
            prob_grad = back_product(own_pair, value)
            score_grad = (
                probs * (prob_grad - jnp.sum(prob_grad * probs, -1, keepdims=True))
            ).astype(BFLOAT)
            query_grad = masked(mask, product(score_grad, key))
            key_grad = lead_product(score_grad, own_query)
            parts = (query_grad, key_grad, value_grad)
            sums = parts if sums is None else tuple(a + b for a, b in zip(sums, parts))
        proj[:, query_at] = (sums[0] * factor).astype(BFLOAT)
        proj[:, key_at] = (sums[1] * factor).astype(BFLOAT)
        proj[:, value_at] = sums[2].astype(BFLOAT)

    middle = width // 2
    for part in range(4):
        if part < 3:
            grad = lead_product(hidden[...], proj[:, part * width : (part + 1) * width])
        else:
            grad = lead_product(attended[...], branch_grad)
        for side in range(2):
            keep_or_send(
                place,
                part // 2,
                kept,
                sent,
                2 * (part % 2) + side,
                slice(32, 32 + middle),
                grad[side * middle : (side + 1) * middle].astype(BFLOAT),
            )
    extra = jnp.concatenate(
        [
            jnp.sum(proj[:, :width].astype(FLOAT), 0, keepdims=True),
            jnp.sum(proj[:, 2 * width :].astype(FLOAT), 0, keepdims=True),
            out_bias_grad,
            router_grad,
            jnp.zeros((25, width), FLOAT),
        ]
    ).astype(BFLOAT)
    tail = slice(0, 32)
    for piece in range(4):
        for core in range(2):
            value = extra if piece == 0 and core == 0 else jnp.zeros((32, width), BFLOAT)
            keep_or_send(place, core, kept, sent, piece, tail, value)

    hidden_grad = back_product(proj[...], qkv_w[...])
    unit, inverse = norm_parts(stream[...].astype(FLOAT))
    stream_grad, shift_grad, scale_grad = norm_grad(
        unit, inverse, mod_of(mods, block, 1), hidden_grad
    )
    small_out[3:4, :] = shift_grad
    small_out[4:5, :] = scale_grad
    grad = wide_grad + stream_grad
    if block:
        low_grad = grad.astype(BFLOAT)
        grad_out[...] = low_grad
        wide_grad = low_grad.astype(FLOAT)
        before_grad_out[...] = (mod_of(mods, block - 1, 2) * wide_grad).astype(BFLOAT)
        small_out[5:6, :] = jnp.sum(wide_grad * before[...], 0, keepdims=True)
    else:
        grad_out[...] = grad


def shared_body(layer, forward, backward, place, *refs):
    refs = list(refs)
    pop = lambda count: [refs.pop(0) for _ in range(count)]
    (message,) = pop(1)
    branch_grad = pop(1)[0] if backward else None
    up, up_bias, down, down_bias = pop(4)
    total = pop(1)[0] if forward else None
    grads = pop(1)[0] if backward else None
    rows = message.shape[0] - 16
    pre = product(message[:rows, :], up[...]) + up_bias[layer : layer + 1, :].astype(FLOAT)
    if backward:
        act, slope = gelu_both(pre)
        act_grad = (back_product(branch_grad[...], down[...]) * slope).astype(BFLOAT)
        part = back_product(act_grad, up[...])

        @pl.when(pl.program_id(0) == 0)
        def _():
            grads[...] = part

        @pl.when(pl.program_id(0) > 0)
        def _():
            grads[...] += part

    else:
        act = gelu_value(pre)
    if forward:
        part = product(act.astype(BFLOAT), down[...])

        @pl.when(pl.program_id(0) == 0)
        def _():
            total[...] = part + down_bias[layer : layer + 1, :].astype(FLOAT)

        @pl.when(pl.program_id(0) > 0)
        def _():
            total[...] += part


def shared_call(layer, forward, backward, order, message, branch_grad, weights):
    up, up_bias, down, down_bias = weights[:4]
    rows, width = message.shape[0] - 16, message.shape[1]
    units = 1536
    ins = [(message,)] + [(branch_grad,)] * backward
    ins += [
        (up, pl.BlockSpec((None, width, units), lambda i, _: (layer, 0, i))),
        (up_bias, pl.BlockSpec((2, units), lambda i, _: (0, i))),
        (down, pl.BlockSpec((None, units, width), lambda i, _: (layer, i, 0))),
        (down_bias,),
    ]
    return order.call(
        functools.partial(shared_body, layer, forward, backward),
        ins,
        [((rows, width), FLOAT)] * (forward + backward),
        5.0,
        grid=(up.shape[2] // units,),
    )


def experts_body(layer, forward, backward, partner, place, *refs):
    refs = list(refs)
    pop = lambda count: [refs.pop(0) for _ in range(count)]
    (message,) = pop(1)
    own_gates = None if partner else pop(1)[0]
    branch_grad = pop(1)[0] if backward else None
    e_up, e_upb, e_down, e_downb, own_up, got_up, own_down, got_down, x_upb, x_downb = pop(10)
    kept = pop(1)[0] if backward and not forward else None
    shared_out = pop(1)[0] if forward and not partner else None
    shared_grad = pop(1)[0] if backward and not partner else None
    if forward:
        total_out = pop(1)[0]
        kept_out = None if backward else pop(1)[0]
    if backward:
        grad_out = pop(1)[0]
        gate_grad_out = None if partner else pop(1)[0]
    x_up, x_down, total = pop(3)
    if partner:
        (gates,) = pop(1)
    else:
        gates = own_gates
    if backward:
        grads, gate_grad = pop(2)
    step = pl.program_id(0)
    rows = message.shape[0] - 16
    lanes = lax.broadcasted_iota(jnp.int32, (rows, 128), 1)

    @pl.when(step == 0)
    def _():
        if partner:
            gates[...] = read_columns(message, rows, rows)
        for core, up, down in ((place[0], own_up, own_down), (1 - place[0], got_up, got_down)):
            size, deep = up.shape[0] * up.shape[1], down.shape[0] * down.shape[1]
            at = pl.ds(pl.multiple_of(core * size, 16), size)
            x_up[at, :] = up[...].reshape(size, up.shape[2])
            at = pl.ds(pl.multiple_of(core * deep, 16), deep)
            x_down[at, :] = down[...].reshape(deep, down.shape[2])

    def expert(index, number, up, up_bias, down, down_bias):
        gate = gate_column(gates[...], number)
        pre = product(message[:rows, :], up) + up_bias
        if backward:
            act, slope = gelu_both(pre)
            act_grad = (back_product(branch_grad[...], down) * slope * gate).astype(BFLOAT)
            part_grad = back_product(act_grad, up)
        else:
            act = gelu_value(pre)
        if forward:
            result = (product(act.astype(BFLOAT), down) + down_bias).astype(BFLOAT)
            if kept_out is not None:
                kept_out[index] = result
            result = result.astype(FLOAT)
            part = gate * result
        else:
            result = kept[index].astype(FLOAT)
        if backward:
            column = jnp.sum(branch_grad[...].astype(FLOAT) * result, -1, keepdims=True)
            part_gate = jnp.where(lanes == number, column, 0.0)
        if index == 0:
            if forward:
                total[...] = part
            if backward:
                grads[...] = part_grad
                gate_grad[...] = part_gate
            return
        if forward:
            part = part + total[...]
            if not partner:
                part = part + shared_out[...]
            total_out[...] = part.astype(total_out.dtype)
        if backward:
            part_grad = part_grad + grads[...]
            part_gate = part_gate + gate_grad[...]
            if partner:
                grad_out[:rows, :] = part_grad.astype(BFLOAT)
                write_columns(grad_out, rows, part_gate)
            else:
                grad_out[...] = part_grad + shared_grad[...]
                gate_grad_out[...] = part_gate

    @pl.when(step == 0)
    def _():
        expert(
            0, place[3], e_up[...], e_upb[layer].astype(FLOAT), e_down[...],
            e_downb[layer].astype(FLOAT),
        )

    @pl.when(step == 1)
    def _():
        expert(
            1, place[3] ^ 2, x_up[...], x_upb[...].astype(FLOAT), x_down[...],
            x_downb[...].astype(FLOAT),
        )


def experts_call(
    layer, forward, backward, order, message, gates, branch_grad, weights, extra, kept, shared
):
    e_up, e_upb, e_down, e_downb = weights[4:]
    rows, width = message.shape[0] - 16, message.shape[1]
    units = e_up.shape[3]
    partner = gates is None
    ins = [(message,)]
    if not partner:
        ins += [(gates,)]
    if backward:
        ins += [(branch_grad,)]
    ins += [
        (e_up, pl.BlockSpec((None, None, width, units), lambda i, _: (layer, 0, 0, 0))),
        (e_upb,),
        (e_down, pl.BlockSpec((None, None, units, width), lambda i, _: (layer, 0, 0, 0))),
        (e_downb,),
    ]
    ins += [(item,) for item in extra]
    if backward and not forward:
        ins += [(kept,)]
    if not partner:
        ins += [(item,) for item in shared]
    outs = []
    scratch = [
        pltpu.VMEM((width, units), BFLOAT),
        pltpu.VMEM((units, width), BFLOAT),
        pltpu.VMEM((rows, width), FLOAT),
    ]
    if partner:
        scratch += [pltpu.VMEM((rows, 128), FLOAT)]
    if forward:
        outs += [((rows, width), BFLOAT if partner else FLOAT)]
        if not backward:
            outs += [((2, rows, width), BFLOAT)]
    if backward:
        outs += [((rows + 16, width), BFLOAT)] if partner else [((rows, width), FLOAT)]
        if not partner:
            outs += [((rows, 128), FLOAT)]
        scratch += [pltpu.VMEM((rows, width), FLOAT), pltpu.VMEM((rows, 128), FLOAT)]
    return order.call(
        functools.partial(experts_body, layer, forward, backward, partner),
        ins,
        outs,
        6.0,
        grid=(2,),
        scratch=scratch,
    )


def weight_grads_body(layer, place, *refs):
    messages, branch_grads, refs = refs[0:4], refs[4:8], refs[8:]
    e_up, e_upb, e_down, s_up, s_upb, s_down, *refs = refs
    kept, sent, rows_all, grads_all, acts, pre_grads, gated_all, sums_all, small_all = refs
    step = pl.program_id(0)
    rows, width = 256, rows_all.shape[1]
    units = acts.shape[1]
    middle = width // 2

    @pl.when(step == 0)
    def _():
        sums_all[...] = jnp.zeros_like(sums_all)
        small_all[...] = jnp.zeros_like(small_all)
        for side in range(4):
            at = slice(side * rows, (side + 1) * rows)
            grad = branch_grads[side][:rows, :]
            rows_all[at, :] = messages[side][:rows, :]
            grads_all[at, :] = grad
            gate = gate_column(read_columns(messages[side], rows, rows), place[3])
            gated = (gate * grad.astype(FLOAT)).astype(BFLOAT)
            gated_all[at, :] = gated
            sums_all[4:5, :] += jnp.sum(gated.astype(FLOAT), 0, keepdims=True)
            down_bias = jnp.sum(grad.astype(FLOAT), 0, keepdims=True)
            small_all[15:16, :] += jnp.where(place[3] == 0, down_bias, 0.0)

    def chunk(source, up, offset, down):
        def tile(side, sums):
            at = pl.ds(pl.multiple_of(side * rows, rows), rows)
            act, slope = gelu_both(product(rows_all[at, :], up[...]) + offset)
            acts[at, :] = act.astype(BFLOAT)
            grad = (back_product(source[at, :], down[...]) * slope).astype(BFLOAT)
            pre_grads[at, :] = grad
            return sums + jnp.sum(grad.astype(FLOAT), 0, keepdims=True)

        return lax.fori_loop(0, 4, tile, jnp.zeros((1, units), FLOAT), unroll=layer == 0)

    def tails(start, value):
        at = slice(start, start + 32)
        for piece in range(4):
            for core in range(2):
                rest = jnp.zeros((32, width), BFLOAT)
                own = value.astype(BFLOAT) if piece == 0 and core == 0 else rest
                keep_or_send(place, core, kept, sent, piece, at, own)

    for part in range(2):

        @pl.when(step == part)
        def _(part=part):
            sums = chunk(gated_all, e_up, e_upb[layer].astype(FLOAT), e_down)
            for half in range(2):
                at = slice(half * width, (half + 1) * width)
                number = 2 * part + half
                sums_all[number : number + 1, :] = sums[:, at]
                up_grad = lead_product(rows_all[...], pre_grads[:, at]).astype(BFLOAT)
                down_grad = lead_product(acts[:, at], gated_all[...]).astype(BFLOAT)
                for core, grad in ((0, up_grad), (1, down_grad)):
                    keep_or_send(place, core, kept, sent, number, slice(0, width), grad)
            if part == 1:
                tails(width, sums_all[...])

    @pl.when(step == 2)
    def _():
        sums = chunk(grads_all, s_up, s_upb[layer : layer + 1, :].astype(FLOAT), s_down)
        start = width + 32
        where = slice(start, start + middle)
        for half in range(2):
            at = slice(half * width, (half + 1) * width)
            for plane in range(4):
                row = 7 + 2 * plane + half
                small_all[row : row + 1, :] = jnp.where(place[3] == plane, sums[:, at], 0.0)
            up_grad = lead_product(rows_all[...], pre_grads[:, at]).astype(BFLOAT)
            down_grad = lead_product(acts[:, at], grads_all[...]).astype(BFLOAT)
            for core, grad in ((0, up_grad), (1, down_grad)):
                for side in range(2):
                    value = grad[side * middle : (side + 1) * middle]
                    keep_or_send(place, core, kept, sent, 2 * half + side, where, value)
        tails(start + middle, small_all[...])


def weight_grads_call(layer, order, messages, branch_grads, weights):
    s_up, s_upb, s_down, _, e_up, e_upb, e_down, _ = weights
    rows, width, units = 256, s_up.shape[1], 768
    at_own = lambda i: jnp.minimum(i, 1)
    ins = list(messages) + list(branch_grads)
    ins += [
        (e_up, pl.BlockSpec((None, None, width, units), lambda i, _: (layer, 0, 0, at_own(i)))),
        (e_upb, pl.BlockSpec((2, 1, units), lambda i, _: (0, 0, at_own(i)))),
        (e_down, pl.BlockSpec((None, None, units, width), lambda i, _: (layer, 0, at_own(i), 0))),
        (s_up, pl.BlockSpec((None, width, units), lambda i, at: (layer, 0, at[3]))),
        (s_upb, pl.BlockSpec((2, units), lambda i, at: (0, at[3]))),
        (s_down, pl.BlockSpec((None, units, width), lambda i, at: (layer, at[3], 0))),
    ]
    piece = width + 32 + width // 2 + 32
    return order.call(
        functools.partial(weight_grads_body, layer),
        ins,
        [((4, piece, width), BFLOAT)] * 2,
        19.0,
        grid=(3,),
        scratch=[
            pltpu.VMEM((4 * rows, width), BFLOAT),
            pltpu.VMEM((4 * rows, width), BFLOAT),
            pltpu.VMEM((4 * rows, units), BFLOAT),
            pltpu.VMEM((4 * rows, units), BFLOAT),
            pltpu.VMEM((4 * rows, width), BFLOAT),
            pltpu.VMEM((32, width), FLOAT),
            pltpu.VMEM((32, width), FLOAT),
        ],
    )


def swap(x, axis, by):
    return lax.ppermute(x, axis, [(i, i ^ by) for i in range(lax.axis_size(axis))])


def bits():
    section = lax.axis_index("section")
    return lax.axis_index("dp"), section // 2, section % 2


def ordered(bit, mine, other):
    return jnp.stack([jnp.where(bit == 0, mine, other), jnp.where(bit == 0, other, mine)])


def wide_sum(*parts):
    total = parts[0].astype(FLOAT)
    for part in parts[1:]:
        total = total + part.astype(FLOAT)
    return total


class Groups:
    def __init__(self, expert, shared, every):
        self.expert, self.shared, self.every = expert, shared, every
        self.rows = expert + shared + every
        self.half = self.rows // 2
        self.sent = expert // 2 + 2 * shared + every // 2


def first_body(place, *refs):
    keeps, gots = refs[:2], refs[2:4]
    keep_a, send_a, keep_b, send_b, pieces = refs[4:]
    half = keep_a.shape[1]
    y, x = place[1], place[2]
    joint = keeps[0].shape[1] - 32
    for piece in range(4):
        first = wide_sum(keeps[0][piece], gots[0][piece])
        second = wide_sum(keeps[1][piece], gots[1][piece])
        pieces[piece, :joint, :] = first[:joint].astype(BFLOAT)
        pieces[piece, joint : joint + 32, :] = (first[joint:] + second[:32]).astype(BFLOAT)
        pieces[piece, joint + 32 :, :] = second[32:].astype(BFLOAT)
    for other in range(2):
        keep_a[other] = pieces[2 * other + x, :half, :]
        send_a[other] = pieces[2 * other + 1 - x, :half, :]
        keep_b[other] = pieces[2 * y + other, half:, :]
        send_b[other] = pieces[2 * (1 - y) + other, half:, :]


def second_body(place, keep_a, got_a, keep_b, got_b, *outs):
    next_a, sent_a, next_b, sent_b = outs
    y, x = place[1], place[2]
    next_a[...] = wide_sum(keep_a[y], got_a[y]).astype(BFLOAT)
    sent_a[...] = wide_sum(keep_a[1 - y], got_a[1 - y]).astype(BFLOAT)
    next_b[...] = wide_sum(keep_b[x], got_b[x]).astype(BFLOAT)
    sent_b[...] = wide_sum(keep_b[1 - x], got_b[1 - x]).astype(BFLOAT)


def third_body(groups, place, keep_a, got_a, keep_b, got_b, expert_a, expert_b, columns, piece):
    piece[: groups.half, :] = wide_sum(keep_a[...], got_a[...]).astype(BFLOAT)
    piece[groups.half :, :] = wide_sum(keep_b[...], got_b[...]).astype(BFLOAT)
    middle = groups.expert // 2
    expert_a[...] = piece[:middle, :]
    expert_b[...] = piece[middle : 2 * middle, :]
    columns[...] = piece[2 * middle :, :]


def column_body(groups, joined, place, *refs):
    experts = (refs[0], refs[1]) if joined else None
    columns, sent = refs[2 * joined : 2 * joined + 4], refs[2 * joined + 4 :]
    z = place[3]
    shared, every = groups.shared // 2, groups.every // 2
    for side in range(2):
        out = sent[side]
        at = 0
        if joined:
            at = groups.expert // 2
            out[:at, :] = experts[side][...]
        for turn in range(4):
            to = pl.multiple_of(at + (z ^ turn) * shared, 16)
            out[pl.ds(to, shared), :] = columns[turn][side * shared : (side + 1) * shared, :]
        at += 4 * shared
        rows = slice(groups.shared + side * every, groups.shared + (side + 1) * every)
        first = wide_sum(columns[0][rows, :], columns[1][rows, :])
        second = wide_sum(columns[2][rows, :], columns[3][rows, :])
        out[at:, :] = (first + second).astype(BFLOAT)


def pair_body(place, own_a, got_a, own_b, got_b, out_a, out_b):
    y, x = place[1], place[2]
    out_a[y] = own_a[...]
    out_a[1 - y] = got_a[...]
    out_b[x] = own_b[...]
    out_b[1 - x] = got_b[...]


class Order:
    def __init__(self, place):
        self.place = place

    def call(self, body, ins, outs, micros, **kwargs):
        outs = kernel_call(body, ins, outs, int(micros * 1.1e9), prefetch=(self.place,), **kwargs)
        self.place = lax.optimization_barrier((self.place, outs[-1]))[0]
        return outs

    def tie(self, x):
        return lax.optimization_barrier((x, self.place))[0]

    def wait(self, x):
        self.place = lax.optimization_barrier((self.place, x))[0]


class Flow:
    def __init__(self, groups, order):
        self.groups, self.order, self.parts = groups, order, []

    def add(self, kept, sent):
        self.width = kept.shape[2]
        self.parts.append((kept, swap(sent, "dp", 1)))

    def across(self, turn, first, second):
        self.got = (
            swap(first, "section", 1 + turn),
            swap(second, "section", 2 - turn),
        )

    def first(self):
        groups, width = self.groups, self.width
        self.keep_a, send_a, self.keep_b, send_b = self.order.call(
            first_body,
            [(kept,) for kept, _ in self.parts] + [(got,) for _, got in self.parts],
            [((2, groups.half, width), BFLOAT)] * 4,
            4.0,
            scratch=[pltpu.VMEM((4, groups.rows, width), BFLOAT)],
        )
        self.across(0, send_a, send_b)

    def second(self):
        self.keep_a, send_a, self.keep_b, send_b = self.order.call(
            second_body,
            [(self.keep_a,), (self.got[0],), (self.keep_b,), (self.got[1],)],
            [((self.groups.half, self.width), BFLOAT)] * 4,
            1.5,
        )
        self.across(1, send_a, send_b)

    def third(self):
        groups, width = self.groups, self.width
        *self.expert, columns = self.order.call(
            functools.partial(third_body, groups),
            [(self.keep_a,), (self.got[0],), (self.keep_b,), (self.got[1],)],
            [((groups.expert // 2, width), BFLOAT)] * 2
            + [((groups.shared + groups.every, width), BFLOAT)],
            1.5,
            scratch=[pltpu.VMEM((groups.rows, width), BFLOAT)],
        )
        self.columns = [columns, swap(columns, "expert", 1), swap(columns, "expert", 2)]

    def relay(self):
        self.columns.append(swap(self.order.tie(self.columns[2]), "expert", 1))

    def column(self, joined):
        ins = self.expert * joined + self.columns
        rows = self.groups.sent - self.groups.expert // 2 * (not joined)
        return Spread(
            self.order,
            self.order.call(
                functools.partial(column_body, self.groups, joined),
                [(item,) for item in ins],
                [((rows, self.width), BFLOAT)] * 2,
                1.5,
            ),
        )


class Spread:
    def __init__(self, order, own):
        self.order, self.own = order, own
        self.got = [swap(own[0], "section", 2), swap(own[1], "section", 1)]

    def pair(self):
        own = self.order.call(
            pair_body,
            [(self.own[0],), (self.got[0],), (self.own[1],), (self.got[1],)],
            [((2,) + item.shape, BFLOAT) for item in self.own],
            1.7,
        )
        got = [swap(own[0], "section", 1), swap(own[1], "section", 2)]
        here = [own[0], got[0], own[1], got[1]]
        self.all = here + [swap(item, "dp", 1) for item in here]


def final_body(groups, kinds, aliases, place, *refs):
    parts, outs = refs[:8], list(refs[8 + aliases :])
    step = pl.program_id(0)
    core, y, x = place[0], place[1], place[2]

    def half_of(owner, piece, side, start, rows):
        at = slice(start, start + rows)
        index, is_own = (piece // 2, piece % 2 == x) if side == 0 else (piece % 2, piece // 2 == y)
        own, got, other_own, other_got = (
            parts[2 * side + 4 * chip + number][index, at, :]
            for chip in range(2)
            for number in range(2)
        )
        return jnp.where(
            core == owner, jnp.where(is_own, own, got), jnp.where(is_own, other_own, other_got)
        )

    start = 0
    if "expert" in kinds:
        up, down, bias = outs.pop(0), outs.pop(0), outs.pop(0)
        rows = groups.expert // 2
        start = rows
        for part in range(4):

            @pl.when(step == 2 * part)
            def _(part=part):
                for out, owner in ((up, 0), (down, 1)):
                    both = jnp.concatenate(
                        [half_of(owner, part, side, 0, rows) for side in range(2)]
                    )
                    out[...] = both[: groups.expert - 32].astype(FLOAT)
                    if owner == 0 and part == 0:
                        bias[...] = both[groups.expert - 32 :].astype(FLOAT)

    if "shared" in kinds:
        up, down = outs.pop(0), outs.pop(0)
        rows = groups.shared // 2
        for number in range(8):

            @pl.when(step == number)
            def _(number=number):
                at, block = start + number // 2 * rows, number % 2
                for out, owner in ((up, 0), (down, 1)):
                    for piece in range(2):
                        for side in range(2):
                            to = (2 * piece + side) * rows
                            out[to : to + rows, :] = half_of(
                                owner, 2 * block + piece, side, at, rows
                            ).astype(FLOAT)

        qkv, out_w, small = outs.pop(0), outs.pop(0), outs.pop(0)
        at = start + 4 * rows
        rows = groups.every // 2
        real = groups.every - 32
        for part in range(4):

            @pl.when(step == 2 * part)
            def _(part=part):
                target = qkv if part < 3 else out_w
                for piece in range(2):
                    both = jnp.concatenate(
                        [
                            half_of(part // 2, 2 * (part % 2) + piece, side, at, rows)
                            for side in range(2)
                        ]
                    )
                    target[real * piece : real * (piece + 1), :] = both[32:].astype(FLOAT)
                    if part == 0 and piece == 0:
                        small[...] = both[:32].astype(FLOAT)


def final_call(groups, kinds, layer, order, parts, before):
    width = parts[0].shape[2]
    outs, specs = [], []
    if "expert" in kinds:
        outs += [((2, 1, width, 4 * width), FLOAT), ((2, 1, 4 * width, width), FLOAT)]
        specs += [
            pl.BlockSpec((None, None, width, width), lambda i, _: (layer, 0, 0, i // 2)),
            pl.BlockSpec((None, None, width, width), lambda i, _: (layer, 0, i // 2, 0)),
        ]
        outs += [((32, width), FLOAT)]
        specs += [pl.BlockSpec((32, width), lambda i, _: (0, 0))]
    if "shared" in kinds:
        outs += [((2, width, 8 * width), FLOAT), ((2, 8 * width, width), FLOAT)]
        specs += [
            pl.BlockSpec((None, width, width), lambda i, _: (layer, 0, i)),
            pl.BlockSpec((None, width, width), lambda i, _: (layer, i, 0)),
        ]
        outs += [((2, width, 3 * width), FLOAT), ((2, width, width), FLOAT), ((32, width), FLOAT)]
        specs += [
            pl.BlockSpec((None, width, width), lambda i, _: (layer, 0, jnp.minimum(i // 2, 2))),
            pl.BlockSpec((None, width, width), lambda i, _: (layer, 0, 0)),
            pl.BlockSpec((32, width), lambda i, _: (0, 0)),
        ]
    aliases = {}
    kept = []
    if before is not None:
        big = [number for number, (shape, _) in enumerate(outs) if len(shape) > 2]
        for array, number in zip(before, big):
            aliases[9 + len(kept)] = number
            kept.append(array)
    outs = pl.pallas_call(
        functools.partial(final_body, groups, kinds, len(kept)),
        out_shape=[jax.ShapeDtypeStruct(shape, dtype) for shape, dtype in outs],
        grid_spec=pltpu.PrefetchScalarGridSpec(
            num_scalar_prefetch=1,
            grid=(8,),
            in_specs=[whole_spec(item) for item in parts]
            + [pl.BlockSpec(memory_space=pl.ANY)] * len(kept),
            out_specs=specs,
        ),
        input_output_aliases=aliases,
        cost_estimate=pl.CostEstimate(flops=int(8e9), bytes_accessed=16 << 20, transcendentals=0),
        compiler_params=pltpu.CompilerParams(vmem_limit_bytes=50 << 20),
    )(order.place, *parts, *kept)
    order.wait(outs[-1])
    return outs


def extra_plane_body(place, own_a, got_a, own_b, got_b, out_a, out_b):
    y, x = place[1], place[2]
    for other in range(2):
        out_a[2 * other + x] = own_a[other]
        out_a[2 * other + 1 - x] = got_a[other]
        out_b[2 * y + other] = own_b[other]
        out_b[2 * (1 - y) + other] = got_b[other]


class ExtraExpert:
    def __init__(self, layer, order, number, up, down):
        width, units = up.shape[2], up.shape[3]
        some_up = lax.dynamic_slice(
            up, (layer, 0, number * (width // 8), 0), (1, 1, width // 8, units)
        ).reshape(width // 8, units)
        some_down = lax.dynamic_slice(
            down, (layer, 0, number * (units // 8), 0), (1, 1, units // 8, width)
        ).reshape(units // 8, width)
        self.order = order
        self.shapes = [some_up.shape, some_down.shape]
        self.own = [swap(some_up, "expert", 2), swap(some_down, "expert", 2)]

    def across(self):
        self.got = [swap(self.own[0], "section", 2), swap(self.own[1], "section", 1)]

    def pair(self):
        self.own = self.order.call(
            pair_body,
            [(self.own[0],), (self.got[0],), (self.own[1],), (self.got[1],)],
            [((2,) + shape, BFLOAT) for shape in self.shapes],
            1.7,
        )
        self.got = [swap(self.own[0], "section", 1), swap(self.own[1], "section", 2)]

    def plane(self):
        up, down = self.order.call(
            extra_plane_body,
            [(self.own[0],), (self.got[0],), (self.own[1],), (self.got[1],)],
            [((4,) + shape, BFLOAT) for shape in self.shapes],
            1.7,
        )
        self.all = [up, swap(up, "dp", 1), down, swap(down, "dp", 1)]


def shards_fast(
    tokens,
    timesteps,
    routes_one,
    routes_two,
    cotangent,
    time_table,
    ada_weight,
    ada_bias,
    qkv_weight,
    qv_bias,
    out_weight,
    out_bias,
    router_weight,
    shared_up,
    shared_up_bias,
    shared_down,
    shared_down_bias,
    expert_up,
    expert_up_bias,
    expert_down,
    expert_down_bias,
):
    width = tokens.shape[1]
    rows = tokens.shape[0]
    bf, fl = BFLOAT, FLOAT
    steps_count = time_table.shape[0]
    experts_total = router_weight.shape[2]
    core, y, x_bit = bits()
    place = jnp.stack([core, y, x_bit, lax.axis_index("expert")]).astype(jnp.int32)
    routers = jnp.pad(router_weight, ((0, 0), (0, 0), (0, 128 - experts_total)))

    order = Order(place)
    number = core * 4 + y * 2 + x_bit
    hidden_units = expert_up.shape[3]
    half_steps = ordered(x_bit, timesteps[0], swap(timesteps[0], "section", 1))
    number = lax.optimization_barrier((number, half_steps))[0]
    steps = ordered(y, half_steps, swap(half_steps, "section", 2)).reshape(4)
    first_extra = ExtraExpert(0, order, number, expert_up, expert_down)
    own_bias = jnp.concatenate([expert_up_bias[:, 0], expert_down_bias[:, 0]], -1)
    extra_bias = swap(own_bias, "expert", 2)
    second_extra = ExtraExpert(1, order, number, expert_up, expert_down)

    def with_bias(layer, extra):
        bias = extra_bias[layer : layer + 1]
        return [*extra.all, bias[:, :hidden_units], bias[:, hidden_units:]]

    embedded = jnp.take(time_table, steps, axis=0)
    condition = jax.nn.silu(embedded.astype(FLOAT)).astype(BFLOAT)
    section_mod = product(condition, ada_weight[0]) + ada_bias[0].astype(FLOAT)
    mods = lax.all_to_all(section_mod, "section", 0, 0, tiled=True).reshape(12, width)
    weights = (
        shared_up,
        shared_up_bias,
        shared_down,
        shared_down_bias,
        expert_up,
        expert_up_bias,
        expert_down,
        expert_down_bias,
    )

    size = rows + 16
    block_outs = [
        ((rows, width), bf),
        ((rows, 3 * width), bf),
        ((rows, width), bf),
        ((rows, width), fl),
        ((rows, width), bf),
        ((size, width), bf),
        ((rows, 128), fl),
    ]

    def attn_ins(layer, routes):
        return [
            (mods,),
            (qkv_weight, layer_spec(qkv_weight, layer)),
            (qv_bias,),
            (out_weight, layer_spec(out_weight, layer)),
            (out_bias,),
            (routers, layer_spec(routers, layer)),
            (routes,),
        ]

    first_extra.across()
    first_extra.pair()
    hidden0, qkv0, attended0, branch0, stream1, message1, gates1, last_grad, bundle = order.call(
        functools.partial(attention_forward_body, 0),
        [(tokens,), (cotangent,), *attn_ins(0, routes_one)],
        block_outs + [((rows, width), bf), ((2 * size, width), bf)],
        4.2,
    )
    got1 = swap(message1, "expert", 1)
    first_extra.plane()
    (shared1,) = shared_call(0, True, False, order, message1, None, weights)
    order.wait(got1)
    got_last = swap(order.tie(last_grad), "expert", 1)
    bundle2 = swap(order.tie(bundle), "expert", 2)
    extra0 = with_bias(0, first_extra)
    sent1, kept_got1 = experts_call(
        0, True, False, order, got1, None, None, weights, extra0, None, ()
    )
    back1 = swap(sent1, "expert", 1)
    own1, kept_own1 = experts_call(
        0, True, False, order, message1, gates1, None, weights, extra0, None, (shared1,)
    )
    second_extra.across()
    stream2, branch1, hidden2, qkv2, attended2, branch2, stream3, message3, gates3 = order.call(
        functools.partial(attention_forward_body, 2),
        [(stream1,), (own1,), (back1,), *attn_ins(1, routes_two)],
        [((rows, width), bf), ((rows, width), fl)] + block_outs,
        4.2,
    )
    got3 = swap(message3, "expert", 1)
    second_extra.pair()
    shared3, shared_grad3 = shared_call(1, True, True, order, message3, last_grad, weights)
    second_extra.plane()
    order.wait(got3)
    far3 = swap(order.tie(message3), "expert", 2)
    bundle3 = swap(order.tie(bundle2), "expert", 1)
    extra1 = with_bias(1, second_extra)
    sent3, back_message3 = experts_call(
        1, True, True, order, got3, None, got_last, weights, extra1, None, ()
    )
    back_grad3 = swap(back_message3, "expert", 1)
    own3, own_grad3, gate_grad3 = experts_call(
        1, True, True, order, message3, gates3, last_grad, weights, extra1, None,
        (shared3, shared_grad3),
    )
    farther3 = swap(order.tie(far3), "expert", 1)
    bundles = [bundle2, bundle3]

    def bundle_block(number):
        return [(item, pl.BlockSpec((size, width), lambda *_: (number, 0))) for item in bundles]

    sources1 = (
        [(item,) for item in (message3, got3, far3, farther3)],
        [(last_grad,), (got_last,)] + bundle_block(1),
    )
    grad_outs = [((4, width // 2 + 32, width), bf)] * 2 + [((16, width), fl)]
    proj = [pltpu.VMEM((rows, 3 * width), bf)]

    def attn_back_ins(layer):
        return [
            (mods,),
            (routers, layer_spec(routers, layer)),
            (qkv_weight, layer_spec(qkv_weight, layer)),
            (out_weight, layer_spec(out_weight, layer)),
        ]

    groups = Groups(width + 32, width // 2, width // 2 + 32)
    flow1, flow0 = Flow(groups, order), Flow(groups, order)
    order.wait(back_grad3)
    grad1, branch_grad1, kept_a, sent_a, small1 = order.call(
        functools.partial(attention_backward_body, 2),
        [
            (item,)
            for item in (
                cotangent, stream3, message3, own_grad3, back_grad3, gates3, gate_grad3,
                stream2, hidden2, qkv2, attended2, branch2,
            )
        ]
        + attn_back_ins(1)
        + [(branch1,)],
        [((rows, width), bf), ((rows, width), bf)] + grad_outs,
        7.7,
        scratch=proj,
    )
    got_grad1 = swap(branch_grad1, "expert", 1)
    kept, sent = weight_grads_call(1, order, *sources1, weights)
    flow1.add(kept, sent)
    flow1.add(kept_a, sent_a)
    (shared_grad1,) = shared_call(0, False, True, order, message1, branch_grad1, weights)
    order.wait(got_grad1)
    far_grad1 = swap(order.tie(branch_grad1), "expert", 2)
    back3 = swap(order.tie(sent3), "expert", 1)
    flow1.first()
    (back_message1,) = experts_call(
        0, False, True, order, got1, None, got_grad1, weights, extra0, kept_got1, ()
    )
    back_grad1 = swap(back_message1, "expert", 1)
    own_grad1, gate_grad1 = experts_call(
        0, False, True, order, message1, gates1, branch_grad1, weights, extra0, kept_own1,
        (shared_grad1,),
    )
    farther_grad1 = swap(order.tie(far_grad1), "expert", 1)
    flow1.second()
    token_grad, kept_a, sent_a, small0 = order.call(
        functools.partial(attention_backward_body, 0),
        [
            (item,)
            for item in (
                grad1, stream1, message1, own_grad1, back_grad1, gates1, gate_grad1,
                tokens, hidden0, qkv0, attended0, branch0,
            )
        ]
        + attn_back_ins(0),
        [((rows, width), fl)] + grad_outs,
        7.7,
        scratch=proj,
    )
    flow1.third()
    branch3 = own3 + back3.astype(FLOAT)
    output = (stream3.astype(FLOAT) + mods[11:12] * branch3).astype(BFLOAT)
    gating3 = jnp.sum(cotangent.astype(FLOAT) * branch3, 0, keepdims=True)

    def counted(route_pair):
        numbers = jnp.arange(experts_total, dtype=jnp.int32)
        return jnp.sum((route_pair.reshape(-1)[:, None] == numbers[None, :]).astype(FLOAT), 0)

    counts = jnp.concatenate([counted(routes_one), counted(routes_two)])
    counts = jnp.pad(counts, (0, width - 2 * experts_total))[None]
    own_step = jnp.full((1, width), timesteps[0], FLOAT)
    none = jnp.concatenate([own_step, jnp.zeros((3, width), FLOAT)])
    to_sections = jnp.concatenate(
        [
            small0[3:5], small0[2:3], counts, none,
            small0[0:2], small1[5:6], counts, none,
            small1[3:5], small1[2:3], counts, none,
            small1[0:2], gating3, counts, none,
        ]
    )
    to_sections = to_sections.reshape(4, 8, width)
    section = 2 * y + x_bit

    def toward(by):
        return lax.dynamic_index_in_dim(to_sections, section ^ by, 0, keepdims=False)

    factors = [toward(0)] + [swap(toward(by), "section", by) for by in (1, 2, 3)]
    factors = jnp.take(jnp.stack(factors), jnp.arange(4) ^ section, axis=0)

    sources0 = (
        [(message1,), (got1,)] + bundle_block(0),
        [(item,) for item in (branch_grad1, got_grad1, far_grad1, farther_grad1)],
    )
    kept, sent = weight_grads_call(0, order, *sources0, weights)
    flow0.add(kept, sent)
    flow0.add(kept_a, sent_a)
    flow0.first()
    flow1.relay()
    def images(x):
        x = ordered(core, x, swap(x, "dp", 1))
        turns = [x] + [swap(x, "expert", by) for by in (1, 2, 3)]
        planes = jnp.take(jnp.stack(turns), jnp.arange(4) ^ place[3], axis=0)
        return planes.reshape((-1,) + x.shape[2:])

    factors = images(order.tie(factors))
    counts_out = jnp.sum(factors[:, 3, : 2 * experts_total], 0)
    counts_out = counts_out.reshape(2, experts_total).astype(jnp.int32)
    mod_grads = factors[:, :3].reshape(-1, 3 * width)

    all_steps = factors[:, 4, 0].astype(jnp.int32)
    all_embedded = jnp.take(time_table, all_steps, axis=0).astype(FLOAT)
    all_condition = jax.nn.silu(all_embedded).astype(BFLOAT)
    low_grads = mod_grads.astype(BFLOAT)
    ada_out = lead_product(all_condition, low_grads)[None]
    ada_bias_out = jnp.sum(mod_grads, 0)[None]
    condition_grad = back_product(low_grads, ada_weight[0])

    condition_grad = condition_grad + swap(condition_grad, "section", 1)
    flow0.second()
    spread1 = flow1.column(True)
    condition_grad = condition_grad + swap(condition_grad, "section", 2)
    flow0.third()
    spread1.pair()
    expert0 = Spread(order, flow0.expert)
    flow0.relay()
    both = ("expert", "shared")
    finals = final_call(groups, both, 1, order, spread1.all, None)
    e_up_out, e_down_out, e_small1, s_up_out, s_down_out, qkv_out, out_w_out, a_small1 = finals
    expert0.pair()
    shared0 = flow0.column(False)
    shared0.pair()
    e_up_out, e_down_out, e_small0 = final_call(
        groups, ("expert",), 0, order, expert0.all, (e_up_out, e_down_out)
    )
    s_up_out, s_down_out, qkv_out, out_w_out, a_small0 = final_call(
        groups, ("shared",), 0, order, shared0.all, (s_up_out, s_down_out, qkv_out, out_w_out)
    )

    def two(take):
        return jnp.stack([take(a_small0), take(a_small1)])

    qv_out = two(lambda small: small[0:2].reshape(-1))
    out_b_out = two(lambda small: small[2])
    router_out = two(lambda small: small[3 : 3 + experts_total].T)
    s_upb_out = two(lambda small: small[7:15].reshape(-1))
    s_downb_out = two(lambda small: small[15])
    e_upb_out = jnp.stack([e_small0[:4].reshape(1, -1), e_small1[:4].reshape(1, -1)])
    e_downb_out = jnp.stack([e_small0[4:5], e_small1[4:5]])

    embed_grad = jax.vjp(jax.nn.silu, all_embedded)[1](condition_grad)[0]
    marks = (all_steps[:, None] == jnp.arange(steps_count, dtype=jnp.int32)[None, :]).astype(BFLOAT)
    table_out = lead_product(marks, embed_grad.astype(BFLOAT))

    return (
        output,
        token_grad,
        table_out,
        ada_out,
        ada_bias_out,
        qkv_out,
        qv_out,
        out_w_out,
        out_b_out,
        router_out,
        s_up_out,
        s_upb_out,
        s_down_out,
        s_downb_out,
        e_up_out,
        e_upb_out,
        e_down_out,
        e_downb_out,
        counts_out,
    )


def shards(*args):
    fits = (
        lax.axis_size("section") == 4
        and lax.axis_size("dp") == 2
        and lax.axis_size("expert") == 4
        and args[12].shape[2] == 4
        and args[1].shape[0] == 1
    )
    return (shards_fast if fits else shards_general)(*args)


def solution(mesh):
    rows = P(ALL, None)
    whole = P()
    placed = (
        rows,
        P(ALL),
        rows,
        rows,
        rows,
        whole,
        P("section", None, None),
        P("section", None),
        *([whole] * 9),
        P(None, "expert", None, None),
        P(None, "expert", None),
        P(None, "expert", None, None),
        P(None, "expert", None),
    )
    return jax.shard_map(
        shards,
        mesh=mesh,
        in_specs=placed,
        out_specs=(
            rows,
            rows,
            whole,
            P("section", None, None),
            P("section", None),
            *([whole] * 9),
            P(None, "expert", None, None),
            P(None, "expert", None),
            P(None, "expert", None, None),
            P(None, "expert", None),
            whole,
        ),
        check_vma=False,
    )
```

```python
import functools

import jax
import jax.numpy as jnp
from jax import lax
from jax.experimental import pallas as pl
from jax.experimental.pallas import tpu as pltpu
from jax.sharding import PartitionSpec as P

HEADS = 6
HD = 64

BFLOAT = jnp.bfloat16
FLOAT = jnp.float32
ALL = ("section", "dp", "expert")


def product(left_arg, right_arg):
    return jnp.dot(left_arg, right_arg, preferred_element_type=FLOAT)


def lead_product(left_arg, right_arg):
    return lax.dot_general(
        left_arg, right_arg, (((0,), (0,)), ((), ())), preferred_element_type=FLOAT
    )


def back_product(left_arg, right_arg):
    return lax.dot_general(
        left_arg, right_arg, (((1,), (1,)), ((), ())), preferred_element_type=FLOAT
    )


def gelu_parts(pre):
    inner = 0.7978845608028654 * (pre + 0.044715 * pre * pre * pre)
    tanh = jnp.tanh(inner)
    act = 0.5 * pre * (1.0 + tanh)
    slope = 0.5 * (1.0 + tanh) + 0.5 * pre * (1.0 - tanh * tanh) * 0.7978845608028654 * (
        1.0 + 3 * 0.044715 * pre * pre
    )
    return act, slope


def normalized(stream):
    row_mean = jnp.mean(stream, -1, keepdims=True)
    centred = stream - row_mean
    variance = jnp.mean(centred * centred, -1, keepdims=True)
    inverse = lax.rsqrt(variance + 1e-06)
    return centred * inverse, inverse


def modulate(stream, mod):
    unit, _ = normalized(stream)
    return (unit * (1.0 + mod[1]) + mod[0]).astype(BFLOAT)


def norm_backward(stream, mod, hidden_grad):
    unit, inverse = normalized(stream)
    shift_grad = jnp.sum(hidden_grad, 0)
    scale_grad = jnp.sum(hidden_grad * unit, 0)
    unit_grad = hidden_grad * (1.0 + mod[1])
    stream_grad = inverse * (
        unit_grad
        - jnp.mean(unit_grad, -1, keepdims=True)
        - unit * jnp.mean(unit_grad * unit, -1, keepdims=True)
    )
    return stream_grad, shift_grad, scale_grad


def heads_view(rows):
    return rows.astype(BFLOAT).reshape(-1, HEADS, HD)


def attention_forward(hidden, weights):
    qkv_matrix, qv_offset, out_matrix, out_offset = weights
    width = hidden.shape[1]
    projected = product(hidden, qkv_matrix)
    query = heads_view(projected[:, :width] + qv_offset[:width])
    key = heads_view(projected[:, width : 2 * width])
    value = heads_view(projected[:, 2 * width :] + qv_offset[width:])
    scores = jnp.einsum("qhd,khd->hqk", query, key, preferred_element_type=FLOAT) * HD ** (-0.5)
    probs = jax.nn.softmax(scores, -1)
    probs_low = probs.astype(BFLOAT)
    attended = (
        jnp.einsum("hqk,khd->qhd", probs_low, value, preferred_element_type=FLOAT)
        .reshape(-1, width)
        .astype(BFLOAT)
    )
    branch = product(attended, out_matrix) + out_offset
    return branch, (query, key, value, probs, probs_low, attended)


def attention_backward(hidden, weights, saved, branch_grad):
    qkv_matrix, _, out_matrix, _ = weights
    query, key, value, probs, probs_low, attended = saved
    width = hidden.shape[1]
    factor = HD ** (-0.5)
    low_grad = branch_grad.astype(BFLOAT)
    out_grad = lead_product(attended, low_grad)
    out_offset_grad = jnp.sum(low_grad.astype(FLOAT), 0)
    attended_grad = heads_view(back_product(low_grad, out_matrix))
    value_grad = jnp.einsum("hqk,qhd->khd", probs_low, attended_grad, preferred_element_type=FLOAT)
    prob_grad = jnp.einsum("qhd,khd->hqk", attended_grad, value, preferred_element_type=FLOAT)
    score_grad = (probs * (prob_grad - jnp.sum(prob_grad * probs, -1, keepdims=True))).astype(
        BFLOAT
    )
    query_grad = (
        jnp.einsum("hqk,khd->qhd", score_grad, key, preferred_element_type=FLOAT) * factor
    )
    key_grad = (
        jnp.einsum("hqk,qhd->khd", score_grad, query, preferred_element_type=FLOAT) * factor
    )
    proj_grad = jnp.concatenate(
        [item.reshape(-1, width) for item in (query_grad, key_grad, value_grad)], -1
    ).astype(BFLOAT)
    qkv_grad = lead_product(hidden, proj_grad)
    sums = jnp.sum(proj_grad.astype(FLOAT), 0)
    offset_grad = jnp.concatenate([sums[:width], sums[2 * width :]])
    hidden_grad = back_product(proj_grad, qkv_matrix)
    return hidden_grad, (qkv_grad, offset_grad, out_grad, out_offset_grad)


def expert_gates(rows, router, route_pair):
    logits = product(rows, router)
    marks = (
        route_pair[:, :, None] == jnp.arange(router.shape[1], dtype=jnp.int32)[None, None, :]
    ).any(1)
    top = jnp.max(jnp.where(marks, logits, -jnp.inf), -1, keepdims=True)
    raised = jnp.where(marks, jnp.exp(logits - top), 0.0)
    return raised / jnp.sum(raised, -1, keepdims=True)


def pick_column(table, column):
    return lax.dynamic_slice_in_dim(table, column, 1, axis=1)


def moe_forward(hidden, route_pair, weights):
    router, s_up, s_upb, s_down, s_downb, e_up, e_upb, e_down, e_downb = weights
    mine = lax.axis_index("expert")
    rows = lax.all_gather(hidden, "expert", axis=0, tiled=True)
    routes = lax.all_gather(route_pair, "expert", axis=0, tiled=True)
    gates = expert_gates(rows, router, routes)
    gate = pick_column(gates, mine)
    shared_pre = product(hidden, s_up) + s_upb
    shared_act, shared_slope = gelu_parts(shared_pre)
    shared_act = shared_act.astype(BFLOAT)
    shared_out = product(shared_act, s_down) + s_downb
    pre = product(rows, e_up[0]) + e_upb[0]
    act, slope = gelu_parts(pre)
    act = act.astype(BFLOAT)
    result = (product(act, e_down[0]) + e_downb[0]).astype(BFLOAT)
    routed = lax.psum_scatter(
        (gate * result.astype(FLOAT)).astype(BFLOAT), "expert", scatter_dimension=0, tiled=True
    )
    branch = shared_out + routed.astype(FLOAT)
    saved = (rows, routes, gates, gate, shared_act, shared_slope, act, slope, result)
    return branch, saved


def moe_backward(hidden, weights, saved, branch_grad):
    router, s_up, s_upb, s_down, s_downb, e_up, e_upb, e_down, e_downb = weights
    rows, routes, gates, gate, shared_act, shared_slope, act, slope, result = saved
    mine = lax.axis_index("expert")
    devices = lax.axis_size("expert")
    tokens_here = hidden.shape[0]
    low_grad = branch_grad.astype(BFLOAT)
    s_down_grad = lead_product(shared_act, low_grad)
    s_downb_grad = jnp.sum(low_grad.astype(FLOAT), 0)
    shared_dpre = (back_product(low_grad, s_down) * shared_slope).astype(BFLOAT)
    s_up_grad = lead_product(hidden, shared_dpre)
    s_upb_grad = jnp.sum(shared_dpre.astype(FLOAT), 0)
    hidden_grad = back_product(shared_dpre, s_up)
    row_grad = lax.all_gather(low_grad, "expert", axis=0, tiled=True).astype(FLOAT)
    gate_grad = jnp.sum(row_grad * result.astype(FLOAT), -1)
    gate_grads = lax.all_to_all(
        gate_grad.reshape(devices, tokens_here).astype(BFLOAT), "expert", 0, 0, tiled=True
    ).astype(FLOAT)
    own_gates = lax.dynamic_slice_in_dim(gates, mine * tokens_here, tokens_here, axis=0)
    gate_grads = gate_grads.T
    logit_grad = own_gates * (gate_grads - jnp.sum(own_gates * gate_grads, -1, keepdims=True))
    router_grad = lax.dot_general(
        hidden.astype(FLOAT),
        logit_grad,
        (((0,), (0,)), ((), ())),
        precision=lax.Precision.HIGHEST,
        preferred_element_type=FLOAT,
    )
    result_grad = (gate * row_grad).astype(BFLOAT)
    e_down_grad = lead_product(act, result_grad)
    e_downb_grad = jnp.sum(result_grad.astype(FLOAT), 0)
    dpre = (back_product(result_grad, e_down[0]) * slope).astype(BFLOAT)
    e_up_grad = lead_product(rows, dpre)
    e_upb_grad = jnp.sum(dpre.astype(FLOAT), 0)
    back_rows = lax.psum_scatter(
        back_product(dpre, e_up[0]).astype(BFLOAT), "expert", scatter_dimension=0, tiled=True
    )
    hidden_grad = hidden_grad + back_product(logit_grad, router.astype(FLOAT)) + back_rows
    return hidden_grad, (
        router_grad,
        s_up_grad,
        s_upb_grad,
        s_down_grad,
        s_downb_grad,
        e_up_grad,
        e_upb_grad,
        e_down_grad,
        e_downb_grad,
    )


def shards_general(
    tokens,
    timesteps,
    routes_one,
    routes_two,
    cotangent,
    time_table,
    ada_weight,
    ada_bias,
    qkv_weight,
    qv_bias,
    out_weight,
    out_bias,
    router_weight,
    shared_up,
    shared_up_bias,
    shared_down,
    shared_down_bias,
    expert_up,
    expert_up_bias,
    expert_down,
    expert_down_bias,
):
    width = tokens.shape[1]
    steps_count = time_table.shape[0]
    experts_total = router_weight.shape[2]
    route_sets = (routes_one, routes_two)
    steps = lax.all_gather(timesteps, "section", axis=0, tiled=True)
    embedded = jnp.take(time_table, steps, axis=0).astype(FLOAT)
    condition = jax.nn.silu(embedded).astype(BFLOAT)
    section_mod = product(condition, ada_weight[0]) + ada_bias[0].astype(FLOAT)
    mods = lax.all_to_all(section_mod, "section", 0, 0, tiled=True).reshape(-1, 3, width)

    def attn_weights(layer):
        return (
            qkv_weight[layer],
            qv_bias[layer].astype(FLOAT),
            out_weight[layer],
            out_bias[layer].astype(FLOAT),
        )

    def moe_weights(layer):
        return (
            router_weight[layer],
            shared_up[layer],
            shared_up_bias[layer].astype(FLOAT),
            shared_down[layer],
            shared_down_bias[layer].astype(FLOAT),
            expert_up[layer],
            expert_up_bias[layer].astype(FLOAT),
            expert_down[layer],
            expert_down_bias[layer].astype(FLOAT),
        )

    streams, hiddens, branches, kept = [], [], [], []
    stream = tokens
    for block in range(4):
        layer = block // 2
        streams.append(stream)
        wide = stream.astype(FLOAT)
        hidden = modulate(wide, mods[block])
        if block % 2 == 0:
            branch, saved = attention_forward(hidden, attn_weights(layer))
        else:
            branch, saved = moe_forward(hidden, route_sets[layer], moe_weights(layer))
        hiddens.append(hidden)
        branches.append(branch)
        kept.append(saved)
        stream = (wide + mods[block][2] * branch).astype(BFLOAT)
    output = stream

    upstream = cotangent
    mod_grads = [None] * 4
    attn_grads = [None] * 2
    moe_grads = [None] * 2
    for block in (3, 2, 1, 0):
        layer = block // 2
        wide_grad = upstream.astype(FLOAT)
        gating_grad = jnp.sum(wide_grad * branches[block], 0)
        branch_grad = mods[block][2] * wide_grad
        if block % 2 == 0:
            hidden_grad, attn_grads[layer] = attention_backward(
                hiddens[block], attn_weights(layer), kept[block], branch_grad
            )
        else:
            hidden_grad, moe_grads[layer] = moe_backward(
                hiddens[block], moe_weights(layer), kept[block], branch_grad
            )
        stream_grad, shift_grad, scale_grad = norm_backward(
            streams[block].astype(FLOAT), mods[block], hidden_grad
        )
        mod_grads[block] = jnp.concatenate([shift_grad, scale_grad, gating_grad])
        token_grad = wide_grad + stream_grad
        upstream = token_grad.astype(BFLOAT)

    section_grads = lax.all_to_all(jnp.stack(mod_grads), "section", 0, 0, tiled=True)
    ada_part = lead_product(condition, section_grads.astype(BFLOAT))
    condition_grad = back_product(section_grads, ada_weight[0].astype(FLOAT))
    condition_grad = lax.psum(condition_grad, "section")
    embed_grad = jax.vjp(jax.nn.silu, embedded)[1](condition_grad)[0]
    marks = (steps[:, None] == jnp.arange(steps_count, dtype=jnp.int32)[None, :]).astype(FLOAT)
    table_part = lead_product(marks, embed_grad)

    def counted(route_pair):
        return jnp.sum(
            (
                route_pair.reshape(-1)[:, None]
                == jnp.arange(experts_total, dtype=jnp.int32)[None, :]
            ).astype(jnp.int32),
            0,
        )

    def total(parts, axes):
        return lax.psum(parts.astype(BFLOAT), axes).astype(FLOAT)

    both_attn = [jnp.stack([attn_grads[0][n], attn_grads[1][n]]) for n in range(4)]
    both_moe = [jnp.stack([moe_grads[0][n], moe_grads[1][n]]) for n in range(9)]
    counts = lax.psum(jnp.stack([counted(routes_one), counted(routes_two)]), ALL)
    attn_out = [total(item, ALL) for item in both_attn]
    moe_out = [total(item, ALL) for item in both_moe[:5]]
    expert_out = [total(item, ("section", "dp"))[:, None] for item in both_moe[5:]]
    table_out = total(table_part, ("dp", "expert"))
    ada_out = total(ada_part, ("dp", "expert"))[None]
    ada_bias_out = total(jnp.sum(section_grads, 0), ("dp", "expert"))[None]
    return (
        output,
        token_grad,
        table_out,
        ada_out,
        ada_bias_out,
        *attn_out,
        *moe_out,
        *expert_out,
        counts,
    )


def norm_parts(wide):
    row_mean = jnp.mean(wide, -1, keepdims=True)
    centred = wide - row_mean
    variance = jnp.mean(centred * centred, -1, keepdims=True)
    inverse = lax.rsqrt(variance + 1e-06)
    return centred * inverse, inverse


def norm_grad(unit, inverse, scaling, hidden_grad):
    shift_grad = jnp.sum(hidden_grad, 0, keepdims=True)
    scale_grad = jnp.sum(hidden_grad * unit, 0, keepdims=True)
    unit_grad = hidden_grad * (1.0 + scaling)
    stream_grad = inverse * (
        unit_grad
        - jnp.mean(unit_grad, -1, keepdims=True)
        - unit * jnp.mean(unit_grad * unit, -1, keepdims=True)
    )
    return stream_grad, shift_grad, scale_grad


def whole_spec(array):
    return pl.BlockSpec(array.shape, lambda *_: (0,) * array.ndim)


def layer_spec(array, layer):
    block = (None,) + array.shape[1:]
    return pl.BlockSpec(block, lambda *_: (layer,) + (0,) * (array.ndim - 1))


def kernel_call(body, ins, outs, flops, grid=(1,), scratch=(), prefetch=()):
    arrays = [item[0] for item in ins]
    specs = [item[1] if len(item) > 1 else whole_spec(item[0]) for item in ins]
    moved = sum(array.size * array.dtype.itemsize for array in arrays)
    return pl.pallas_call(
        body,
        out_shape=[
            (pltpu.HBM if far else jax.ShapeDtypeStruct)(shape, dtype) for shape, dtype, *far in outs
        ],
        grid_spec=pltpu.PrefetchScalarGridSpec(
            num_scalar_prefetch=len(prefetch),
            grid=grid,
            in_specs=specs,
            out_specs=[
                pl.BlockSpec(item[0], lambda *_, rank=len(item[0]): (0,) * rank) for item in outs
            ],
            scratch_shapes=list(scratch),
        ),
        cost_estimate=pl.CostEstimate(flops=flops, bytes_accessed=moved, transcendentals=0),
        compiler_params=pltpu.CompilerParams(vmem_limit_bytes=32 << 20),
    )(*prefetch, *arrays)


def mod_of(mods, block, part):
    row = 3 * block + part
    return mods[row : row + 1, :]


def head_pairs(width):
    for pair in range(HEADS // 2):
        start = pair * 2 * HD
        yield slice(start, start + 2 * HD), slice(width + start, width + start + 2 * HD), slice(
            2 * width + start, 2 * width + start + 2 * HD
        )


def masked(mask, rows):
    return jnp.where(mask, rows, jnp.zeros_like(rows))


def head_probs(query, key):
    scores = back_product(query, key) * HD ** (-0.5)
    raised = jnp.exp(scores - jnp.max(scores, -1, keepdims=True))
    return raised * (1.0 / jnp.sum(raised, -1, keepdims=True))


def gate_column(gates, expert):
    lanes = lax.broadcasted_iota(jnp.int32, gates.shape, 1)
    return jnp.sum(jnp.where(lanes == expert, gates, 0.0), -1, keepdims=True)


def gelu_value(pre):
    pre = pre.astype(BFLOAT)
    tanh = jnp.tanh(pre * (BFLOAT(0.7978845608028654) + BFLOAT(0.035677408136300125) * (pre * pre)))
    half = BFLOAT(0.5) * pre
    return half + half * tanh


def gelu_both(pre):
    pre = pre.astype(BFLOAT)
    square = pre * pre
    tanh = jnp.tanh(pre * (BFLOAT(0.7978845608028654) + BFLOAT(0.035677408136300125) * square))
    half = BFLOAT(0.5) * pre
    slope = (BFLOAT(0.5) + BFLOAT(0.5) * tanh) + (half * (BFLOAT(1.0) - tanh * tanh)) * (
        BFLOAT(0.7978845608028654) + BFLOAT(0.10703222440890037) * square
    )
    return half + half * tanh, slope


def far(x):
    return pltpu.with_memory_space_constraint(x, pltpu.HBM)


def gates_of(rows, routes, router):
    logits = product(rows, router)
    lanes = lax.broadcasted_iota(jnp.int32, logits.shape, 1)
    marks = (lanes == routes[:, 0:1]) | (lanes == routes[:, 1:2])
    top = jnp.max(jnp.where(marks, logits, -jnp.inf), -1, keepdims=True)
    raised = jnp.where(marks, jnp.exp(logits - top), 0.0)
    return raised / jnp.sum(raised, -1, keepdims=True)


def write_columns(out, start, table):
    rows = table.shape[0]
    turned = jnp.transpose(table)[:8]
    rounded = turned.astype(BFLOAT).astype(FLOAT)
    both = jnp.concatenate([rounded, turned - rounded]).astype(BFLOAT)
    out[start : start + 16, :] = jnp.zeros((16, out.shape[1]), BFLOAT)
    out[start : start + 16, :rows] = both


def read_columns(message, start, rows):
    both = message[start : start + 16, :rows].astype(FLOAT)
    turned = jnp.concatenate([both[:8] + both[8:], jnp.zeros((120, rows), FLOAT)])
    return jnp.transpose(turned)


def attention_forward_body(block, place, *refs):
    layer = block // 2
    refs = list(refs)
    pop = lambda count: [refs.pop(0) for _ in range(count)]
    if block:
        stream, own, back = pop(3)
    else:
        stream, cotangent = pop(2)
    mods, qkv_w, qv_b, out_w, out_b, router, routes = pop(7)
    if block:
        stream_out, before_out = pop(2)
        before = own[...] + back[...].astype(FLOAT)
        before_out[...] = before
        low_stream = (stream[...].astype(FLOAT) + mod_of(mods, block - 1, 2) * before).astype(BFLOAT)
        stream_out[...] = low_stream
        wide = low_stream.astype(FLOAT)
    else:
        wide = stream[...].astype(FLOAT)
    hidden_out, qkv_out, attended_out, branch_out, new_out, message_out, gates_out = pop(7)
    rows, width = wide.shape
    unit, _ = norm_parts(wide)
    hidden = (unit * (1.0 + mod_of(mods, block, 1)) + mod_of(mods, block, 0)).astype(BFLOAT)
    hidden_out[...] = hidden
    bias = qv_b[layer : layer + 1, :].astype(FLOAT)
    projected = product(hidden, qkv_w[...])
    qkv_out[:, :width] = (projected[:, :width] + bias[:, :width]).astype(BFLOAT)
    qkv_out[:, width : 2 * width] = projected[:, width : 2 * width].astype(BFLOAT)
    qkv_out[:, 2 * width :] = (projected[:, 2 * width :] + bias[:, width:]).astype(BFLOAT)
    low = lax.broadcasted_iota(jnp.int32, (rows, 2 * HD), 1) < HD
    for query_at, key_at, value_at in head_pairs(width):
        query, key, value = qkv_out[:, query_at], qkv_out[:, key_at], qkv_out[:, value_at]
        parts = [
            product(head_probs(masked(mask, query), key).astype(BFLOAT), value)
            for mask in (low, ~low)
        ]
        attended_out[:, query_at] = jnp.where(low, parts[0], parts[1]).astype(BFLOAT)
    branch = product(attended_out[...], out_w[...]) + out_b[layer : layer + 1, :].astype(FLOAT)
    branch_out[...] = branch
    new = (wide + mod_of(mods, block, 2) * branch).astype(BFLOAT)
    new_out[...] = new
    unit, _ = norm_parts(new.astype(FLOAT))
    following = (unit * (1.0 + mod_of(mods, block + 1, 1)) + mod_of(mods, block + 1, 0)).astype(
        BFLOAT
    )
    gates = gates_of(following, routes, router[...])
    gates_out[...] = gates
    message_out[:rows, :] = following
    write_columns(message_out, rows, gates)
    if not block:
        (last,) = pop(1)
        last[...] = (mod_of(mods, 3, 2) * cotangent[...].astype(FLOAT)).astype(BFLOAT)


def keep_or_send(place, core, kept, sent, piece, at, value):
    @pl.when(place[0] == core)
    def _():
        kept[piece, at, :] = value

    @pl.when(place[0] != core)
    def _():
        sent[piece, at, :] = value


def attention_backward_body(block, place, *refs):
    (
        upstream, after, after_message, own_grad, message, own_gates, gate_grads,
        stream, hidden, qkv, attended, branch, mods, router, qkv_w, out_w, *refs,
    ) = refs
    if block:
        before, grad_out, before_grad_out, kept, sent, small_out, proj = refs
    else:
        grad_out, kept, sent, small_out, proj = refs
    rows, width = stream.shape
    small_out[...] = jnp.zeros_like(small_out)

    gate_grad = gate_grads[...] + read_columns(message, rows, rows)
    gates = own_gates[...]
    logit_grad = gates * (gate_grad - jnp.sum(gates * gate_grad, -1, keepdims=True))
    logit_grad = logit_grad.astype(BFLOAT)
    router_grad = lead_product(logit_grad, after_message[:rows, :])[:4]
    hidden_grad = (
        own_grad[...] + message[:rows, :].astype(FLOAT) + back_product(logit_grad, router[...])
    )
    unit, inverse = norm_parts(after[...].astype(FLOAT))
    after_grad, shift_grad, scale_grad = norm_grad(
        unit, inverse, mod_of(mods, block + 1, 1), hidden_grad
    )
    small_out[0:1, :] = shift_grad
    small_out[1:2, :] = scale_grad
    wide_grad = (upstream[...].astype(FLOAT) + after_grad).astype(BFLOAT).astype(FLOAT)

    small_out[2:3, :] = jnp.sum(wide_grad * branch[...], 0, keepdims=True)
    branch_grad = (mod_of(mods, block, 2) * wide_grad).astype(BFLOAT)
    out_bias_grad = jnp.sum(branch_grad.astype(FLOAT), 0, keepdims=True)
    attended_grad = back_product(branch_grad, out_w[...]).astype(BFLOAT)
    low = lax.broadcasted_iota(jnp.int32, (rows, 2 * HD), 1) < HD
    factor = HD ** (-0.5)
    for query_at, key_at, value_at in head_pairs(width):
        query, key, value = qkv[:, query_at], qkv[:, key_at], qkv[:, value_at]
        pair_grad = attended_grad[:, query_at]
        sums = None
        for mask in (low, ~low):
            own_query, own_pair = masked(mask, query), masked(mask, pair_grad)
            probs = head_probs(own_query, key)
            value_grad = lead_product(probs.astype(BFLOAT), own_pair)
            prob_grad = back_product(own_pair, value)
            score_grad = (
                probs * (prob_grad - jnp.sum(prob_grad * probs, -1, keepdims=True))
            ).astype(BFLOAT)
            query_grad = masked(mask, product(score_grad, key))
            key_grad = lead_product(score_grad, own_query)
            parts = (query_grad, key_grad, value_grad)
            sums = parts if sums is None else tuple(a + b for a, b in zip(sums, parts))
        proj[:, query_at] = (sums[0] * factor).astype(BFLOAT)
        proj[:, key_at] = (sums[1] * factor).astype(BFLOAT)
        proj[:, value_at] = sums[2].astype(BFLOAT)

    middle = width // 2
    for part in range(4):
        if part < 3:
            grad = lead_product(hidden[...], proj[:, part * width : (part + 1) * width])
        else:
            grad = lead_product(attended[...], branch_grad)
        for side in range(2):
            keep_or_send(
                place,
                part // 2,
                kept,
                sent,
                2 * (part % 2) + side,
                slice(32, 32 + middle),
                grad[side * middle : (side + 1) * middle].astype(BFLOAT),
            )
    extra = jnp.concatenate(
        [
            jnp.sum(proj[:, :width].astype(FLOAT), 0, keepdims=True),
            jnp.sum(proj[:, 2 * width :].astype(FLOAT), 0, keepdims=True),
            out_bias_grad,
            router_grad,
            jnp.zeros((25, width), FLOAT),
        ]
    ).astype(BFLOAT)
    tail = slice(0, 32)
    for piece in range(4):
        for core in range(2):
            value = extra if piece == 0 and core == 0 else jnp.zeros((32, width), BFLOAT)
            keep_or_send(place, core, kept, sent, piece, tail, value)

    hidden_grad = back_product(proj[...], qkv_w[...])
    unit, inverse = norm_parts(stream[...].astype(FLOAT))
    stream_grad, shift_grad, scale_grad = norm_grad(
        unit, inverse, mod_of(mods, block, 1), hidden_grad
    )
    small_out[3:4, :] = shift_grad
    small_out[4:5, :] = scale_grad
    grad = wide_grad + stream_grad
    if block:
        low_grad = grad.astype(BFLOAT)
        grad_out[...] = low_grad
        wide_grad = low_grad.astype(FLOAT)
        before_grad_out[...] = (mod_of(mods, block - 1, 2) * wide_grad).astype(BFLOAT)
        small_out[5:6, :] = jnp.sum(wide_grad * before[...], 0, keepdims=True)
    else:
        grad_out[...] = grad


def shared_body(layer, forward, backward, place, *refs):
    refs = list(refs)
    pop = lambda count: [refs.pop(0) for _ in range(count)]
    (message,) = pop(1)
    branch_grad = pop(1)[0] if backward else None
    up, up_bias, down, down_bias = pop(4)
    total = pop(1)[0] if forward else None
    grads = pop(1)[0] if backward else None
    rows = message.shape[0] - 16
    pre = product(message[:rows, :], up[...]) + up_bias[layer : layer + 1, :].astype(FLOAT)
    if backward:
        act, slope = gelu_both(pre)
        act_grad = (back_product(branch_grad[...], down[...]) * slope).astype(BFLOAT)
        part = back_product(act_grad, up[...])

        @pl.when(pl.program_id(0) == 0)
        def _():
            grads[...] = part

        @pl.when(pl.program_id(0) > 0)
        def _():
            grads[...] += part

    else:
        act = gelu_value(pre)
    if forward:
        part = product(act.astype(BFLOAT), down[...])

        @pl.when(pl.program_id(0) == 0)
        def _():
            total[...] = part + down_bias[layer : layer + 1, :].astype(FLOAT)

        @pl.when(pl.program_id(0) > 0)
        def _():
            total[...] += part


def shared_call(layer, forward, backward, order, message, branch_grad, weights, hide=None):
    up, up_bias, down, down_bias = weights[:4]
    rows, width = message.shape[0] - 16, message.shape[1]
    units = 1536
    ins = [(message,)] + [(branch_grad,)] * backward
    ins += [
        (up, pl.BlockSpec((None, width, units), lambda i, _: (layer, 0, i))),
        (up_bias, pl.BlockSpec((2, units), lambda i, _: (0, i))),
        (down, pl.BlockSpec((None, units, width), lambda i, _: (layer, i, 0))),
        (down_bias,),
    ]
    return order.call(
        functools.partial(shared_body, layer, forward, backward),
        ins,
        [((rows, width), FLOAT)] * (forward + backward),
        5.0,
        hide=hide,
        grid=(up.shape[2] // units,),
    )


def experts_body(layer, forward, backward, partner, place, *refs):
    refs = list(refs)
    pop = lambda count: [refs.pop(0) for _ in range(count)]
    (message,) = pop(1)
    own_gates = None if partner else pop(1)[0]
    branch_grad = pop(1)[0] if backward else None
    e_up, e_upb, e_down, e_downb, own_up, got_up, own_down, got_down, x_upb, x_downb = pop(10)
    kept = pop(1)[0] if backward and not forward else None
    shared_out = pop(1)[0] if forward and not partner else None
    shared_grad = pop(1)[0] if backward and not partner else None
    if forward:
        total_out = pop(1)[0]
        kept_out = None if backward else pop(1)[0]
    if backward:
        grad_out = pop(1)[0]
        gate_grad_out = None if partner else pop(1)[0]
    x_up, x_down, total, sems = pop(4)
    if partner:
        (gates,) = pop(1)
    else:
        gates = own_gates
    if backward:
        grads, gate_grad = pop(2)
    step = pl.program_id(0)
    rows = message.shape[0] - 16
    lanes = lax.broadcasted_iota(jnp.int32, (rows, 128), 1)

    def copies():
        pairs = (
            (own_up, x_up.at[place[0]]),
            (own_down, x_down.at[place[0]]),
            (got_up, x_up.at[1 - place[0]]),
            (got_down, x_down.at[1 - place[0]]),
        )
        return [
            pltpu.make_async_copy(source, target, sems.at[number])
            for number, (source, target) in enumerate(pairs)
        ]

    @pl.when(step == 0)
    def _():
        if partner:
            gates[...] = read_columns(message, rows, rows)
        for copy in copies():
            copy.start()

    def expert(index, number, up, up_bias, down, down_bias):
        gate = gate_column(gates[...], number)
        pre = product(message[:rows, :], up) + up_bias
        if backward:
            act, slope = gelu_both(pre)
            act_grad = (back_product(branch_grad[...], down) * slope * gate).astype(BFLOAT)
            part_grad = back_product(act_grad, up)
        else:
            act = gelu_value(pre)
        if forward:
            result = (product(act.astype(BFLOAT), down) + down_bias).astype(BFLOAT)
            if kept_out is not None:
                kept_out[index] = result
            result = result.astype(FLOAT)
            part = gate * result
        else:
            result = kept[index].astype(FLOAT)
        if backward:
            column = jnp.sum(branch_grad[...].astype(FLOAT) * result, -1, keepdims=True)
            part_gate = jnp.where(lanes == number, column, 0.0)
        if index == 0:
            if forward:
                total[...] = part
            if backward:
                grads[...] = part_grad
                gate_grad[...] = part_gate
            return
        if forward:
            part = part + total[...]
            if not partner:
                part = part + shared_out[...]
            total_out[...] = part.astype(total_out.dtype)
        if backward:
            part_grad = part_grad + grads[...]
            part_gate = part_gate + gate_grad[...]
            if partner:
                grad_out[:rows, :] = part_grad.astype(BFLOAT)
                write_columns(grad_out, rows, part_gate)
            else:
                grad_out[...] = part_grad + shared_grad[...]
                gate_grad_out[...] = part_gate

    @pl.when(step == 0)
    def _():
        expert(
            0, place[3], e_up[...], e_upb[layer].astype(FLOAT), e_down[...],
            e_downb[layer].astype(FLOAT),
        )

    @pl.when(step == 1)
    def _():
        for copy in copies():
            copy.wait()
        width, units = e_up.shape
        expert(
            1, place[3] ^ 2, x_up[...].reshape(width, units), x_upb[...].astype(FLOAT),
            x_down[...].reshape(units, width),
            x_downb[...].astype(FLOAT),
        )


def experts_call(
    layer,
    forward,
    backward,
    order,
    message,
    gates,
    branch_grad,
    weights,
    extra,
    kept,
    shared,
    hide=None,
):
    e_up, e_upb, e_down, e_downb = weights[4:]
    rows, width = message.shape[0] - 16, message.shape[1]
    units = e_up.shape[3]
    partner = gates is None
    ins = [(message,)]
    if not partner:
        ins += [(gates,)]
    if backward:
        ins += [(branch_grad,)]
    ins += [
        (e_up, pl.BlockSpec((None, None, width, units), lambda i, _: (layer, 0, 0, 0))),
        (e_upb,),
        (e_down, pl.BlockSpec((None, None, units, width), lambda i, _: (layer, 0, 0, 0))),
        (e_downb,),
    ]
    ins += [(item, pl.BlockSpec(memory_space=pltpu.HBM)) for item in extra[:4]]
    ins += [(item,) for item in extra[4:]]
    if backward and not forward:
        ins += [(far(kept),)]
    if not partner:
        ins += [(item,) for item in shared]
    outs = []
    scratch = [
        pltpu.VMEM((2,) + extra[0].shape, BFLOAT),
        pltpu.VMEM((2,) + extra[2].shape, BFLOAT),
        pltpu.VMEM((rows, width), FLOAT),
        pltpu.SemaphoreType.DMA((4,)),
    ]
    if partner:
        scratch += [pltpu.VMEM((rows, 128), FLOAT)]
    if forward:
        outs += [((rows, width), BFLOAT if partner else FLOAT)]
        if not backward:
            outs += [((2, rows, width), BFLOAT, True)]
    if backward:
        outs += [((rows + 16, width), BFLOAT)] if partner else [((rows, width), FLOAT)]
        if not partner:
            outs += [((rows, 128), FLOAT)]
        scratch += [pltpu.VMEM((rows, width), FLOAT), pltpu.VMEM((rows, 128), FLOAT)]
    return order.call(
        functools.partial(experts_body, layer, forward, backward, partner),
        ins,
        outs,
        6.0,
        hide=hide,
        grid=(2,),
        scratch=scratch,
    )


def weight_grads_body(layer, expert, shared, place, *refs):
    messages, branch_grads, refs = refs[0:4], refs[4:8], list(refs[8:])
    pop = lambda count: [refs.pop(0) for _ in range(count)]
    if expert:
        e_up, e_upb, e_down = pop(3)
    if shared:
        s_up, s_upb, s_down = pop(3)
    kept, sent, rows_all, grads_all, acts, pre_grads, sums_all = pop(7)
    step = pl.program_id(0)
    rows, width = 256, rows_all.shape[1]
    units = acts.shape[1]
    middle = width // 2
    unroll = True

    def fill_rows(gated):
        for side in range(4):
            at = slice(side * rows, (side + 1) * rows)
            grad = branch_grads[side][:rows, :]
            rows_all[at, :] = messages[side][:rows, :]
            if gated:
                gate = gate_column(read_columns(messages[side], rows, rows), place[3])
                grad = (gate * grad.astype(FLOAT)).astype(BFLOAT)
            grads_all[at, :] = grad
            bias = jnp.sum(grad.astype(FLOAT), 0, keepdims=True)
            if gated:
                sums_all[4:5, :] += bias
            else:
                sums_all[15:16, :] += jnp.where(place[3] == 0, bias, 0.0)

    def chunk(up, offset, down):
        def tile(side, sums):
            at = pl.ds(pl.multiple_of(side * rows, rows), rows)
            act, slope = gelu_both(product(rows_all[at, :], up[...]) + offset)
            acts[at, :] = act.astype(BFLOAT)
            grad = (back_product(grads_all[at, :], down[...]) * slope).astype(BFLOAT)
            pre_grads[at, :] = grad
            return sums + jnp.sum(grad.astype(FLOAT), 0, keepdims=True)

        return lax.fori_loop(0, 4, tile, jnp.zeros((1, units), FLOAT), unroll=unroll)

    def weight_pair(half):
        at = slice(half * width, (half + 1) * width)
        up_grad = lead_product(rows_all[...], pre_grads[:, at]).astype(BFLOAT)
        down_grad = lead_product(acts[:, at], grads_all[...]).astype(BFLOAT)
        return (0, up_grad), (1, down_grad)

    def tails(start):
        at = slice(start, start + 32)
        value = sums_all[...].astype(BFLOAT)
        for piece in range(4):
            for core in range(2):
                rest = jnp.zeros((32, width), BFLOAT)
                own = value if piece == 0 and core == 0 else rest
                keep_or_send(place, core, kept, sent, piece, at, own)

    if expert:
        for part in range(2):

            @pl.when(step == part)
            def _(part=part):
                if part == 0:
                    sums_all[...] = jnp.zeros_like(sums_all)
                    fill_rows(True)
                sums = chunk(e_up, e_upb[layer].astype(FLOAT), e_down)
                for half in range(2):
                    number = 2 * part + half
                    sums_all[number : number + 1, :] = sums[:, half * width : (half + 1) * width]
                    for core, grad in weight_pair(half):
                        keep_or_send(place, core, kept, sent, number, slice(0, width), grad)
                if part == 1:
                    tails(width)

    if shared:

        @pl.when(step == 2 * expert)
        def _():
            sums_all[...] = jnp.zeros_like(sums_all)
            fill_rows(False)
            sums = chunk(s_up, s_upb[layer : layer + 1, :].astype(FLOAT), s_down)
            start = (width + 32) * expert
            where = slice(start, start + middle)
            for half in range(2):
                part_sums = sums[:, half * width : (half + 1) * width]
                for plane in range(4):
                    row = 7 + 2 * plane + half
                    sums_all[row : row + 1, :] = jnp.where(place[3] == plane, part_sums, 0.0)
                for core, grad in weight_pair(half):
                    for side in range(2):
                        value = grad[side * middle : (side + 1) * middle]
                        keep_or_send(place, core, kept, sent, 2 * half + side, where, value)
            tails(start + middle)


def weight_grads_call(layer, expert, shared, order, messages, branch_grads, weights, hide=None):
    s_up, s_upb, s_down, _, e_up, e_upb, e_down, _ = weights
    rows, width, units = 256, s_up.shape[1], 768
    at_own = lambda i: jnp.minimum(i, 1)
    ins = list(messages) + list(branch_grads)
    if expert:
        ins += [
            (e_up, pl.BlockSpec((None, None, width, units), lambda i, _: (layer, 0, 0, at_own(i)))),
            (e_upb, pl.BlockSpec((2, 1, units), lambda i, _: (0, 0, at_own(i)))),
            (
                e_down,
                pl.BlockSpec((None, None, units, width), lambda i, _: (layer, 0, at_own(i), 0)),
            ),
        ]
    if shared:
        ins += [
            (s_up, pl.BlockSpec((None, width, units), lambda i, at: (layer, 0, at[3]))),
            (s_upb, pl.BlockSpec((2, units), lambda i, at: (0, at[3]))),
            (s_down, pl.BlockSpec((None, units, width), lambda i, at: (layer, at[3], 0))),
        ]
    piece = (width + 32) * expert + (width // 2 + 32) * shared
    return order.call(
        functools.partial(weight_grads_body, layer, expert, shared),
        ins,
        [((4, piece, width), BFLOAT, True)] * 2,
        7.0 * (2 * expert + shared),
        hide=hide,
        grid=(2 * expert + shared,),
        scratch=[
            pltpu.VMEM((4 * rows, width), BFLOAT),
            pltpu.VMEM((4 * rows, width), BFLOAT),
            pltpu.VMEM((4 * rows, units), BFLOAT),
            pltpu.VMEM((4 * rows, units), BFLOAT),
            pltpu.VMEM((32, width), FLOAT),
        ],
    )


def swap(x, axis, by):
    return lax.ppermute(x, axis, [(i, i ^ by) for i in range(lax.axis_size(axis))])


def bits():
    section = lax.axis_index("section")
    return lax.axis_index("dp"), section // 2, section % 2


def ordered(bit, mine, other):
    return jnp.stack([jnp.where(bit == 0, mine, other), jnp.where(bit == 0, other, mine)])


def wide_sum(*parts):
    total = parts[0].astype(FLOAT)
    for part in parts[1:]:
        total = total + part.astype(FLOAT)
    return total


class Groups:
    def __init__(self, expert, shared, every):
        self.expert, self.shared, self.every = expert, shared, every
        self.rows = expert + shared + every
        self.half = self.rows // 2
        self.sent = expert // 2 + 2 * shared + every // 2


def first_body(has_misc, place, *refs):
    keeps, gots, refs = refs[:2], refs[2:4], refs[4:]
    if has_misc:
        misc, got_misc, *refs = refs
    keep_a, send_a, keep_b, send_b, pieces = refs
    half = keep_a.shape[1]
    y, x = place[1], place[2]
    joint = keeps[0].shape[1] - 32
    for piece in range(4):
        first = wide_sum(keeps[0][piece], gots[0][piece])
        second = wide_sum(keeps[1][piece], gots[1][piece])
        pieces[piece, :joint, :] = first[:joint].astype(BFLOAT)
        small = first[joint:] + second[:32]
        if has_misc and piece in (1, 2):
            at = slice(32 * (piece - 1), 32 * piece)
            small = small + jnp.where(place[0] == 0, misc[at, :] + got_misc[at, :], 0.0)
        pieces[piece, joint : joint + 32, :] = small.astype(BFLOAT)
        pieces[piece, joint + 32 :, :] = second[32:].astype(BFLOAT)
    for other in range(2):
        keep_a[other] = pieces[2 * other + x, :half, :]
        send_a[other] = pieces[2 * other + 1 - x, :half, :]
        keep_b[other] = pieces[2 * y + other, half:, :]
        send_b[other] = pieces[2 * (1 - y) + other, half:, :]


def second_body(place, keep_a, got_a, keep_b, got_b, *outs):
    next_a, sent_a, next_b, sent_b = outs
    y, x = place[1], place[2]
    next_a[...] = wide_sum(keep_a[y], got_a[y]).astype(BFLOAT)
    sent_a[...] = wide_sum(keep_a[1 - y], got_a[1 - y]).astype(BFLOAT)
    next_b[...] = wide_sum(keep_b[x], got_b[x]).astype(BFLOAT)
    sent_b[...] = wide_sum(keep_b[1 - x], got_b[1 - x]).astype(BFLOAT)


def third_body(groups, place, keep_a, got_a, keep_b, got_b, *refs):
    *outs, piece = refs
    piece[: groups.half, :] = wide_sum(keep_a[...], got_a[...]).astype(BFLOAT)
    piece[groups.half :, :] = wide_sum(keep_b[...], got_b[...]).astype(BFLOAT)
    middle = groups.expert // 2
    if groups.expert:
        outs[0][...] = piece[:middle, :]
        outs[1][...] = piece[middle : 2 * middle, :]
    if groups.shared:
        outs[-1][...] = piece[2 * middle :, :]


def column_body(groups, joined, place, *refs):
    experts = (refs[0], refs[1]) if joined else None
    columns, sent = refs[2 * joined : 2 * joined + 4], refs[2 * joined + 4 :]
    z = place[3]
    shared, every = groups.shared // 2, groups.every // 2
    for side in range(2):
        out = sent[side]
        at = 0
        if joined:
            at = groups.expert // 2
            out[:at, :] = experts[side][...]
        for turn in range(4):
            to = pl.multiple_of(at + (z ^ turn) * shared, 16)
            out[pl.ds(to, shared), :] = columns[turn][side * shared : (side + 1) * shared, :]
        at += 4 * shared
        rows = slice(groups.shared + side * every, groups.shared + (side + 1) * every)
        first = wide_sum(columns[0][rows, :], columns[1][rows, :])
        second = wide_sum(columns[2][rows, :], columns[3][rows, :])
        out[at:, :] = (first + second).astype(BFLOAT)


def pair_body(place, own_a, got_a, own_b, got_b, out_a, out_b):
    y, x = place[1], place[2]
    out_a[y] = own_a[...]
    out_a[1 - y] = got_a[...]
    out_b[x] = own_b[...]
    out_b[1 - x] = got_b[...]


COST = 1.1e9


class Order:
    def __init__(self, place):
        self.place = place

    def call(self, body, ins, outs, micros, hide=None, **kwargs):
        outs = kernel_call(body, ins, outs, int(micros * COST), prefetch=(self.place,), **kwargs)
        if hide is None:
            self.place = lax.optimization_barrier((self.place, outs[-1]))[0]
            return outs
        self.place, outs, hide = lax.optimization_barrier((self.place, outs, hide))
        return outs, hide

    def arrive(self, xs):
        self.place, xs = lax.optimization_barrier((self.place, xs))
        return xs

    def tie(self, x):
        return lax.optimization_barrier((x, self.place))[0]

    def wait(self, x):
        self.place = lax.optimization_barrier((self.place, x))[0]


class Flow:
    def __init__(self, groups, order, slow):
        self.groups, self.order, self.parts = groups, order, []
        self.far = (True,) * slow

    def add(self, kept, sent):
        self.width = kept.shape[2]
        self.parts.append([kept, swap(sent, "dp", 1)])

    def across(self, turn, first, second):
        self.got = (
            swap(first, "section", 1 + turn),
            swap(second, "section", 2 - turn),
        )

    def first(self, misc=()):
        groups, width = self.groups, self.width
        ins = [kept for kept, _ in self.parts] + [got for _, got in self.parts] + list(misc)
        self.keep_a, send_a, self.keep_b, send_b = self.order.call(
            functools.partial(first_body, bool(misc)),
            [(item,) for item in ins],
            [((2, groups.half, width), BFLOAT, *self.far), ((2, groups.half, width), BFLOAT)] * 2,
            4.0,
            scratch=[pltpu.VMEM((4, groups.rows, width), BFLOAT)],
        )
        self.across(0, send_a, send_b)

    def second(self):
        self.keep_a, send_a, self.keep_b, send_b = self.order.call(
            second_body,
            [(self.keep_a,), (self.got[0],), (self.keep_b,), (self.got[1],)],
            [
                ((self.groups.half, self.width), BFLOAT, *self.far),
                ((self.groups.half, self.width), BFLOAT),
            ]
            * 2,
            1.5,
        )
        self.across(1, send_a, send_b)

    def third(self):
        groups, width = self.groups, self.width
        outs = []
        if groups.expert:
            outs += [((groups.expert // 2, width), BFLOAT)] * 2
        if groups.shared:
            outs += [((groups.shared + groups.every, width), BFLOAT)]
        outs = self.order.call(
            functools.partial(third_body, groups),
            [(self.keep_a,), (self.got[0],), (self.keep_b,), (self.got[1],)],
            outs,
            1.5,
            scratch=[pltpu.VMEM((groups.rows, width), BFLOAT)],
        )
        self.expert = list(outs[:2]) if groups.expert else []
        if groups.shared:
            columns = outs[-1]
            self.columns = [columns, swap(columns, "expert", 1), swap(columns, "expert", 2)]

    def relay(self):
        self.columns.append(swap(self.order.tie(self.columns[2]), "expert", 1))

    def column(self, joined):
        ins = self.expert * joined + self.columns
        rows = self.groups.sent - self.groups.expert // 2 * (not joined)
        return Spread(
            self.order,
            self.order.call(
                functools.partial(column_body, self.groups, joined),
                [(item,) for item in ins],
                [((rows, self.width), BFLOAT)] * 2,
                1.5,
            ),
        )


class Spread:
    def __init__(self, order, own):
        self.order, self.own = order, own
        self.got = [swap(own[0], "section", 2), swap(own[1], "section", 1)]

    def pair(self):
        self.own = self.order.call(
            pair_body,
            [(self.own[0],), (self.got[0],), (self.own[1],), (self.got[1],)],
            [((2,) + item.shape, BFLOAT) for item in self.own],
            1.7,
        )
        self.got = [swap(self.own[0], "section", 1), swap(self.own[1], "section", 2)]
        self.other_own = [swap(item, "dp", 1) for item in self.own]

    def finish(self):
        for item in self.other_own:
            self.order.wait(item)
        other_got = [swap(item, "dp", 1) for item in self.got]
        own, got, other_own = self.own, self.got, self.other_own
        self.all = [own[0], got[0], own[1], got[1]]
        self.all += [other_own[0], other_got[0], other_own[1], other_got[1]]


def table_rows(steps, rows):
    count, width = steps.shape[1], rows.shape[1]
    lanes = lax.broadcasted_iota(jnp.int32, (1000, count), 1)
    places = lax.broadcasted_iota(jnp.int32, (1000, count), 0)
    marks = jnp.where((places == steps) & (lanes < 32), 1.0, 0.0).astype(BFLOAT)
    wide = jnp.concatenate([rows, jnp.zeros((count - 32, width), FLOAT)]).astype(BFLOAT)
    return product(marks, wide)


def final_body(groups, last, place, *refs):
    parts, refs = refs[:8], refs[8:]
    if last:
        small_one, bias_one, *refs = refs
        refs = refs[6:]
    up, down, bias, s_up, s_down, qkv, out_w, small, *refs = refs
    *refs, data = refs
    step = pl.program_id(0)
    core, y, x = place[0], place[1], place[2]

    @pl.when(step == 0)
    def _():
        for chip in range(2):
            own_a, got_a, own_b, got_b = parts[4 * chip : 4 * chip + 4]
            owner = 1 - core if chip else core
            for other in range(2):
                data[owner, 2 * other + x, 0] = own_a[other]
                data[owner, 2 * other + 1 - x, 0] = got_a[other]
                data[owner, 2 * y + other, 1] = own_b[other]
                data[owner, 2 * (1 - y) + other, 1] = got_b[other]

    rows = groups.expert // 2
    for part in range(4):

        @pl.when(step == 2 * part)
        def _(part=part):
            for out, owner in ((up, 0), (down, 1)):
                both = data[owner, part, :, :rows, :].reshape(groups.expert, -1)
                out[...] = both[: groups.expert - 32].astype(FLOAT)
                if owner == 0 and part == 0:
                    bias[...] = both[groups.expert - 32 :].astype(FLOAT)

    half = groups.shared // 2
    for number in range(8):

        @pl.when(step == number)
        def _(number=number):
            at, block = rows + number // 2 * half, number % 2
            for out, owner in ((s_up, 0), (s_down, 1)):
                both = data[owner, 2 * block : 2 * block + 2, :, at : at + half, :]
                out[...] = both.reshape(4 * half, -1).astype(FLOAT)

    every = groups.every // 2
    real = groups.every - 32
    start = rows + 4 * half
    for part in range(4):

        @pl.when(step == 2 * part)
        def _(part=part):
            target = qkv if part < 3 else out_w
            for piece in range(2):
                number = 2 * (part % 2) + piece
                both = data[part // 2, number, :, start : start + every, :]
                both = both.reshape(groups.every, -1)
                target[real * piece : real * (piece + 1), :] = both[32:].astype(FLOAT)
                if part < 2:
                    small[number] = both[:32].astype(FLOAT)

    if last:

        @pl.when(step == 7)
        def _():
            qv_b, out_b, router, s_upb, s_downb, e_upb, e_downb, table, counts = refs
            width = data.shape[4]
            for layer, rest, biases in ((0, small, bias), (1, small_one, bias_one)):
                at = slice(layer, layer + 1)
                for row in range(2):
                    qv_b[at, row * width : (row + 1) * width] = rest[0, row : row + 1, :]
                out_b[at, :] = rest[0, 2:3, :]
                turned = jnp.transpose(
                    jnp.concatenate([rest[0, 3:7, :], jnp.zeros((124, width), FLOAT)])
                )
                router[layer] = turned[:, :4]
                for row in range(8):
                    s_upb[at, row * width : (row + 1) * width] = rest[0, 7 + row : 8 + row, :]
                s_downb[at, :] = rest[0, 15:16, :]
                for row in range(4):
                    e_upb[layer, :, row * width : (row + 1) * width] = biases[row : row + 1, :]
                e_downb[layer] = biases[4:5, :]
            steps = 32.0 * small[2, 0:1, :128] + small[2, 1:2, :128]
            table[...] = table_rows(steps.astype(jnp.int32), small[1])
            spots = lax.broadcasted_iota(jnp.int32, (256, 128), 0) % 8
            lanes = lax.broadcasted_iota(jnp.int32, (256, 128), 1)
            marks = jnp.where(spots == lanes, 1.0, 0.0).astype(BFLOAT)
            numbers = small[2, 0:8, :256].astype(BFLOAT)
            counts[...] = product(numbers, marks)[2:3, :].astype(jnp.int32)


def final_call(groups, layer, order, parts, before, hide=()):
    width = parts[0].shape[2]
    outs = [
        (2, 1, width, 4 * width),
        (2, 1, 4 * width, width),
        (32, width),
        (2, width, 8 * width),
        (2, 8 * width, width),
        (2, width, 3 * width),
        (2, width, width),
        (4, 32, width),
    ]
    specs = [
        pl.BlockSpec((None, None, width, width), lambda i, _: (layer, 0, 0, i // 2)),
        pl.BlockSpec((None, None, width, width), lambda i, _: (layer, 0, i // 2, 0)),
        pl.BlockSpec((32, width), lambda i, _: (0, 0)),
        pl.BlockSpec((None, width, width), lambda i, _: (layer, 0, i)),
        pl.BlockSpec((None, width, width), lambda i, _: (layer, i, 0)),
        pl.BlockSpec((None, width, width), lambda i, _: (layer, 0, jnp.minimum(i // 2, 2))),
        pl.BlockSpec((None, width, width), lambda i, _: (layer, 0, 0)),
        pl.BlockSpec((4, 32, width), lambda i, _: (0, 0, 0)),
    ]
    ins = list(parts)
    in_specs = [
        pl.BlockSpec(item.shape, lambda *_: (0, 0, 0), pipeline_mode=pl.Buffered(1))
        for item in parts
    ]
    aliases = {}
    shapes = [jax.ShapeDtypeStruct(shape, FLOAT) for shape in outs]
    if before is not None:
        ins += [before[7], before[2]]
        in_specs += [whole_spec(before[7]), whole_spec(before[2])]
        for number in (0, 1, 3, 4, 5, 6):
            aliases[1 + len(ins)] = number
            ins.append(before[number])
            in_specs.append(pl.BlockSpec(memory_space=pl.ANY))
        rest = [
            (2, 2 * width),
            (2, width),
            (2, width, 4),
            (2, 8 * width),
            (2, width),
            (2, 1, 4 * width),
            (2, 1, width),
            (1000, width),
        ]
        shapes += [jax.ShapeDtypeStruct(shape, FLOAT) for shape in rest]
        shapes += [jax.ShapeDtypeStruct((1, 128), jnp.int32)]
        specs += [
            pl.BlockSpec(item.shape, lambda *_, rank=len(item.shape): (0,) * rank)
            for item in shapes[8:]
        ]
    outs = pl.pallas_call(
        functools.partial(final_body, groups, before is not None),
        out_shape=shapes,
        grid_spec=pltpu.PrefetchScalarGridSpec(
            num_scalar_prefetch=1,
            grid=(8,),
            in_specs=in_specs,
            out_specs=specs,
            scratch_shapes=[pltpu.VMEM((2, 4, 2, parts[0].shape[1], width), BFLOAT)],
        ),
        input_output_aliases=aliases,
        cost_estimate=pl.CostEstimate(flops=int(8e9), bytes_accessed=16 << 20, transcendentals=0),
        compiler_params=pltpu.CompilerParams(vmem_limit_bytes=50 << 20),
    )(order.place, *ins)
    outs, hide = order.arrive((outs, hide))
    return outs, hide


def extra_plane_body(place, own_a, got_a, own_b, got_b, out_a, out_b):
    y, x = place[1], place[2]
    for other in range(2):
        out_a[2 * other + x] = own_a[other]
        out_a[2 * other + 1 - x] = got_a[other]
        out_b[2 * y + other] = own_b[other]
        out_b[2 * (1 - y) + other] = got_b[other]


class ExtraExpert:
    def __init__(self, layer, order, number, up, down):
        width, units = up.shape[2], up.shape[3]
        some_up = lax.dynamic_slice(
            up, (layer, 0, number * (width // 8), 0), (1, 1, width // 8, units)
        ).reshape(width // 8, units)
        some_down = lax.dynamic_slice(
            down, (layer, 0, number * (units // 8), 0), (1, 1, units // 8, width)
        ).reshape(units // 8, width)
        self.order = order
        self.shapes = [some_up.shape, some_down.shape]
        self.own = [swap(some_up, "expert", 2), swap(some_down, "expert", 2)]

    def across(self, after):
        self.own = [lax.optimization_barrier((item, after))[0] for item in self.own]
        self.got = [swap(self.own[0], "section", 2), swap(self.own[1], "section", 1)]

    def pair(self):
        self.own = self.order.call(
            pair_body,
            [(self.own[0],), (self.got[0],), (self.own[1],), (self.got[1],)],
            [((2,) + shape, BFLOAT) for shape in self.shapes],
            1.7,
        )
        self.got = [swap(self.own[0], "section", 1), swap(self.own[1], "section", 2)]

    def plane(self):
        up, down = self.order.call(
            extra_plane_body,
            [(self.own[0],), (self.got[0],), (self.own[1],), (self.got[1],)],
            [((4,) + shape, BFLOAT) for shape in self.shapes],
            1.7,
        )
        self.all = [up, swap(up, "dp", 1), down, swap(down, "dp", 1)]


def shards_fast(
    tokens,
    timesteps,
    routes_one,
    routes_two,
    cotangent,
    time_table,
    ada_weight,
    ada_bias,
    qkv_weight,
    qv_bias,
    out_weight,
    out_bias,
    router_weight,
    shared_up,
    shared_up_bias,
    shared_down,
    shared_down_bias,
    expert_up,
    expert_up_bias,
    expert_down,
    expert_down_bias,
):
    width = tokens.shape[1]
    rows = tokens.shape[0]
    bf, fl = BFLOAT, FLOAT
    experts_total = router_weight.shape[2]
    core, y, x_bit = bits()
    place = jnp.stack([core, y, x_bit, lax.axis_index("expert")]).astype(jnp.int32)
    routers = jnp.pad(router_weight, ((0, 0), (0, 0), (0, 128 - experts_total)))

    order = Order(place)
    number = core * 4 + y * 2 + x_bit
    hidden_units = expert_up.shape[3]
    first_extra = ExtraExpert(0, order, number, expert_up, expert_down)
    half_steps = ordered(x_bit, timesteps[0], swap(timesteps[0], "section", 1))
    number = lax.optimization_barrier((number, half_steps))[0]
    second_extra = ExtraExpert(1, order, number, expert_up, expert_down)
    steps = ordered(y, half_steps, swap(half_steps, "section", 2)).reshape(4)
    embedded = jnp.take(time_table, steps, axis=0)
    condition = jax.nn.silu(embedded.astype(FLOAT)).astype(BFLOAT)
    section_mod = product(condition, ada_weight[0]) + ada_bias[0].astype(FLOAT)
    mods = lax.all_to_all(section_mod, "section", 0, 0, tiled=True).reshape(12, width)
    first_extra.across(section_mod)
    first_extra.pair()
    own_bias = jnp.concatenate([expert_up_bias[:, 0], expert_down_bias[:, 0]], -1)
    own_bias = lax.optimization_barrier((own_bias, section_mod))[0]
    extra_bias = swap(own_bias, "expert", 2)

    def with_bias(layer, extra):
        bias = extra_bias[layer : layer + 1]
        return [*(far(item) for item in extra.all), bias[:, :hidden_units], bias[:, hidden_units:]]

    weights = (
        far(shared_up),
        shared_up_bias,
        far(shared_down),
        shared_down_bias,
        far(expert_up),
        expert_up_bias,
        far(expert_down),
        expert_down_bias,
    )

    size = rows + 16
    block_outs = [
        ((rows, width), bf, True),
        ((rows, 3 * width), bf, True),
        ((rows, width), bf, True),
        ((rows, width), fl, True),
        ((rows, width), bf, True),
        ((size, width), bf),
        ((rows, 128), fl, True),
    ]

    def attn_ins(layer, routes):
        return [
            (mods,),
            (qkv_weight, layer_spec(qkv_weight, layer)),
            (qv_bias,),
            (out_weight, layer_spec(out_weight, layer)),
            (out_bias,),
            (routers, layer_spec(routers, layer)),
            (routes,),
        ]

    def z(x, by):
        return swap(order.tie(x), "expert", by)

    (hidden0, qkv0, attended0, branch0, stream1, message1, gates1, last_grad), (first_extra.got,) = (
        order.call(
            functools.partial(attention_forward_body, 0),
            [(tokens,), (cotangent,), *attn_ins(0, routes_one)],
            block_outs + [((rows, width), bf)],
            4.2,
            hide=[first_extra.got],
        )
    )
    got1 = swap(message1, "expert", 1)
    first_extra.plane()
    (shared1,), (got1, first_extra.all) = shared_call(
        0, True, False, order, message1, None, weights, hide=[got1, first_extra.all]
    )
    extra0 = with_bias(0, first_extra)
    sent1, kept_got1 = experts_call(
        0, True, False, order, got1, None, None, weights, extra0, None, ()
    )
    back1 = swap(sent1, "expert", 1)
    second_extra.across(sent1)
    (own1, kept_own1), (back1,) = experts_call(
        0, True, False, order, message1, gates1, None, weights, extra0, None, (shared1,),
        hide=[back1],
    )
    got_last = z(last_grad, 1)
    second_extra.pair()
    (stream2, branch1, hidden2, qkv2, attended2, branch2, stream3, message3, gates3), (got_last,) = (
        order.call(
            functools.partial(attention_forward_body, 2),
            [(stream1,), (own1,), (back1,), *attn_ins(1, routes_two)],
            [((rows, width), bf, True), ((rows, width), fl, True)] + block_outs,
            4.2,
            hide=[got_last],
        )
    )
    got3 = swap(message3, "expert", 1)
    second_extra.plane()
    (shared3, shared_grad3), (got3, second_extra.all) = shared_call(
        1, True, True, order, message3, last_grad, weights, hide=[got3, second_extra.all]
    )
    far_last = z(last_grad, 2)
    extra1 = with_bias(1, second_extra)
    (sent3, back_message3), (far_last,) = experts_call(
        1, True, True, order, got3, None, got_last, weights, extra1, None, (), hide=[far_last]
    )
    back_grad3 = swap(back_message3, "expert", 1)
    far3 = z(message3, 2)
    (own3, own_grad3, gate_grad3), (back_grad3, far3) = experts_call(
        1, True, True, order, message3, gates3, last_grad, weights, extra1, None,
        (shared3, shared_grad3), hide=[back_grad3, far3],
    )
    farther_last, farther3 = z(far_last, 1), z(far3, 1)
    grad_outs = [((4, width // 2 + 32, width), bf)] * 2 + [((16, width), fl)]
    proj = [pltpu.VMEM((rows, 3 * width), bf)]

    def attn_back_ins(layer):
        return [
            (mods,),
            (routers, layer_spec(routers, layer)),
            (qkv_weight, layer_spec(qkv_weight, layer)),
            (out_weight, layer_spec(out_weight, layer)),
        ]

    groups = Groups(width + 32, width // 2, width // 2 + 32)
    flow1, flow0 = Flow(groups, order, True), Flow(groups, order, False)
    (grad1, branch_grad1, kept_a, sent_a, small1), (farther_last, farther3) = order.call(
        functools.partial(attention_backward_body, 2),
        [
            (item,)
            for item in (
                cotangent, stream3, message3, own_grad3, back_grad3, gates3, gate_grad3,
                stream2, hidden2, qkv2, attended2, branch2,
            )
        ]
        + attn_back_ins(1)
        + [(branch1,)],
        [((rows, width), bf), ((rows, width), bf)] + grad_outs,
        7.7,
        hide=[farther_last, farther3],
        scratch=proj,
    )
    got_grad1 = swap(branch_grad1, "expert", 1)
    (shared_grad1,), (got_grad1,) = shared_call(
        0, False, True, order, message1, branch_grad1, weights, hide=[got_grad1]
    )
    far_grad1, far1, back3 = z(branch_grad1, 2), z(message1, 2), z(sent3, 1)
    (kept, sent), (far_grad1, far1, back3) = weight_grads_call(
        1,
        True,
        True,
        order,
        [(item,) for item in (message3, got3, far3, farther3)],
        [(item,) for item in (last_grad, got_last, far_last, farther_last)],
        weights,
        hide=[far_grad1, far1, back3],
    )
    flow1.add(kept, sent)
    flow1.add(kept_a, sent_a)
    (back_message1,), (flow1.parts[0][1], flow1.parts[1][1]) = experts_call(
        0, False, True, order, got1, None, got_grad1, weights, extra0, kept_got1, (),
        hide=[flow1.parts[0][1], flow1.parts[1][1]],
    )
    back_grad1 = swap(back_message1, "expert", 1)
    flow1.first()
    (own_grad1, gate_grad1), (back_grad1,) = experts_call(
        0, False, True, order, message1, gates1, branch_grad1, weights, extra0, kept_own1,
        (shared_grad1,), hide=[back_grad1],
    )
    farther1, farther_grad1 = z(far1, 1), z(far_grad1, 1)
    (token_grad, kept_a, sent_a, small0), (farther1, farther_grad1) = order.call(
        functools.partial(attention_backward_body, 0),
        [
            (item,)
            for item in (
                grad1, stream1, message1, own_grad1, back_grad1, gates1, gate_grad1,
                tokens, hidden0, qkv0, attended0, branch0,
            )
        ]
        + attn_back_ins(0),
        [((rows, width), fl)] + grad_outs,
        7.7,
        hide=[farther1, farther_grad1],
        scratch=proj,
    )
    flow1.second()

    branch3 = own3 + back3.astype(FLOAT)
    output = (stream3.astype(FLOAT) + mods[11:12] * branch3).astype(BFLOAT)
    gating3 = jnp.sum(cotangent.astype(FLOAT) * branch3, 0, keepdims=True)
    own_condition = jax.nn.silu(lax.dynamic_slice_in_dim(embedded, 2 * y + x_bit, 1).astype(FLOAT))
    own_condition = own_condition.astype(BFLOAT).astype(FLOAT)
    none = jnp.zeros((4, width), FLOAT)
    to_sections = jnp.concatenate(
        [
            small0[3:5], small0[2:3], own_condition, none,
            small0[0:2], small1[5:6], own_condition, none,
            small1[3:5], small1[2:3], own_condition, none,
            small1[0:2], gating3, own_condition, none,
        ]
    )
    to_sections = to_sections.reshape(4, 8, width)
    section = 2 * y + x_bit

    image = core * 4 + lax.axis_index("expert")
    spots = jnp.arange(32)[:, None] == jnp.arange(4)[None, :] * 8 + image
    def counted(route_pair):
        numbers = jnp.arange(experts_total, dtype=jnp.int32)
        return jnp.sum((route_pair.reshape(-1)[:, None] == numbers[None, :]).astype(FLOAT), 0)

    device = section * 8 + image
    counts = jnp.tile(jnp.concatenate([counted(routes_one), counted(routes_two)]), 32)
    places = jnp.arange(width) // (2 * experts_total)
    counts = jnp.where(places == device, jnp.pad(counts, (0, width - 64 * experts_total)), 0.0)
    is_mine = jnp.arange(width) == device
    high, low = timesteps[0] // 32, timesteps[0] % 32
    def toward(by):
        return lax.dynamic_index_in_dim(to_sections, section ^ by, 0, keepdims=False)

    factors = [toward(0)] + [swap(toward(by), "section", by) for by in (1, 2, 3)]
    sources0 = (
        [(item,) for item in (message1, got1, far1, farther1)],
        [(item,) for item in (branch_grad1, got_grad1, far_grad1, farther_grad1)],
    )
    (kept, sent), (factors, flow1.got) = weight_grads_call(
        0, True, True, order, *sources0, weights, hide=[factors, flow1.got]
    )
    flow1.third()
    factors = jnp.take(jnp.stack(factors), jnp.arange(4) ^ section, axis=0)
    flow0.add(kept, sent)
    flow0.add(kept_a, sent_a)

    low_grads = factors[:, :3].reshape(4, 3 * width).astype(BFLOAT)
    condition_grad = back_product(low_grads, ada_weight[0])
    embed_grad = jax.vjp(jax.nn.silu, embedded.astype(FLOAT))[1](condition_grad)[0]
    embed_rows = jnp.sum(jnp.where(spots[:, :, None], embed_grad[None], 0.0), 1)

    misc = jnp.concatenate(
        [
            embed_rows,
            jnp.where(is_mine, high.astype(FLOAT), 0.0)[None],
            jnp.where(is_mine, low.astype(FLOAT), 0.0)[None],
            counts[None],
            jnp.zeros((29, width), FLOAT),
        ]
    )
    got_misc = swap(misc, "dp", 1)
    factors = ordered(core, factors, swap(factors, "dp", 1))
    flow0.first((misc, got_misc))
    flow0.got, flow1.columns, factors = order.arrive((flow0.got, flow1.columns, factors))
    flow1.relay()
    flow0.second()
    turns = [factors] + [z(factors, by) for by in (1, 2)]
    flow0.got, flow1.columns, turns = order.arrive((flow0.got, flow1.columns, turns))
    spread1 = flow1.column(True)
    flow0.third()
    turns.append(z(turns[2], 1))
    flow0.columns, spread1.got, turns = order.arrive((flow0.columns, spread1.got, turns))
    spread1.pair()
    flow0.relay()
    flow0.columns, spread1.other_own = order.arrive((flow0.columns, spread1.other_own))
    spread0 = flow0.column(True)
    turns = jnp.take(jnp.stack(turns), jnp.arange(4) ^ place[3], axis=0)
    factors = turns.reshape(32, 8, width)
    mod_grads = factors[:, :3].reshape(-1, 3 * width)
    ada_out = lead_product(factors[:, 3].astype(BFLOAT), mod_grads.astype(BFLOAT))[None]
    ada_bias_out = jnp.sum(mod_grads, 0)[None]
    spread1.got, spread0.got, ada_out, ada_bias_out = order.arrive(
        (spread1.got, spread0.got, ada_out, ada_bias_out)
    )
    spread1.finish()
    spread0.pair()
    spread1.all, spread0.other_own = order.arrive((spread1.all, spread0.other_own))
    finals, spread0.got = final_call(groups, 1, order, spread1.all, None, spread0.got)
    spread0.finish()
    finals, _ = final_call(groups, 0, order, spread0.all, finals)
    e_up_out, e_down_out, _, s_up_out, s_down_out, qkv_out, out_w_out, _, *rest = finals
    qv_out, out_b_out, router_out, s_upb_out, s_downb_out, *rest = rest
    e_upb_out, e_downb_out, table_out, counts_out = rest
    counts_out = counts_out[0, : 2 * experts_total].reshape(2, experts_total)

    return (
        output,
        token_grad,
        table_out,
        ada_out,
        ada_bias_out,
        qkv_out,
        qv_out,
        out_w_out,
        out_b_out,
        router_out,
        s_up_out,
        s_upb_out,
        s_down_out,
        s_downb_out,
        e_up_out,
        e_upb_out,
        e_down_out,
        e_downb_out,
        counts_out,
    )


def shards(*args):
    fits = (
        lax.axis_size("section") == 4
        and lax.axis_size("dp") == 2
        and lax.axis_size("expert") == 4
        and args[12].shape[2] == 4
        and args[1].shape[0] == 1
    )
    return (shards_fast if fits else shards_general)(*args)


def solution(mesh):
    rows = P(ALL, None)
    whole = P()
    placed = (
        rows,
        P(ALL),
        rows,
        rows,
        rows,
        whole,
        P("section", None, None),
        P("section", None),
        *([whole] * 9),
        P(None, "expert", None, None),
        P(None, "expert", None),
        P(None, "expert", None, None),
        P(None, "expert", None),
    )
    return jax.shard_map(
        shards,
        mesh=mesh,
        in_specs=placed,
        out_specs=(
            rows,
            rows,
            whole,
            P("section", None, None),
            P("section", None),
            *([whole] * 9),
            P(None, "expert", None, None),
            P(None, "expert", None),
            P(None, "expert", None, None),
            P(None, "expert", None),
            whole,
        ),
        check_vma=False,
    )
```

```python
import functools

import jax
import jax.numpy as jnp
from jax import lax
from jax.experimental import pallas as pl
from jax.experimental.pallas import tpu as pltpu
from jax.sharding import PartitionSpec as P

HEADS = 6
HD = 64

BFLOAT = jnp.bfloat16
FLOAT = jnp.float32
ALL = ("section", "dp", "expert")


def product(left_arg, right_arg):
    return jnp.dot(left_arg, right_arg, preferred_element_type=FLOAT)


def lead_product(left_arg, right_arg):
    return lax.dot_general(
        left_arg, right_arg, (((0,), (0,)), ((), ())), preferred_element_type=FLOAT
    )


def back_product(left_arg, right_arg):
    return lax.dot_general(
        left_arg, right_arg, (((1,), (1,)), ((), ())), preferred_element_type=FLOAT
    )


def gelu_parts(pre):
    inner = 0.7978845608028654 * (pre + 0.044715 * pre * pre * pre)
    tanh = jnp.tanh(inner)
    act = 0.5 * pre * (1.0 + tanh)
    slope = 0.5 * (1.0 + tanh) + 0.5 * pre * (1.0 - tanh * tanh) * 0.7978845608028654 * (
        1.0 + 3 * 0.044715 * pre * pre
    )
    return act, slope


def normalized(stream):
    row_mean = jnp.mean(stream, -1, keepdims=True)
    centred = stream - row_mean
    variance = jnp.mean(centred * centred, -1, keepdims=True)
    inverse = lax.rsqrt(variance + 1e-06)
    return centred * inverse, inverse


def modulate(stream, mod):
    unit, _ = normalized(stream)
    return (unit * (1.0 + mod[1]) + mod[0]).astype(BFLOAT)


def norm_backward(stream, mod, hidden_grad):
    unit, inverse = normalized(stream)
    shift_grad = jnp.sum(hidden_grad, 0)
    scale_grad = jnp.sum(hidden_grad * unit, 0)
    unit_grad = hidden_grad * (1.0 + mod[1])
    stream_grad = inverse * (
        unit_grad
        - jnp.mean(unit_grad, -1, keepdims=True)
        - unit * jnp.mean(unit_grad * unit, -1, keepdims=True)
    )
    return stream_grad, shift_grad, scale_grad


def heads_view(rows):
    return rows.astype(BFLOAT).reshape(-1, HEADS, HD)


def attention_forward(hidden, weights):
    qkv_matrix, qv_offset, out_matrix, out_offset = weights
    width = hidden.shape[1]
    projected = product(hidden, qkv_matrix)
    query = heads_view(projected[:, :width] + qv_offset[:width])
    key = heads_view(projected[:, width : 2 * width])
    value = heads_view(projected[:, 2 * width :] + qv_offset[width:])
    scores = jnp.einsum("qhd,khd->hqk", query, key, preferred_element_type=FLOAT) * HD ** (-0.5)
    probs = jax.nn.softmax(scores, -1)
    probs_low = probs.astype(BFLOAT)
    attended = (
        jnp.einsum("hqk,khd->qhd", probs_low, value, preferred_element_type=FLOAT)
        .reshape(-1, width)
        .astype(BFLOAT)
    )
    branch = product(attended, out_matrix) + out_offset
    return branch, (query, key, value, probs, probs_low, attended)


def attention_backward(hidden, weights, saved, branch_grad):
    qkv_matrix, _, out_matrix, _ = weights
    query, key, value, probs, probs_low, attended = saved
    width = hidden.shape[1]
    factor = HD ** (-0.5)
    low_grad = branch_grad.astype(BFLOAT)
    out_grad = lead_product(attended, low_grad)
    out_offset_grad = jnp.sum(low_grad.astype(FLOAT), 0)
    attended_grad = heads_view(back_product(low_grad, out_matrix))
    value_grad = jnp.einsum("hqk,qhd->khd", probs_low, attended_grad, preferred_element_type=FLOAT)
    prob_grad = jnp.einsum("qhd,khd->hqk", attended_grad, value, preferred_element_type=FLOAT)
    score_grad = (probs * (prob_grad - jnp.sum(prob_grad * probs, -1, keepdims=True))).astype(
        BFLOAT
    )
    query_grad = (
        jnp.einsum("hqk,khd->qhd", score_grad, key, preferred_element_type=FLOAT) * factor
    )
    key_grad = (
        jnp.einsum("hqk,qhd->khd", score_grad, query, preferred_element_type=FLOAT) * factor
    )
    proj_grad = jnp.concatenate(
        [item.reshape(-1, width) for item in (query_grad, key_grad, value_grad)], -1
    ).astype(BFLOAT)
    qkv_grad = lead_product(hidden, proj_grad)
    sums = jnp.sum(proj_grad.astype(FLOAT), 0)
    offset_grad = jnp.concatenate([sums[:width], sums[2 * width :]])
    hidden_grad = back_product(proj_grad, qkv_matrix)
    return hidden_grad, (qkv_grad, offset_grad, out_grad, out_offset_grad)


def expert_gates(rows, router, route_pair):
    logits = product(rows, router)
    marks = (
        route_pair[:, :, None] == jnp.arange(router.shape[1], dtype=jnp.int32)[None, None, :]
    ).any(1)
    top = jnp.max(jnp.where(marks, logits, -jnp.inf), -1, keepdims=True)
    raised = jnp.where(marks, jnp.exp(logits - top), 0.0)
    return raised / jnp.sum(raised, -1, keepdims=True)


def pick_column(table, column):
    return lax.dynamic_slice_in_dim(table, column, 1, axis=1)


def moe_forward(hidden, route_pair, weights):
    router, s_up, s_upb, s_down, s_downb, e_up, e_upb, e_down, e_downb = weights
    mine = lax.axis_index("expert")
    rows = lax.all_gather(hidden, "expert", axis=0, tiled=True)
    routes = lax.all_gather(route_pair, "expert", axis=0, tiled=True)
    gates = expert_gates(rows, router, routes)
    gate = pick_column(gates, mine)
    shared_pre = product(hidden, s_up) + s_upb
    shared_act, shared_slope = gelu_parts(shared_pre)
    shared_act = shared_act.astype(BFLOAT)
    shared_out = product(shared_act, s_down) + s_downb
    pre = product(rows, e_up[0]) + e_upb[0]
    act, slope = gelu_parts(pre)
    act = act.astype(BFLOAT)
    result = (product(act, e_down[0]) + e_downb[0]).astype(BFLOAT)
    routed = lax.psum_scatter(
        (gate * result.astype(FLOAT)).astype(BFLOAT), "expert", scatter_dimension=0, tiled=True
    )
    branch = shared_out + routed.astype(FLOAT)
    saved = (rows, routes, gates, gate, shared_act, shared_slope, act, slope, result)
    return branch, saved


def moe_backward(hidden, weights, saved, branch_grad):
    router, s_up, s_upb, s_down, s_downb, e_up, e_upb, e_down, e_downb = weights
    rows, routes, gates, gate, shared_act, shared_slope, act, slope, result = saved
    mine = lax.axis_index("expert")
    devices = lax.axis_size("expert")
    tokens_here = hidden.shape[0]
    low_grad = branch_grad.astype(BFLOAT)
    s_down_grad = lead_product(shared_act, low_grad)
    s_downb_grad = jnp.sum(low_grad.astype(FLOAT), 0)
    shared_dpre = (back_product(low_grad, s_down) * shared_slope).astype(BFLOAT)
    s_up_grad = lead_product(hidden, shared_dpre)
    s_upb_grad = jnp.sum(shared_dpre.astype(FLOAT), 0)
    hidden_grad = back_product(shared_dpre, s_up)
    row_grad = lax.all_gather(low_grad, "expert", axis=0, tiled=True).astype(FLOAT)
    gate_grad = jnp.sum(row_grad * result.astype(FLOAT), -1)
    gate_grads = lax.all_to_all(
        gate_grad.reshape(devices, tokens_here).astype(BFLOAT), "expert", 0, 0, tiled=True
    ).astype(FLOAT)
    own_gates = lax.dynamic_slice_in_dim(gates, mine * tokens_here, tokens_here, axis=0)
    gate_grads = gate_grads.T
    logit_grad = own_gates * (gate_grads - jnp.sum(own_gates * gate_grads, -1, keepdims=True))
    router_grad = lax.dot_general(
        hidden.astype(FLOAT),
        logit_grad,
        (((0,), (0,)), ((), ())),
        precision=lax.Precision.HIGHEST,
        preferred_element_type=FLOAT,
    )
    result_grad = (gate * row_grad).astype(BFLOAT)
    e_down_grad = lead_product(act, result_grad)
    e_downb_grad = jnp.sum(result_grad.astype(FLOAT), 0)
    dpre = (back_product(result_grad, e_down[0]) * slope).astype(BFLOAT)
    e_up_grad = lead_product(rows, dpre)
    e_upb_grad = jnp.sum(dpre.astype(FLOAT), 0)
    back_rows = lax.psum_scatter(
        back_product(dpre, e_up[0]).astype(BFLOAT), "expert", scatter_dimension=0, tiled=True
    )
    hidden_grad = hidden_grad + back_product(logit_grad, router.astype(FLOAT)) + back_rows
    return hidden_grad, (
        router_grad,
        s_up_grad,
        s_upb_grad,
        s_down_grad,
        s_downb_grad,
        e_up_grad,
        e_upb_grad,
        e_down_grad,
        e_downb_grad,
    )


def shards_general(
    tokens,
    timesteps,
    routes_one,
    routes_two,
    cotangent,
    time_table,
    ada_weight,
    ada_bias,
    qkv_weight,
    qv_bias,
    out_weight,
    out_bias,
    router_weight,
    shared_up,
    shared_up_bias,
    shared_down,
    shared_down_bias,
    expert_up,
    expert_up_bias,
    expert_down,
    expert_down_bias,
):
    width = tokens.shape[1]
    steps_count = time_table.shape[0]
    experts_total = router_weight.shape[2]
    route_sets = (routes_one, routes_two)
    steps = lax.all_gather(timesteps, "section", axis=0, tiled=True)
    embedded = jnp.take(time_table, steps, axis=0).astype(FLOAT)
    condition = jax.nn.silu(embedded).astype(BFLOAT)
    section_mod = product(condition, ada_weight[0]) + ada_bias[0].astype(FLOAT)
    mods = lax.all_to_all(section_mod, "section", 0, 0, tiled=True).reshape(-1, 3, width)

    def attn_weights(layer):
        return (
            qkv_weight[layer],
            qv_bias[layer].astype(FLOAT),
            out_weight[layer],
            out_bias[layer].astype(FLOAT),
        )

    def moe_weights(layer):
        return (
            router_weight[layer],
            shared_up[layer],
            shared_up_bias[layer].astype(FLOAT),
            shared_down[layer],
            shared_down_bias[layer].astype(FLOAT),
            expert_up[layer],
            expert_up_bias[layer].astype(FLOAT),
            expert_down[layer],
            expert_down_bias[layer].astype(FLOAT),
        )

    streams, hiddens, branches, kept = [], [], [], []
    stream = tokens
    for block in range(4):
        layer = block // 2
        streams.append(stream)
        wide = stream.astype(FLOAT)
        hidden = modulate(wide, mods[block])
        if block % 2 == 0:
            branch, saved = attention_forward(hidden, attn_weights(layer))
        else:
            branch, saved = moe_forward(hidden, route_sets[layer], moe_weights(layer))
        hiddens.append(hidden)
        branches.append(branch)
        kept.append(saved)
        stream = (wide + mods[block][2] * branch).astype(BFLOAT)
    output = stream

    upstream = cotangent
    mod_grads = [None] * 4
    attn_grads = [None] * 2
    moe_grads = [None] * 2
    for block in (3, 2, 1, 0):
        layer = block // 2
        wide_grad = upstream.astype(FLOAT)
        gating_grad = jnp.sum(wide_grad * branches[block], 0)
        branch_grad = mods[block][2] * wide_grad
        if block % 2 == 0:
            hidden_grad, attn_grads[layer] = attention_backward(
                hiddens[block], attn_weights(layer), kept[block], branch_grad
            )
        else:
            hidden_grad, moe_grads[layer] = moe_backward(
                hiddens[block], moe_weights(layer), kept[block], branch_grad
            )
        stream_grad, shift_grad, scale_grad = norm_backward(
            streams[block].astype(FLOAT), mods[block], hidden_grad
        )
        mod_grads[block] = jnp.concatenate([shift_grad, scale_grad, gating_grad])
        token_grad = wide_grad + stream_grad
        upstream = token_grad.astype(BFLOAT)

    section_grads = lax.all_to_all(jnp.stack(mod_grads), "section", 0, 0, tiled=True)
    ada_part = lead_product(condition, section_grads.astype(BFLOAT))
    condition_grad = back_product(section_grads, ada_weight[0].astype(FLOAT))
    condition_grad = lax.psum(condition_grad, "section")
    embed_grad = jax.vjp(jax.nn.silu, embedded)[1](condition_grad)[0]
    marks = (steps[:, None] == jnp.arange(steps_count, dtype=jnp.int32)[None, :]).astype(FLOAT)
    table_part = lead_product(marks, embed_grad)

    def counted(route_pair):
        return jnp.sum(
            (
                route_pair.reshape(-1)[:, None]
                == jnp.arange(experts_total, dtype=jnp.int32)[None, :]
            ).astype(jnp.int32),
            0,
        )

    def total(parts, axes):
        return lax.psum(parts.astype(BFLOAT), axes).astype(FLOAT)

    both_attn = [jnp.stack([attn_grads[0][n], attn_grads[1][n]]) for n in range(4)]
    both_moe = [jnp.stack([moe_grads[0][n], moe_grads[1][n]]) for n in range(9)]
    counts = lax.psum(jnp.stack([counted(routes_one), counted(routes_two)]), ALL)
    attn_out = [total(item, ALL) for item in both_attn]
    moe_out = [total(item, ALL) for item in both_moe[:5]]
    expert_out = [total(item, ("section", "dp"))[:, None] for item in both_moe[5:]]
    table_out = total(table_part, ("dp", "expert"))
    ada_out = total(ada_part, ("dp", "expert"))[None]
    ada_bias_out = total(jnp.sum(section_grads, 0), ("dp", "expert"))[None]
    return (
        output,
        token_grad,
        table_out,
        ada_out,
        ada_bias_out,
        *attn_out,
        *moe_out,
        *expert_out,
        counts,
    )


def norm_parts(wide):
    row_mean = jnp.mean(wide, -1, keepdims=True)
    centred = wide - row_mean
    variance = jnp.mean(centred * centred, -1, keepdims=True)
    inverse = lax.rsqrt(variance + 1e-06)
    return centred * inverse, inverse


def norm_grad(unit, inverse, scaling, hidden_grad):
    shift_grad = jnp.sum(hidden_grad, 0, keepdims=True)
    scale_grad = jnp.sum(hidden_grad * unit, 0, keepdims=True)
    unit_grad = hidden_grad * (1.0 + scaling)
    stream_grad = inverse * (
        unit_grad
        - jnp.mean(unit_grad, -1, keepdims=True)
        - unit * jnp.mean(unit_grad * unit, -1, keepdims=True)
    )
    return stream_grad, shift_grad, scale_grad


def whole_spec(array):
    return pl.BlockSpec(array.shape, lambda *_: (0,) * array.ndim)


def layer_spec(array, layer):
    block = (None,) + array.shape[1:]
    return pl.BlockSpec(block, lambda *_: (layer,) + (0,) * (array.ndim - 1))


def kernel_call(body, ins, outs, flops, grid=(1,), scratch=(), prefetch=()):
    arrays = [item[0] for item in ins]
    specs = [item[1] if len(item) > 1 else whole_spec(item[0]) for item in ins]
    moved = sum(array.size * array.dtype.itemsize for array in arrays)
    return pl.pallas_call(
        body,
        out_shape=[
            (pltpu.HBM if far else jax.ShapeDtypeStruct)(shape, dtype) for shape, dtype, *far in outs
        ],
        grid_spec=pltpu.PrefetchScalarGridSpec(
            num_scalar_prefetch=len(prefetch),
            grid=grid,
            in_specs=specs,
            out_specs=[
                pl.BlockSpec(item[0], lambda *_, rank=len(item[0]): (0,) * rank) for item in outs
            ],
            scratch_shapes=list(scratch),
        ),
        cost_estimate=pl.CostEstimate(flops=flops, bytes_accessed=moved, transcendentals=0),
        compiler_params=pltpu.CompilerParams(vmem_limit_bytes=32 << 20),
    )(*prefetch, *arrays)


def mod_of(mods, block, part):
    row = 3 * block + part
    return mods[row : row + 1, :]


def head_pairs(width):
    for pair in range(HEADS // 2):
        start = pair * 2 * HD
        yield slice(start, start + 2 * HD), slice(width + start, width + start + 2 * HD), slice(
            2 * width + start, 2 * width + start + 2 * HD
        )


def masked(mask, rows):
    return jnp.where(mask, rows, jnp.zeros_like(rows))


def head_probs(query, key):
    scores = back_product(query, key) * HD ** (-0.5)
    raised = jnp.exp(scores - jnp.max(scores, -1, keepdims=True))
    return raised * (1.0 / jnp.sum(raised, -1, keepdims=True))


def gate_column(gates, expert):
    lanes = lax.broadcasted_iota(jnp.int32, gates.shape, 1)
    return jnp.sum(jnp.where(lanes == expert, gates, 0.0), -1, keepdims=True)


def gelu_value(pre):
    pre = pre.astype(BFLOAT)
    tanh = jnp.tanh(pre * (BFLOAT(0.7978845608028654) + BFLOAT(0.035677408136300125) * (pre * pre)))
    half = BFLOAT(0.5) * pre
    return half + half * tanh


def gelu_both(pre):
    pre = pre.astype(BFLOAT)
    square = pre * pre
    tanh = jnp.tanh(pre * (BFLOAT(0.7978845608028654) + BFLOAT(0.035677408136300125) * square))
    half = BFLOAT(0.5) * pre
    slope = (BFLOAT(0.5) + BFLOAT(0.5) * tanh) + (half * (BFLOAT(1.0) - tanh * tanh)) * (
        BFLOAT(0.7978845608028654) + BFLOAT(0.10703222440890037) * square
    )
    return half + half * tanh, slope


def far(x):
    return pltpu.with_memory_space_constraint(x, pltpu.HBM)


def gates_of(rows, routes, router):
    logits = product(rows, router)
    lanes = lax.broadcasted_iota(jnp.int32, logits.shape, 1)
    marks = (lanes == routes[:, 0:1]) | (lanes == routes[:, 1:2])
    top = jnp.max(jnp.where(marks, logits, -jnp.inf), -1, keepdims=True)
    raised = jnp.where(marks, jnp.exp(logits - top), 0.0)
    return raised / jnp.sum(raised, -1, keepdims=True)


def write_columns(out, start, table):
    rows = table.shape[0]
    turned = jnp.transpose(table)[:8]
    rounded = turned.astype(BFLOAT).astype(FLOAT)
    both = jnp.concatenate([rounded, turned - rounded]).astype(BFLOAT)
    out[start : start + 16, :] = jnp.zeros((16, out.shape[1]), BFLOAT)
    out[start : start + 16, :rows] = both


def read_columns(message, start, rows):
    both = message[start : start + 16, :rows].astype(FLOAT)
    turned = jnp.concatenate([both[:8] + both[8:], jnp.zeros((120, rows), FLOAT)])
    return jnp.transpose(turned)


def attention_forward_body(block, place, *refs):
    layer = block // 2
    refs = list(refs)
    pop = lambda count: [refs.pop(0) for _ in range(count)]
    if block:
        stream, own, back = pop(3)
    else:
        stream, cotangent = pop(2)
    mods, qkv_w, qv_b, out_w, out_b, router, routes = pop(7)
    if block:
        stream_out, before_out = pop(2)
        before = own[...] + back[...].astype(FLOAT)
        before_out[...] = before
        low_stream = (stream[...].astype(FLOAT) + mod_of(mods, block - 1, 2) * before).astype(BFLOAT)
        stream_out[...] = low_stream
        wide = low_stream.astype(FLOAT)
    else:
        wide = stream[...].astype(FLOAT)
    hidden_out, qkv_out, attended_out, branch_out, new_out, message_out, gates_out = pop(7)
    rows, width = wide.shape
    unit, _ = norm_parts(wide)
    hidden = (unit * (1.0 + mod_of(mods, block, 1)) + mod_of(mods, block, 0)).astype(BFLOAT)
    hidden_out[...] = hidden
    bias = qv_b[layer : layer + 1, :].astype(FLOAT)
    projected = product(hidden, qkv_w[...])
    qkv_out[:, :width] = (projected[:, :width] + bias[:, :width]).astype(BFLOAT)
    qkv_out[:, width : 2 * width] = projected[:, width : 2 * width].astype(BFLOAT)
    qkv_out[:, 2 * width :] = (projected[:, 2 * width :] + bias[:, width:]).astype(BFLOAT)
    low = lax.broadcasted_iota(jnp.int32, (rows, 2 * HD), 1) < HD
    for query_at, key_at, value_at in head_pairs(width):
        query, key, value = qkv_out[:, query_at], qkv_out[:, key_at], qkv_out[:, value_at]
        parts = [
            product(head_probs(masked(mask, query), key).astype(BFLOAT), value)
            for mask in (low, ~low)
        ]
        attended_out[:, query_at] = jnp.where(low, parts[0], parts[1]).astype(BFLOAT)
    branch = product(attended_out[...], out_w[...]) + out_b[layer : layer + 1, :].astype(FLOAT)
    branch_out[...] = branch
    new = (wide + mod_of(mods, block, 2) * branch).astype(BFLOAT)
    new_out[...] = new
    unit, _ = norm_parts(new.astype(FLOAT))
    following = (unit * (1.0 + mod_of(mods, block + 1, 1)) + mod_of(mods, block + 1, 0)).astype(
        BFLOAT
    )
    gates = gates_of(following, routes, router[...])
    gates_out[...] = gates
    message_out[:rows, :] = following
    write_columns(message_out, rows, gates)
    if not block:
        (last,) = pop(1)
        last[...] = (mod_of(mods, 3, 2) * cotangent[...].astype(FLOAT)).astype(BFLOAT)


def keep_or_send(place, core, kept, sent, piece, at, value):
    @pl.when(place[0] == core)
    def _():
        kept[piece, at, :] = value

    @pl.when(place[0] != core)
    def _():
        sent[piece, at, :] = value


def attention_backward_body(block, place, *refs):
    (
        upstream, after, after_message, own_grad, message, own_gates, gate_grads,
        stream, hidden, qkv, attended, branch, mods, router, qkv_w, out_w, *refs,
    ) = refs
    if block:
        before, grad_out, before_grad_out, kept, sent, small_out, proj = refs
    else:
        grad_out, kept, sent, small_out, proj = refs
    rows, width = stream.shape
    small_out[...] = jnp.zeros_like(small_out)

    gate_grad = gate_grads[...] + read_columns(message, rows, rows)
    gates = own_gates[...]
    logit_grad = gates * (gate_grad - jnp.sum(gates * gate_grad, -1, keepdims=True))
    logit_grad = logit_grad.astype(BFLOAT)
    router_grad = lead_product(logit_grad, after_message[:rows, :])[:4]
    hidden_grad = (
        own_grad[...] + message[:rows, :].astype(FLOAT) + back_product(logit_grad, router[...])
    )
    unit, inverse = norm_parts(after[...].astype(FLOAT))
    after_grad, shift_grad, scale_grad = norm_grad(
        unit, inverse, mod_of(mods, block + 1, 1), hidden_grad
    )
    small_out[0:1, :] = shift_grad
    small_out[1:2, :] = scale_grad
    wide_grad = (upstream[...].astype(FLOAT) + after_grad).astype(BFLOAT).astype(FLOAT)

    small_out[2:3, :] = jnp.sum(wide_grad * branch[...], 0, keepdims=True)
    branch_grad = (mod_of(mods, block, 2) * wide_grad).astype(BFLOAT)
    out_bias_grad = jnp.sum(branch_grad.astype(FLOAT), 0, keepdims=True)
    attended_grad = back_product(branch_grad, out_w[...]).astype(BFLOAT)
    low = lax.broadcasted_iota(jnp.int32, (rows, 2 * HD), 1) < HD
    factor = HD ** (-0.5)
    for query_at, key_at, value_at in head_pairs(width):
        query, key, value = qkv[:, query_at], qkv[:, key_at], qkv[:, value_at]
        pair_grad = attended_grad[:, query_at]
        sums = None
        for mask in (low, ~low):
            own_query, own_pair = masked(mask, query), masked(mask, pair_grad)
            probs = head_probs(own_query, key)
            value_grad = lead_product(probs.astype(BFLOAT), own_pair)
            prob_grad = back_product(own_pair, value)
            score_grad = (
                probs * (prob_grad - jnp.sum(prob_grad * probs, -1, keepdims=True))
            ).astype(BFLOAT)
            query_grad = masked(mask, product(score_grad, key))
            key_grad = lead_product(score_grad, own_query)
            parts = (query_grad, key_grad, value_grad)
            sums = parts if sums is None else tuple(a + b for a, b in zip(sums, parts))
        proj[:, query_at] = (sums[0] * factor).astype(BFLOAT)
        proj[:, key_at] = (sums[1] * factor).astype(BFLOAT)
        proj[:, value_at] = sums[2].astype(BFLOAT)

    middle = width // 2
    for part in range(4):
        if part < 3:
            grad = lead_product(hidden[...], proj[:, part * width : (part + 1) * width])
        else:
            grad = lead_product(attended[...], branch_grad)
        for side in range(2):
            keep_or_send(
                place,
                part // 2,
                kept,
                sent,
                2 * (part % 2) + side,
                slice(32, 32 + middle),
                grad[side * middle : (side + 1) * middle].astype(BFLOAT),
            )
    extra = jnp.concatenate(
        [
            jnp.sum(proj[:, :width].astype(FLOAT), 0, keepdims=True),
            jnp.sum(proj[:, 2 * width :].astype(FLOAT), 0, keepdims=True),
            out_bias_grad,
            router_grad,
            jnp.zeros((25, width), FLOAT),
        ]
    ).astype(BFLOAT)
    tail = slice(0, 32)
    for piece in range(4):
        for core in range(2):
            value = extra if piece == 0 and core == 0 else jnp.zeros((32, width), BFLOAT)
            keep_or_send(place, core, kept, sent, piece, tail, value)

    hidden_grad = back_product(proj[...], qkv_w[...])
    unit, inverse = norm_parts(stream[...].astype(FLOAT))
    stream_grad, shift_grad, scale_grad = norm_grad(
        unit, inverse, mod_of(mods, block, 1), hidden_grad
    )
    small_out[3:4, :] = shift_grad
    small_out[4:5, :] = scale_grad
    grad = wide_grad + stream_grad
    if block:
        low_grad = grad.astype(BFLOAT)
        grad_out[...] = low_grad
        wide_grad = low_grad.astype(FLOAT)
        before_grad_out[...] = (mod_of(mods, block - 1, 2) * wide_grad).astype(BFLOAT)
        small_out[5:6, :] = jnp.sum(wide_grad * before[...], 0, keepdims=True)
    else:
        grad_out[...] = grad


def shared_body(layer, forward, backward, place, *refs):
    refs = list(refs)
    pop = lambda count: [refs.pop(0) for _ in range(count)]
    (message,) = pop(1)
    branch_grad = pop(1)[0] if backward else None
    up, up_bias, down, down_bias = pop(4)
    total = pop(1)[0] if forward else None
    grads = pop(1)[0] if backward else None
    rows = message.shape[0] - 16
    pre = product(message[:rows, :], up[...]) + up_bias[layer : layer + 1, :].astype(FLOAT)
    if backward:
        act, slope = gelu_both(pre)
        act_grad = (back_product(branch_grad[...], down[...]) * slope).astype(BFLOAT)
        part = back_product(act_grad, up[...])

        @pl.when(pl.program_id(0) == 0)
        def _():
            grads[...] = part

        @pl.when(pl.program_id(0) > 0)
        def _():
            grads[...] += part

    else:
        act = gelu_value(pre)
    if forward:
        part = product(act.astype(BFLOAT), down[...])

        @pl.when(pl.program_id(0) == 0)
        def _():
            total[...] = part + down_bias[layer : layer + 1, :].astype(FLOAT)

        @pl.when(pl.program_id(0) > 0)
        def _():
            total[...] += part


def shared_call(layer, forward, backward, order, message, branch_grad, weights, hide=None):
    up, up_bias, down, down_bias = weights[:4]
    rows, width = message.shape[0] - 16, message.shape[1]
    units = 768 if forward and backward else 1536
    ins = [(message,)] + [(branch_grad,)] * backward
    ins += [
        (up, pl.BlockSpec((None, width, units), lambda i, _: (layer, 0, i))),
        (up_bias, pl.BlockSpec((2, units), lambda i, _: (0, i))),
        (down, pl.BlockSpec((None, units, width), lambda i, _: (layer, i, 0))),
        (down_bias,),
    ]
    return order.call(
        functools.partial(shared_body, layer, forward, backward),
        ins,
        [((rows, width), FLOAT)] * (forward + backward),
        5.0,
        hide=hide,
        grid=(up.shape[2] // units,),
    )


def experts_body(layer, forward, backward, partner, place, *refs):
    refs = list(refs)
    pop = lambda count: [refs.pop(0) for _ in range(count)]
    (message,) = pop(1)
    own_gates = None if partner else pop(1)[0]
    branch_grad = pop(1)[0] if backward else None
    e_up, e_upb, e_down, e_downb, own_up, got_up, own_down, got_down, x_upb, x_downb = pop(10)
    kept = pop(1)[0] if backward and not forward else None
    shared_out = pop(1)[0] if forward and not partner else None
    shared_grad = pop(1)[0] if backward and not partner else None
    if forward:
        total_out = pop(1)[0]
        kept_out = None if backward else pop(1)[0]
    if backward:
        grad_out = pop(1)[0]
        gate_grad_out = None if partner else pop(1)[0]
    x_up, x_down, total, sems = pop(4)
    if partner:
        (gates,) = pop(1)
    else:
        gates = own_gates
    if backward:
        grads, gate_grad = pop(2)
    step = pl.program_id(0)
    rows = message.shape[0] - 16
    lanes = lax.broadcasted_iota(jnp.int32, (rows, 128), 1)

    def copies():
        pairs = (
            (own_up, x_up.at[place[0]]),
            (own_down, x_down.at[place[0]]),
            (got_up, x_up.at[1 - place[0]]),
            (got_down, x_down.at[1 - place[0]]),
        )
        return [
            pltpu.make_async_copy(source, target, sems.at[number])
            for number, (source, target) in enumerate(pairs)
        ]

    @pl.when(step == 0)
    def _():
        if partner:
            gates[...] = read_columns(message, rows, rows)
        for copy in copies():
            copy.start()

    def expert(index, number, up, up_bias, down, down_bias):
        gate = gate_column(gates[...], number)
        pre = product(message[:rows, :], up) + up_bias
        if backward:
            act, slope = gelu_both(pre)
            act_grad = (back_product(branch_grad[...], down) * slope * gate).astype(BFLOAT)
            part_grad = back_product(act_grad, up)
        else:
            act = gelu_value(pre)
        if forward:
            result = (product(act.astype(BFLOAT), down) + down_bias).astype(BFLOAT)
            if kept_out is not None:
                kept_out[index] = result
            result = result.astype(FLOAT)
            part = gate * result
        else:
            result = kept[index].astype(FLOAT)
        if backward:
            column = jnp.sum(branch_grad[...].astype(FLOAT) * result, -1, keepdims=True)
            part_gate = jnp.where(lanes == number, column, 0.0)
        if index == 0:
            if forward:
                total[...] = part
            if backward:
                grads[...] = part_grad
                gate_grad[...] = part_gate
            return
        if forward:
            part = part + total[...]
            if not partner:
                part = part + shared_out[...]
            total_out[...] = part.astype(total_out.dtype)
        if backward:
            part_grad = part_grad + grads[...]
            part_gate = part_gate + gate_grad[...]
            if partner:
                grad_out[:rows, :] = part_grad.astype(BFLOAT)
                write_columns(grad_out, rows, part_gate)
            else:
                grad_out[...] = part_grad + shared_grad[...]
                gate_grad_out[...] = part_gate

    @pl.when(step == 0)
    def _():
        expert(
            0, place[3], e_up[...], e_upb[layer].astype(FLOAT), e_down[...],
            e_downb[layer].astype(FLOAT),
        )

    @pl.when(step == 1)
    def _():
        for copy in copies():
            copy.wait()
        width, units = e_up.shape
        expert(
            1, place[3] ^ 2, x_up[...].reshape(width, units), x_upb[...].astype(FLOAT),
            x_down[...].reshape(units, width),
            x_downb[...].astype(FLOAT),
        )


def experts_call(
    layer,
    forward,
    backward,
    order,
    message,
    gates,
    branch_grad,
    weights,
    extra,
    kept,
    shared,
    hide=None,
):
    e_up, e_upb, e_down, e_downb = weights[4:]
    rows, width = message.shape[0] - 16, message.shape[1]
    units = e_up.shape[3]
    partner = gates is None
    ins = [(message,)]
    if not partner:
        ins += [(gates,)]
    if backward:
        ins += [(branch_grad,)]
    ins += [
        (e_up, pl.BlockSpec((None, None, width, units), lambda i, _: (layer, 0, 0, 0))),
        (e_upb,),
        (e_down, pl.BlockSpec((None, None, units, width), lambda i, _: (layer, 0, 0, 0))),
        (e_downb,),
    ]
    ins += [(item, pl.BlockSpec(memory_space=pltpu.HBM)) for item in extra[:4]]
    ins += [(item,) for item in extra[4:]]
    if backward and not forward:
        ins += [(far(kept),)]
    if not partner:
        ins += [(item,) for item in shared]
    outs = []
    scratch = [
        pltpu.VMEM((2,) + extra[0].shape, BFLOAT),
        pltpu.VMEM((2,) + extra[2].shape, BFLOAT),
        pltpu.VMEM((rows, width), FLOAT),
        pltpu.SemaphoreType.DMA((4,)),
    ]
    if partner:
        scratch += [pltpu.VMEM((rows, 128), FLOAT)]
    if forward:
        outs += [((rows, width), BFLOAT if partner else FLOAT)]
        if not backward:
            outs += [((2, rows, width), BFLOAT, True)]
    if backward:
        outs += [((rows + 16, width), BFLOAT)] if partner else [((rows, width), FLOAT)]
        if not partner:
            outs += [((rows, 128), FLOAT)]
        scratch += [pltpu.VMEM((rows, width), FLOAT), pltpu.VMEM((rows, 128), FLOAT)]
    return order.call(
        functools.partial(experts_body, layer, forward, backward, partner),
        ins,
        outs,
        6.0,
        hide=hide,
        grid=(2,),
        scratch=scratch,
    )


def weight_grads_body(layer, expert, shared, place, *refs):
    messages, branch_grads, refs = refs[0:4], refs[4:8], list(refs[8:])
    pop = lambda count: [refs.pop(0) for _ in range(count)]
    if expert:
        e_up, e_upb, e_down = pop(3)
    if shared:
        s_up, s_upb, s_down = pop(3)
    kept, sent, rows_all, grads_all, acts, pre_grads, sums_all = pop(7)
    step = pl.program_id(0)
    rows, width = 256, rows_all.shape[1]
    units = acts.shape[1]
    middle = width // 2
    unroll = True

    def fill_rows(gated):
        for side in range(4):
            at = slice(side * rows, (side + 1) * rows)
            grad = branch_grads[side][:rows, :]
            rows_all[at, :] = messages[side][:rows, :]
            if gated:
                gate = gate_column(read_columns(messages[side], rows, rows), place[3])
                grad = (gate * grad.astype(FLOAT)).astype(BFLOAT)
            grads_all[at, :] = grad
            bias = jnp.sum(grad.astype(FLOAT), 0, keepdims=True)
            if gated:
                sums_all[4:5, :] += bias
            else:
                sums_all[15:16, :] += jnp.where(place[3] == 0, bias, 0.0)

    def chunk(up, offset, down):
        def tile(side, sums):
            at = pl.ds(pl.multiple_of(side * rows, rows), rows)
            act, slope = gelu_both(product(rows_all[at, :], up[...]) + offset)
            acts[at, :] = act.astype(BFLOAT)
            grad = (back_product(grads_all[at, :], down[...]) * slope).astype(BFLOAT)
            pre_grads[at, :] = grad
            return sums + jnp.sum(grad.astype(FLOAT), 0, keepdims=True)

        return lax.fori_loop(0, 4, tile, jnp.zeros((1, units), FLOAT), unroll=unroll)

    def weight_pair(half):
        at = slice(half * width, (half + 1) * width)
        up_grad = lead_product(rows_all[...], pre_grads[:, at]).astype(BFLOAT)
        down_grad = lead_product(acts[:, at], grads_all[...]).astype(BFLOAT)
        return (0, up_grad), (1, down_grad)

    def tails(start):
        at = slice(start, start + 32)
        value = sums_all[...].astype(BFLOAT)
        for piece in range(4):
            for core in range(2):
                rest = jnp.zeros((32, width), BFLOAT)
                own = value if piece == 0 and core == 0 else rest
                keep_or_send(place, core, kept, sent, piece, at, own)

    if expert:
        for part in range(2):

            @pl.when(step == part)
            def _(part=part):
                if part == 0:
                    sums_all[...] = jnp.zeros_like(sums_all)
                    fill_rows(True)
                sums = chunk(e_up, e_upb[layer].astype(FLOAT), e_down)
                for half in range(2):
                    number = 2 * part + half
                    sums_all[number : number + 1, :] = sums[:, half * width : (half + 1) * width]
                    for core, grad in weight_pair(half):
                        keep_or_send(place, core, kept, sent, number, slice(0, width), grad)
                if part == 1:
                    tails(width)

    if shared:

        @pl.when(step == 2 * expert)
        def _():
            sums_all[...] = jnp.zeros_like(sums_all)
            fill_rows(False)
            sums = chunk(s_up, s_upb[layer : layer + 1, :].astype(FLOAT), s_down)
            start = (width + 32) * expert
            where = slice(start, start + middle)
            for half in range(2):
                part_sums = sums[:, half * width : (half + 1) * width]
                for plane in range(4):
                    row = 7 + 2 * plane + half
                    sums_all[row : row + 1, :] = jnp.where(place[3] == plane, part_sums, 0.0)
                for core, grad in weight_pair(half):
                    for side in range(2):
                        value = grad[side * middle : (side + 1) * middle]
                        keep_or_send(place, core, kept, sent, 2 * half + side, where, value)
            tails(start + middle)


def weight_grads_call(layer, expert, shared, order, messages, branch_grads, weights, hide=None):
    s_up, s_upb, s_down, _, e_up, e_upb, e_down, _ = weights
    rows, width, units = 256, s_up.shape[1], 768
    at_own = lambda i: jnp.minimum(i, 1)
    ins = [(far(item[0]), *item[1:]) for item in (*messages, *branch_grads)]
    if expert:
        ins += [
            (e_up, pl.BlockSpec((None, None, width, units), lambda i, _: (layer, 0, 0, at_own(i)))),
            (e_upb, pl.BlockSpec((2, 1, units), lambda i, _: (0, 0, at_own(i)))),
            (
                e_down,
                pl.BlockSpec((None, None, units, width), lambda i, _: (layer, 0, at_own(i), 0)),
            ),
        ]
    if shared:
        ins += [
            (s_up, pl.BlockSpec((None, width, units), lambda i, at: (layer, 0, at[3]))),
            (s_upb, pl.BlockSpec((2, units), lambda i, at: (0, at[3]))),
            (s_down, pl.BlockSpec((None, units, width), lambda i, at: (layer, at[3], 0))),
        ]
    piece = (width + 32) * expert + (width // 2 + 32) * shared
    return order.call(
        functools.partial(weight_grads_body, layer, expert, shared),
        ins,
        [((4, piece, width), BFLOAT, True)] * 2,
        7.0 * (2 * expert + shared),
        hide=hide,
        grid=(2 * expert + shared,),
        scratch=[
            pltpu.VMEM((4 * rows, width), BFLOAT),
            pltpu.VMEM((4 * rows, width), BFLOAT),
            pltpu.VMEM((4 * rows, units), BFLOAT),
            pltpu.VMEM((4 * rows, units), BFLOAT),
            pltpu.VMEM((32, width), FLOAT),
        ],
    )


def swap(x, axis, by):
    return lax.ppermute(x, axis, [(i, i ^ by) for i in range(lax.axis_size(axis))])


def bits():
    section = lax.axis_index("section")
    return lax.axis_index("dp"), section // 2, section % 2


def ordered(bit, mine, other):
    return jnp.stack([jnp.where(bit == 0, mine, other), jnp.where(bit == 0, other, mine)])


def wide_sum(*parts):
    total = parts[0].astype(FLOAT)
    for part in parts[1:]:
        total = total + part.astype(FLOAT)
    return total


class Groups:
    def __init__(self, expert, shared, every):
        self.expert, self.shared, self.every = expert, shared, every
        self.rows = expert + shared + every
        self.half = self.rows // 2
        self.sent = expert // 2 + 2 * shared + every // 2


def first_body(parts, has_misc, place, *refs):
    keeps, gots, refs = refs[:parts], refs[parts : 2 * parts], refs[2 * parts :]
    if has_misc:
        misc, got_misc, *refs = refs
    keep_a, send_a, keep_b, send_b, pieces = refs
    half = keep_a.shape[1]
    y, x = place[1], place[2]
    for piece in range(4):
        at = 0
        for keep, got in zip(keeps[:-1], gots[:-1]):
            rows = keep.shape[1]
            total = wide_sum(keep[piece], got[piece])
            pieces[piece, at : at + rows, :] = total.astype(BFLOAT)
            at += rows
        joint = at - 32
        first = total[rows - 32 :]
        second = wide_sum(keeps[-1][piece], gots[-1][piece])
        small = first + second[:32]
        if has_misc and piece in (1, 2):
            at = slice(32 * (piece - 1), 32 * piece)
            small = small + jnp.where(place[0] == 0, misc[at, :] + got_misc[at, :], 0.0)
        pieces[piece, joint : joint + 32, :] = small.astype(BFLOAT)
        pieces[piece, joint + 32 :, :] = second[32:].astype(BFLOAT)
    for other in range(2):
        keep_a[other] = pieces[2 * other + x, :half, :]
        send_a[other] = pieces[2 * other + 1 - x, :half, :]
        keep_b[other] = pieces[2 * y + other, half:, :]
        send_b[other] = pieces[2 * (1 - y) + other, half:, :]


def second_body(place, keep_a, got_a, keep_b, got_b, *outs):
    next_a, sent_a, next_b, sent_b = outs
    y, x = place[1], place[2]
    next_a[...] = wide_sum(keep_a[y], got_a[y]).astype(BFLOAT)
    sent_a[...] = wide_sum(keep_a[1 - y], got_a[1 - y]).astype(BFLOAT)
    next_b[...] = wide_sum(keep_b[x], got_b[x]).astype(BFLOAT)
    sent_b[...] = wide_sum(keep_b[1 - x], got_b[1 - x]).astype(BFLOAT)


def third_body(groups, place, keep_a, got_a, keep_b, got_b, *refs):
    *outs, piece = refs
    piece[: groups.half, :] = wide_sum(keep_a[...], got_a[...]).astype(BFLOAT)
    piece[groups.half :, :] = wide_sum(keep_b[...], got_b[...]).astype(BFLOAT)
    middle = groups.expert // 2
    if groups.expert:
        outs[0][...] = piece[:middle, :]
        outs[1][...] = piece[middle : 2 * middle, :]
    if groups.shared:
        outs[-1][...] = piece[2 * middle :, :]


def column_body(groups, joined, place, *refs):
    experts = (refs[0], refs[1]) if joined else None
    columns, sent = refs[2 * joined : 2 * joined + 4], refs[2 * joined + 4 :]
    z = place[3]
    shared, every = groups.shared // 2, groups.every // 2
    for side in range(2):
        out = sent[side]
        at = 0
        if joined:
            at = groups.expert // 2
            out[:at, :] = experts[side][...]
        for turn in range(4):
            to = pl.multiple_of(at + (z ^ turn) * shared, 16)
            out[pl.ds(to, shared), :] = columns[turn][side * shared : (side + 1) * shared, :]
        at += 4 * shared
        rows = slice(groups.shared + side * every, groups.shared + (side + 1) * every)
        first = wide_sum(columns[0][rows, :], columns[1][rows, :])
        second = wide_sum(columns[2][rows, :], columns[3][rows, :])
        out[at:, :] = (first + second).astype(BFLOAT)


def pair_body(place, own_a, got_a, own_b, got_b, out_a, out_b):
    y, x = place[1], place[2]
    out_a[y] = own_a[...]
    out_a[1 - y] = got_a[...]
    out_b[x] = own_b[...]
    out_b[1 - x] = got_b[...]


COST = 1.1e9


class Order:
    def __init__(self, place):
        self.place = place

    def call(self, body, ins, outs, micros, hide=None, **kwargs):
        outs = kernel_call(body, ins, outs, int(micros * COST), prefetch=(self.place,), **kwargs)
        if hide is None:
            self.place = lax.optimization_barrier((self.place, outs[-1]))[0]
            return outs
        self.place, outs, hide = lax.optimization_barrier((self.place, outs, hide))
        return outs, hide

    def arrive(self, xs):
        self.place, xs = lax.optimization_barrier((self.place, xs))
        return xs

    def tie(self, x):
        return lax.optimization_barrier((x, self.place))[0]

    def wait(self, x):
        self.place = lax.optimization_barrier((self.place, x))[0]


class Flow:
    def __init__(self, groups, order, slow):
        self.groups, self.order, self.parts = groups, order, []
        self.far = (True,) * slow

    def add(self, kept, sent):
        self.width = kept.shape[2]
        self.parts.append([kept, swap(sent, "dp", 1)])

    def across(self, turn, first, second):
        self.got = (
            swap(first, "section", 1 + turn),
            swap(second, "section", 2 - turn),
        )

    def first(self, misc=()):
        groups, width = self.groups, self.width
        ins = [kept for kept, _ in self.parts] + [got for _, got in self.parts] + list(misc)
        self.keep_a, send_a, self.keep_b, send_b = self.order.call(
            functools.partial(first_body, len(self.parts), bool(misc)),
            [(item,) for item in ins],
            [((2, groups.half, width), BFLOAT, *self.far), ((2, groups.half, width), BFLOAT)] * 2,
            4.0,
            scratch=[pltpu.VMEM((4, groups.rows, width), BFLOAT)],
        )
        self.across(0, send_a, send_b)

    def second(self):
        self.keep_a, send_a, self.keep_b, send_b = self.order.call(
            second_body,
            [(far(item),) for item in (self.keep_a, self.got[0], self.keep_b, self.got[1])],
            [
                ((self.groups.half, self.width), BFLOAT, *self.far),
                ((self.groups.half, self.width), BFLOAT),
            ]
            * 2,
            1.5,
        )
        self.across(1, send_a, send_b)

    def third(self):
        groups, width = self.groups, self.width
        outs = []
        if groups.expert:
            outs += [((groups.expert // 2, width), BFLOAT)] * 2
        if groups.shared:
            outs += [((groups.shared + groups.every, width), BFLOAT)]
        outs = self.order.call(
            functools.partial(third_body, groups),
            [(self.keep_a,), (self.got[0],), (self.keep_b,), (self.got[1],)],
            outs,
            1.5,
            scratch=[pltpu.VMEM((groups.rows, width), BFLOAT)],
        )
        self.expert = list(outs[:2]) if groups.expert else []
        if groups.shared:
            columns = outs[-1]
            self.columns = [columns, swap(columns, "expert", 1), swap(columns, "expert", 2)]

    def relay(self):
        self.columns.append(swap(self.order.tie(self.columns[2]), "expert", 1))

    def column(self, joined):
        ins = self.expert * joined + self.columns
        rows = self.groups.sent - self.groups.expert // 2 * (not joined)
        return Spread(
            self.order,
            self.order.call(
                functools.partial(column_body, self.groups, joined),
                [(far(item),) for item in ins],
                [((rows, self.width), BFLOAT)] * 2,
                1.5,
            ),
        )


class Spread:
    def __init__(self, order, own):
        self.order, self.own = order, own
        self.got = [swap(own[0], "section", 2), swap(own[1], "section", 1)]

    def pair(self):
        self.own = self.order.call(
            pair_body,
            [(self.own[0],), (self.got[0],), (self.own[1],), (self.got[1],)],
            [((2,) + item.shape, BFLOAT) for item in self.own],
            1.7,
        )
        self.got = [swap(self.own[0], "section", 1), swap(self.own[1], "section", 2)]
        self.other_own = [swap(item, "dp", 1) for item in self.own]

    def finish(self):
        for item in self.other_own:
            self.order.wait(item)
        other_got = [swap(item, "dp", 1) for item in self.got]
        own, got, other_own = self.own, self.got, self.other_own
        self.all = [own[0], got[0], own[1], got[1]]
        self.all += [other_own[0], other_got[0], other_own[1], other_got[1]]


def table_rows(steps, rows):
    count, width = steps.shape[1], rows.shape[1]
    lanes = lax.broadcasted_iota(jnp.int32, (1000, count), 1)
    places = lax.broadcasted_iota(jnp.int32, (1000, count), 0)
    marks = jnp.where((places == steps) & (lanes < 32), 1.0, 0.0).astype(BFLOAT)
    wide = jnp.concatenate([rows, jnp.zeros((count - 32, width), FLOAT)]).astype(BFLOAT)
    return product(marks, wide)


def final_body(groups, last, place, *refs):
    parts, refs = refs[:8], refs[8:]
    if last:
        small_one, bias_one, *refs = refs
        refs = refs[6:]
    up, down, bias, s_up, s_down, qkv, out_w, small, *refs = refs
    *refs, data = refs
    step = pl.program_id(0)
    core, y, x = place[0], place[1], place[2]

    @pl.when(step == 0)
    def _():
        for chip in range(2):
            own_a, got_a, own_b, got_b = parts[4 * chip : 4 * chip + 4]
            owner = 1 - core if chip else core
            for other in range(2):
                data[owner, 2 * other + x, 0] = own_a[other]
                data[owner, 2 * other + 1 - x, 0] = got_a[other]
                data[owner, 2 * y + other, 1] = own_b[other]
                data[owner, 2 * (1 - y) + other, 1] = got_b[other]

    rows = groups.expert // 2
    for part in range(4):

        @pl.when(step == 2 * part)
        def _(part=part):
            for out, owner in ((up, 0), (down, 1)):
                both = data[owner, part, :, :rows, :].reshape(groups.expert, -1)
                out[...] = both[: groups.expert - 32].astype(FLOAT)
                if owner == 0 and part == 0:
                    bias[...] = both[groups.expert - 32 :].astype(FLOAT)

    half = groups.shared // 2
    for number in range(8):

        @pl.when(step == number)
        def _(number=number):
            at, block = rows + number // 2 * half, number % 2
            for out, owner in ((s_up, 0), (s_down, 1)):
                both = data[owner, 2 * block : 2 * block + 2, :, at : at + half, :]
                out[...] = both.reshape(4 * half, -1).astype(FLOAT)

    every = groups.every // 2
    real = groups.every - 32
    start = rows + 4 * half
    for part in range(4):

        @pl.when(step == 2 * part)
        def _(part=part):
            target = qkv if part < 3 else out_w
            for piece in range(2):
                number = 2 * (part % 2) + piece
                both = data[part // 2, number, :, start : start + every, :]
                both = both.reshape(groups.every, -1)
                target[real * piece : real * (piece + 1), :] = both[32:].astype(FLOAT)
                if part < 2:
                    small[number] = both[:32].astype(FLOAT)

    if last:

        @pl.when(step == 7)
        def _():
            qv_b, out_b, router, s_upb, s_downb, e_upb, e_downb, table, counts = refs
            width = data.shape[4]
            for layer, rest, biases in ((0, small, bias), (1, small_one, bias_one)):
                at = slice(layer, layer + 1)
                for row in range(2):
                    qv_b[at, row * width : (row + 1) * width] = rest[0, row : row + 1, :]
                out_b[at, :] = rest[0, 2:3, :]
                turned = jnp.transpose(
                    jnp.concatenate([rest[0, 3:7, :], jnp.zeros((124, width), FLOAT)])
                )
                router[layer] = turned[:, :4]
                for row in range(8):
                    s_upb[at, row * width : (row + 1) * width] = rest[0, 7 + row : 8 + row, :]
                s_downb[at, :] = rest[0, 15:16, :]
                for row in range(4):
                    e_upb[layer, :, row * width : (row + 1) * width] = biases[row : row + 1, :]
                e_downb[layer] = biases[4:5, :]
            steps = 32.0 * small[2, 0:1, :128] + small[2, 1:2, :128]
            table[...] = table_rows(steps.astype(jnp.int32), small[1])
            spots = lax.broadcasted_iota(jnp.int32, (256, 128), 0) % 8
            lanes = lax.broadcasted_iota(jnp.int32, (256, 128), 1)
            marks = jnp.where(spots == lanes, 1.0, 0.0).astype(BFLOAT)
            numbers = small[2, 0:8, :256].astype(BFLOAT)
            counts[...] = product(numbers, marks)[2:3, :].astype(jnp.int32)


def final_call(groups, layer, order, parts, before, hide=()):
    width = parts[0].shape[2]
    outs = [
        (2, 1, width, 4 * width),
        (2, 1, 4 * width, width),
        (32, width),
        (2, width, 8 * width),
        (2, 8 * width, width),
        (2, width, 3 * width),
        (2, width, width),
        (4, 32, width),
    ]
    specs = [
        pl.BlockSpec((None, None, width, width), lambda i, _: (layer, 0, 0, i // 2)),
        pl.BlockSpec((None, None, width, width), lambda i, _: (layer, 0, i // 2, 0)),
        pl.BlockSpec((32, width), lambda i, _: (0, 0)),
        pl.BlockSpec((None, width, width), lambda i, _: (layer, 0, i)),
        pl.BlockSpec((None, width, width), lambda i, _: (layer, i, 0)),
        pl.BlockSpec((None, width, width), lambda i, _: (layer, 0, jnp.minimum(i // 2, 2))),
        pl.BlockSpec((None, width, width), lambda i, _: (layer, 0, 0)),
        pl.BlockSpec((4, 32, width), lambda i, _: (0, 0, 0)),
    ]
    ins = list(parts)
    in_specs = [
        pl.BlockSpec(item.shape, lambda *_: (0, 0, 0), pipeline_mode=pl.Buffered(1))
        for item in parts
    ]
    aliases = {}
    shapes = [jax.ShapeDtypeStruct(shape, FLOAT) for shape in outs]
    if before is not None:
        ins += [before[7], before[2]]
        in_specs += [whole_spec(before[7]), whole_spec(before[2])]
        for number in (0, 1, 3, 4, 5, 6):
            aliases[1 + len(ins)] = number
            ins.append(before[number])
            in_specs.append(pl.BlockSpec(memory_space=pl.ANY))
        rest = [
            (2, 2 * width),
            (2, width),
            (2, width, 4),
            (2, 8 * width),
            (2, width),
            (2, 1, 4 * width),
            (2, 1, width),
            (1000, width),
        ]
        shapes += [jax.ShapeDtypeStruct(shape, FLOAT) for shape in rest]
        shapes += [jax.ShapeDtypeStruct((1, 128), jnp.int32)]
        specs += [
            pl.BlockSpec(item.shape, lambda *_, rank=len(item.shape): (0,) * rank)
            for item in shapes[8:]
        ]
    outs = pl.pallas_call(
        functools.partial(final_body, groups, before is not None),
        out_shape=shapes,
        grid_spec=pltpu.PrefetchScalarGridSpec(
            num_scalar_prefetch=1,
            grid=(8,),
            in_specs=in_specs,
            out_specs=specs,
            scratch_shapes=[pltpu.VMEM((2, 4, 2, parts[0].shape[1], width), BFLOAT)],
        ),
        input_output_aliases=aliases,
        cost_estimate=pl.CostEstimate(flops=int(8e9), bytes_accessed=16 << 20, transcendentals=0),
        compiler_params=pltpu.CompilerParams(vmem_limit_bytes=50 << 20),
    )(order.place, *ins)
    outs, hide = order.arrive((outs, hide))
    return outs, hide


def extra_plane_body(place, own_a, got_a, own_b, got_b, out_a, out_b):
    y, x = place[1], place[2]
    for other in range(2):
        out_a[2 * other + x] = own_a[other]
        out_a[2 * other + 1 - x] = got_a[other]
        out_b[2 * y + other] = own_b[other]
        out_b[2 * (1 - y) + other] = got_b[other]


class ExtraExpert:
    def __init__(self, layer, order, number, up, down):
        width, units = up.shape[2], up.shape[3]
        some_up = lax.dynamic_slice(
            up, (layer, 0, number * (width // 8), 0), (1, 1, width // 8, units)
        ).reshape(width // 8, units)
        some_down = lax.dynamic_slice(
            down, (layer, 0, number * (units // 8), 0), (1, 1, units // 8, width)
        ).reshape(units // 8, width)
        self.order = order
        self.shapes = [some_up.shape, some_down.shape]
        self.own = [swap(some_up, "expert", 2), swap(some_down, "expert", 2)]

    def across(self, after):
        self.own = [lax.optimization_barrier((item, after))[0] for item in self.own]
        self.got = [swap(self.own[0], "section", 2), swap(self.own[1], "section", 1)]

    def pair(self):
        self.own = self.order.call(
            pair_body,
            [(self.own[0],), (self.got[0],), (self.own[1],), (self.got[1],)],
            [((2,) + shape, BFLOAT) for shape in self.shapes],
            1.7,
        )
        self.got = [swap(self.own[0], "section", 1), swap(self.own[1], "section", 2)]

    def plane(self):
        up, down = self.order.call(
            extra_plane_body,
            [(self.own[0],), (self.got[0],), (self.own[1],), (self.got[1],)],
            [((4,) + shape, BFLOAT) for shape in self.shapes],
            1.7,
        )
        self.all = [up, swap(up, "dp", 1), down, swap(down, "dp", 1)]


def shards_fast(
    tokens,
    timesteps,
    routes_one,
    routes_two,
    cotangent,
    time_table,
    ada_weight,
    ada_bias,
    qkv_weight,
    qv_bias,
    out_weight,
    out_bias,
    router_weight,
    shared_up,
    shared_up_bias,
    shared_down,
    shared_down_bias,
    expert_up,
    expert_up_bias,
    expert_down,
    expert_down_bias,
):
    width = tokens.shape[1]
    rows = tokens.shape[0]
    bf, fl = BFLOAT, FLOAT
    experts_total = router_weight.shape[2]
    core, y, x_bit = bits()
    place = jnp.stack([core, y, x_bit, lax.axis_index("expert")]).astype(jnp.int32)
    routers = jnp.pad(router_weight, ((0, 0), (0, 0), (0, 128 - experts_total)))

    order = Order(place)
    number = core * 4 + y * 2 + x_bit
    hidden_units = expert_up.shape[3]
    first_extra = ExtraExpert(0, order, number, expert_up, expert_down)
    half_steps = ordered(x_bit, timesteps[0], swap(timesteps[0], "section", 1))
    number = lax.optimization_barrier((number, half_steps))[0]
    second_extra = ExtraExpert(1, order, number, expert_up, expert_down)
    steps = ordered(y, half_steps, swap(half_steps, "section", 2)).reshape(4)
    embedded = jnp.take(time_table, steps, axis=0)
    condition = jax.nn.silu(embedded.astype(FLOAT)).astype(BFLOAT)
    section_mod = product(condition, ada_weight[0]) + ada_bias[0].astype(FLOAT)
    mods = lax.all_to_all(section_mod, "section", 0, 0, tiled=True).reshape(12, width)
    first_extra.across(section_mod)
    first_extra.pair()
    own_bias = jnp.concatenate([expert_up_bias[:, 0], expert_down_bias[:, 0]], -1)
    own_bias = lax.optimization_barrier((own_bias, section_mod))[0]
    extra_bias = swap(own_bias, "expert", 2)

    def with_bias(layer, extra):
        bias = extra_bias[layer : layer + 1]
        return [*(far(item) for item in extra.all), bias[:, :hidden_units], bias[:, hidden_units:]]

    weights = (
        far(shared_up),
        shared_up_bias,
        far(shared_down),
        shared_down_bias,
        far(expert_up),
        expert_up_bias,
        far(expert_down),
        expert_down_bias,
    )

    size = rows + 16
    block_outs = [
        ((rows, width), bf, True),
        ((rows, 3 * width), bf, True),
        ((rows, width), bf, True),
        ((rows, width), fl, True),
        ((rows, width), bf, True),
        ((size, width), bf),
        ((rows, 128), fl, True),
    ]

    def attn_ins(layer, routes):
        return [
            (mods,),
            (qkv_weight, layer_spec(qkv_weight, layer)),
            (qv_bias,),
            (out_weight, layer_spec(out_weight, layer)),
            (out_bias,),
            (routers, layer_spec(routers, layer)),
            (routes,),
        ]

    def z(x, by):
        return swap(order.tie(x), "expert", by)

    (hidden0, qkv0, attended0, branch0, stream1, message1, gates1, last_grad), (first_extra.got,) = (
        order.call(
            functools.partial(attention_forward_body, 0),
            [(tokens,), (cotangent,), *attn_ins(0, routes_one)],
            block_outs + [((rows, width), bf)],
            4.2,
            hide=[first_extra.got],
        )
    )
    got1 = swap(message1, "expert", 1)
    first_extra.plane()
    (shared1,), (got1, first_extra.all) = shared_call(
        0, True, False, order, message1, None, weights, hide=[got1, first_extra.all]
    )
    extra0 = with_bias(0, first_extra)
    sent1, kept_got1 = experts_call(
        0, True, False, order, got1, None, None, weights, extra0, None, ()
    )
    back1 = swap(sent1, "expert", 1)
    second_extra.across(sent1)
    (own1, kept_own1), (back1,) = experts_call(
        0, True, False, order, message1, gates1, None, weights, extra0, None, (shared1,),
        hide=[back1],
    )
    got_last = z(last_grad, 1)
    second_extra.pair()
    (stream2, branch1, hidden2, qkv2, attended2, branch2, stream3, message3, gates3), (got_last,) = (
        order.call(
            functools.partial(attention_forward_body, 2),
            [(stream1,), (own1,), (back1,), *attn_ins(1, routes_two)],
            [((rows, width), bf, True), ((rows, width), fl, True)] + block_outs,
            4.2,
            hide=[got_last],
        )
    )
    got3 = swap(message3, "expert", 1)
    second_extra.plane()
    (shared3, shared_grad3), (got3, second_extra.all) = shared_call(
        1, True, True, order, message3, last_grad, weights, hide=[got3, second_extra.all]
    )
    far_last = z(last_grad, 2)
    extra1 = with_bias(1, second_extra)
    (sent3, back_message3), (far_last,) = experts_call(
        1, True, True, order, got3, None, got_last, weights, extra1, None, (), hide=[far_last]
    )
    back_grad3 = swap(back_message3, "expert", 1)
    far3 = z(message3, 2)
    (own3, own_grad3, gate_grad3), (back_grad3, far3) = experts_call(
        1, True, True, order, message3, gates3, last_grad, weights, extra1, None,
        (shared3, shared_grad3), hide=[back_grad3, far3],
    )
    farther_last, farther3 = z(far_last, 1), z(far3, 1)
    grad_outs = [((4, width // 2 + 32, width), bf, True)] * 2 + [((16, width), fl)]
    proj = [pltpu.VMEM((rows, 3 * width), bf)]

    def attn_back_ins(layer):
        return [
            (mods,),
            (routers, layer_spec(routers, layer)),
            (qkv_weight, layer_spec(qkv_weight, layer)),
            (out_weight, layer_spec(out_weight, layer)),
        ]

    groups = Groups(width + 32, width // 2, width // 2 + 32)
    flow1, flow0 = Flow(groups, order, True), Flow(groups, order, True)
    (grad1, branch_grad1, kept_a, sent_a, small1), (farther_last, farther3) = order.call(
        functools.partial(attention_backward_body, 2),
        [
            (item,)
            for item in (
                cotangent, stream3, message3, own_grad3, back_grad3, gates3, gate_grad3,
                stream2, hidden2, qkv2, attended2, branch2,
            )
        ]
        + attn_back_ins(1)
        + [(branch1,)],
        [((rows, width), bf), ((rows, width), bf)] + grad_outs,
        7.7,
        hide=[farther_last, farther3],
        scratch=proj,
    )
    got_grad1 = swap(branch_grad1, "expert", 1)
    (shared_grad1,), (got_grad1,) = shared_call(
        0, False, True, order, message1, branch_grad1, weights, hide=[got_grad1]
    )
    far_grad1, far1, back3 = z(branch_grad1, 2), z(message1, 2), z(sent3, 1)
    (kept, sent), (far_grad1, far1, back3) = weight_grads_call(
        1,
        True,
        True,
        order,
        [(item,) for item in (message3, got3, far3, farther3)],
        [(item,) for item in (last_grad, got_last, far_last, farther_last)],
        weights,
        hide=[far_grad1, far1, back3],
    )
    flow1.add(kept, sent)
    flow1.add(kept_a, sent_a)
    (back_message1,), (flow1.parts[0][1], flow1.parts[1][1]) = experts_call(
        0, False, True, order, got1, None, got_grad1, weights, extra0, kept_got1, (),
        hide=[flow1.parts[0][1], flow1.parts[1][1]],
    )
    back_grad1 = swap(back_message1, "expert", 1)
    flow1.first()
    (own_grad1, gate_grad1), (back_grad1,) = experts_call(
        0, False, True, order, message1, gates1, branch_grad1, weights, extra0, kept_own1,
        (shared_grad1,), hide=[back_grad1],
    )
    farther1, farther_grad1 = z(far1, 1), z(far_grad1, 1)
    (token_grad, kept_a, sent_a, small0), (farther1, farther_grad1) = order.call(
        functools.partial(attention_backward_body, 0),
        [
            (item,)
            for item in (
                grad1, stream1, message1, own_grad1, back_grad1, gates1, gate_grad1,
                tokens, hidden0, qkv0, attended0, branch0,
            )
        ]
        + attn_back_ins(0),
        [((rows, width), fl)] + grad_outs,
        7.7,
        hide=[farther1, farther_grad1],
        scratch=proj,
    )
    flow1.second()

    branch3 = own3 + back3.astype(FLOAT)
    output = (stream3.astype(FLOAT) + mods[11:12] * branch3).astype(BFLOAT)
    gating3 = jnp.sum(cotangent.astype(FLOAT) * branch3, 0, keepdims=True)
    own_condition = jax.nn.silu(lax.dynamic_slice_in_dim(embedded, 2 * y + x_bit, 1).astype(FLOAT))
    own_condition = own_condition.astype(BFLOAT).astype(FLOAT)
    none = jnp.zeros((4, width), FLOAT)
    to_sections = jnp.concatenate(
        [
            small0[3:5], small0[2:3], own_condition, none,
            small0[0:2], small1[5:6], own_condition, none,
            small1[3:5], small1[2:3], own_condition, none,
            small1[0:2], gating3, own_condition, none,
        ]
    )
    to_sections = to_sections.reshape(4, 8, width)
    section = 2 * y + x_bit

    image = core * 4 + lax.axis_index("expert")
    spots = jnp.arange(32)[:, None] == jnp.arange(4)[None, :] * 8 + image
    def counted(route_pair):
        numbers = jnp.arange(experts_total, dtype=jnp.int32)
        return jnp.sum((route_pair.reshape(-1)[:, None] == numbers[None, :]).astype(FLOAT), 0)

    device = section * 8 + image
    counts = jnp.tile(jnp.concatenate([counted(routes_one), counted(routes_two)]), 32)
    places = jnp.arange(width) // (2 * experts_total)
    counts = jnp.where(places == device, jnp.pad(counts, (0, width - 64 * experts_total)), 0.0)
    is_mine = jnp.arange(width) == device
    high, low = timesteps[0] // 32, timesteps[0] % 32
    def toward(by):
        return lax.dynamic_index_in_dim(to_sections, section ^ by, 0, keepdims=False)

    factors = [toward(0)] + [swap(toward(by), "section", by) for by in (1, 2, 3)]
    sources0 = (
        [(item,) for item in (message1, got1, far1, farther1)],
        [(item,) for item in (branch_grad1, got_grad1, far_grad1, farther_grad1)],
    )
    (kept, sent), (factors, flow1.got) = weight_grads_call(
        0, False, True, order, *sources0, weights, hide=[factors, flow1.got]
    )
    flow1.third()
    flow0.add(kept, sent)
    flow0.add(kept_a, sent_a)
    factors = jnp.take(jnp.stack(factors), jnp.arange(4) ^ section, axis=0)
    low_grads = factors[:, :3].reshape(4, 3 * width).astype(BFLOAT)
    condition_grad = back_product(low_grads, ada_weight[0])
    embed_grad = jax.vjp(jax.nn.silu, embedded.astype(FLOAT))[1](condition_grad)[0]
    embed_rows = jnp.sum(jnp.where(spots[:, :, None], embed_grad[None], 0.0), 1)

    misc = jnp.concatenate(
        [
            embed_rows,
            jnp.where(is_mine, high.astype(FLOAT), 0.0)[None],
            jnp.where(is_mine, low.astype(FLOAT), 0.0)[None],
            counts[None],
            jnp.zeros((29, width), FLOAT),
        ]
    )
    got_misc = swap(misc, "dp", 1)
    factors = ordered(core, factors, swap(factors, "dp", 1))
    hidden = [flow0.parts[0][1], flow0.parts[1][1], flow1.columns, got_misc]
    (kept, sent), hidden = weight_grads_call(
        0, True, False, order, *sources0, weights, hide=hidden
    )
    flow0.parts[0][1], flow0.parts[1][1], flow1.columns, got_misc = hidden
    flow0.add(kept, sent)
    flow0.parts = [flow0.parts[2], flow0.parts[0], flow0.parts[1]]
    flow1.relay()
    flow0.first((misc, got_misc))
    flow0.got, flow1.columns, factors = order.arrive((flow0.got, flow1.columns, factors))
    flow0.second()
    spread1 = flow1.column(True)
    flow0.got = order.arrive(flow0.got)
    flow0.third()
    flow0.columns, spread1.got = order.arrive((flow0.columns, spread1.got))
    spread1.pair()
    flow0.relay()
    flow0.columns, spread1.other_own = order.arrive((flow0.columns, spread1.other_own))
    spread0 = flow0.column(True)
    turns = [factors] + [z(factors, by) for by in (2, 1)]
    spread1.got, spread0.got, turns = order.arrive((spread1.got, spread0.got, turns))
    turns = [turns[0], turns[2], turns[1], z(turns[1], 1)]
    spread1.finish()
    spread0.pair()
    spread1.all, spread0.other_own, turns = order.arrive((spread1.all, spread0.other_own, turns))
    turns = jnp.take(jnp.stack(turns), jnp.arange(4) ^ place[3], axis=0)
    factors = turns.reshape(32, 8, width)
    mod_grads = factors[:, :3].reshape(-1, 3 * width)
    ada_out = lead_product(factors[:, 3].astype(BFLOAT), mod_grads.astype(BFLOAT))[None]
    ada_bias_out = jnp.sum(mod_grads, 0)[None]
    finals, (spread0.got, ada_out, ada_bias_out) = final_call(
        groups, 1, order, spread1.all, None, [spread0.got, ada_out, ada_bias_out]
    )
    spread0.finish()
    finals, _ = final_call(groups, 0, order, spread0.all, finals)
    e_up_out, e_down_out, _, s_up_out, s_down_out, qkv_out, out_w_out, _, *rest = finals
    qv_out, out_b_out, router_out, s_upb_out, s_downb_out, *rest = rest
    e_upb_out, e_downb_out, table_out, counts_out = rest
    counts_out = counts_out[0, : 2 * experts_total].reshape(2, experts_total)

    return (
        output,
        token_grad,
        table_out,
        ada_out,
        ada_bias_out,
        qkv_out,
        qv_out,
        out_w_out,
        out_b_out,
        router_out,
        s_up_out,
        s_upb_out,
        s_down_out,
        s_downb_out,
        e_up_out,
        e_upb_out,
        e_down_out,
        e_downb_out,
        counts_out,
    )


def shards(*args):
    fits = (
        lax.axis_size("section") == 4
        and lax.axis_size("dp") == 2
        and lax.axis_size("expert") == 4
        and args[12].shape[2] == 4
        and args[1].shape[0] == 1
    )
    return (shards_fast if fits else shards_general)(*args)


def solution(mesh):
    rows = P(ALL, None)
    whole = P()
    placed = (
        rows,
        P(ALL),
        rows,
        rows,
        rows,
        whole,
        P("section", None, None),
        P("section", None),
        *([whole] * 9),
        P(None, "expert", None, None),
        P(None, "expert", None),
        P(None, "expert", None, None),
        P(None, "expert", None),
    )
    return jax.shard_map(
        shards,
        mesh=mesh,
        in_specs=placed,
        out_specs=(
            rows,
            rows,
            whole,
            P("section", None, None),
            P("section", None),
            *([whole] * 9),
            P(None, "expert", None, None),
            P(None, "expert", None),
            P(None, "expert", None, None),
            P(None, "expert", None),
            whole,
        ),
        check_vma=False,
    )
```

```python
import functools

import jax
import jax.numpy as jnp
from jax import lax
from jax.experimental import pallas as pl
from jax.experimental.pallas import tpu as pltpu
from jax.sharding import PartitionSpec as P

HEADS = 6
HD = 64

BFLOAT = jnp.bfloat16
FLOAT = jnp.float32
ALL = ("section", "dp", "expert")


def product(left_arg, right_arg):
    return jnp.dot(left_arg, right_arg, preferred_element_type=FLOAT)


def lead_product(left_arg, right_arg):
    return lax.dot_general(
        left_arg, right_arg, (((0,), (0,)), ((), ())), preferred_element_type=FLOAT
    )


def back_product(left_arg, right_arg):
    return lax.dot_general(
        left_arg, right_arg, (((1,), (1,)), ((), ())), preferred_element_type=FLOAT
    )


def gelu_parts(pre):
    inner = 0.7978845608028654 * (pre + 0.044715 * pre * pre * pre)
    tanh = jnp.tanh(inner)
    act = 0.5 * pre * (1.0 + tanh)
    slope = 0.5 * (1.0 + tanh) + 0.5 * pre * (1.0 - tanh * tanh) * 0.7978845608028654 * (
        1.0 + 3 * 0.044715 * pre * pre
    )
    return act, slope


def normalized(stream):
    row_mean = jnp.mean(stream, -1, keepdims=True)
    centred = stream - row_mean
    variance = jnp.mean(centred * centred, -1, keepdims=True)
    inverse = lax.rsqrt(variance + 1e-06)
    return centred * inverse, inverse


def modulate(stream, mod):
    unit, _ = normalized(stream)
    return (unit * (1.0 + mod[1]) + mod[0]).astype(BFLOAT)


def norm_backward(stream, mod, hidden_grad):
    unit, inverse = normalized(stream)
    shift_grad = jnp.sum(hidden_grad, 0)
    scale_grad = jnp.sum(hidden_grad * unit, 0)
    unit_grad = hidden_grad * (1.0 + mod[1])
    stream_grad = inverse * (
        unit_grad
        - jnp.mean(unit_grad, -1, keepdims=True)
        - unit * jnp.mean(unit_grad * unit, -1, keepdims=True)
    )
    return stream_grad, shift_grad, scale_grad


def heads_view(rows):
    return rows.astype(BFLOAT).reshape(-1, HEADS, HD)


def attention_forward(hidden, weights):
    qkv_matrix, qv_offset, out_matrix, out_offset = weights
    width = hidden.shape[1]
    projected = product(hidden, qkv_matrix)
    query = heads_view(projected[:, :width] + qv_offset[:width])
    key = heads_view(projected[:, width : 2 * width])
    value = heads_view(projected[:, 2 * width :] + qv_offset[width:])
    scores = jnp.einsum("qhd,khd->hqk", query, key, preferred_element_type=FLOAT) * HD ** (-0.5)
    probs = jax.nn.softmax(scores, -1)
    probs_low = probs.astype(BFLOAT)
    attended = (
        jnp.einsum("hqk,khd->qhd", probs_low, value, preferred_element_type=FLOAT)
        .reshape(-1, width)
        .astype(BFLOAT)
    )
    branch = product(attended, out_matrix) + out_offset
    return branch, (query, key, value, probs, probs_low, attended)


def attention_backward(hidden, weights, saved, branch_grad):
    qkv_matrix, _, out_matrix, _ = weights
    query, key, value, probs, probs_low, attended = saved
    width = hidden.shape[1]
    factor = HD ** (-0.5)
    low_grad = branch_grad.astype(BFLOAT)
    out_grad = lead_product(attended, low_grad)
    out_offset_grad = jnp.sum(low_grad.astype(FLOAT), 0)
    attended_grad = heads_view(back_product(low_grad, out_matrix))
    value_grad = jnp.einsum("hqk,qhd->khd", probs_low, attended_grad, preferred_element_type=FLOAT)
    prob_grad = jnp.einsum("qhd,khd->hqk", attended_grad, value, preferred_element_type=FLOAT)
    score_grad = (probs * (prob_grad - jnp.sum(prob_grad * probs, -1, keepdims=True))).astype(
        BFLOAT
    )
    query_grad = (
        jnp.einsum("hqk,khd->qhd", score_grad, key, preferred_element_type=FLOAT) * factor
    )
    key_grad = (
        jnp.einsum("hqk,qhd->khd", score_grad, query, preferred_element_type=FLOAT) * factor
    )
    proj_grad = jnp.concatenate(
        [item.reshape(-1, width) for item in (query_grad, key_grad, value_grad)], -1
    ).astype(BFLOAT)
    qkv_grad = lead_product(hidden, proj_grad)
    sums = jnp.sum(proj_grad.astype(FLOAT), 0)
    offset_grad = jnp.concatenate([sums[:width], sums[2 * width :]])
    hidden_grad = back_product(proj_grad, qkv_matrix)
    return hidden_grad, (qkv_grad, offset_grad, out_grad, out_offset_grad)


def expert_gates(rows, router, route_pair):
    logits = product(rows, router)
    marks = (
        route_pair[:, :, None] == jnp.arange(router.shape[1], dtype=jnp.int32)[None, None, :]
    ).any(1)
    top = jnp.max(jnp.where(marks, logits, -jnp.inf), -1, keepdims=True)
    raised = jnp.where(marks, jnp.exp(logits - top), 0.0)
    return raised / jnp.sum(raised, -1, keepdims=True)


def pick_column(table, column):
    return lax.dynamic_slice_in_dim(table, column, 1, axis=1)


def moe_forward(hidden, route_pair, weights):
    router, s_up, s_upb, s_down, s_downb, e_up, e_upb, e_down, e_downb = weights
    mine = lax.axis_index("expert")
    rows = lax.all_gather(hidden, "expert", axis=0, tiled=True)
    routes = lax.all_gather(route_pair, "expert", axis=0, tiled=True)
    gates = expert_gates(rows, router, routes)
    gate = pick_column(gates, mine)
    shared_pre = product(hidden, s_up) + s_upb
    shared_act, shared_slope = gelu_parts(shared_pre)
    shared_act = shared_act.astype(BFLOAT)
    shared_out = product(shared_act, s_down) + s_downb
    pre = product(rows, e_up[0]) + e_upb[0]
    act, slope = gelu_parts(pre)
    act = act.astype(BFLOAT)
    result = (product(act, e_down[0]) + e_downb[0]).astype(BFLOAT)
    routed = lax.psum_scatter(
        (gate * result.astype(FLOAT)).astype(BFLOAT), "expert", scatter_dimension=0, tiled=True
    )
    branch = shared_out + routed.astype(FLOAT)
    saved = (rows, routes, gates, gate, shared_act, shared_slope, act, slope, result)
    return branch, saved


def moe_backward(hidden, weights, saved, branch_grad):
    router, s_up, s_upb, s_down, s_downb, e_up, e_upb, e_down, e_downb = weights
    rows, routes, gates, gate, shared_act, shared_slope, act, slope, result = saved
    mine = lax.axis_index("expert")
    devices = lax.axis_size("expert")
    tokens_here = hidden.shape[0]
    low_grad = branch_grad.astype(BFLOAT)
    s_down_grad = lead_product(shared_act, low_grad)
    s_downb_grad = jnp.sum(low_grad.astype(FLOAT), 0)
    shared_dpre = (back_product(low_grad, s_down) * shared_slope).astype(BFLOAT)
    s_up_grad = lead_product(hidden, shared_dpre)
    s_upb_grad = jnp.sum(shared_dpre.astype(FLOAT), 0)
    hidden_grad = back_product(shared_dpre, s_up)
    row_grad = lax.all_gather(low_grad, "expert", axis=0, tiled=True).astype(FLOAT)
    gate_grad = jnp.sum(row_grad * result.astype(FLOAT), -1)
    gate_grads = lax.all_to_all(
        gate_grad.reshape(devices, tokens_here).astype(BFLOAT), "expert", 0, 0, tiled=True
    ).astype(FLOAT)
    own_gates = lax.dynamic_slice_in_dim(gates, mine * tokens_here, tokens_here, axis=0)
    gate_grads = gate_grads.T
    logit_grad = own_gates * (gate_grads - jnp.sum(own_gates * gate_grads, -1, keepdims=True))
    router_grad = lax.dot_general(
        hidden.astype(FLOAT),
        logit_grad,
        (((0,), (0,)), ((), ())),
        precision=lax.Precision.HIGHEST,
        preferred_element_type=FLOAT,
    )
    result_grad = (gate * row_grad).astype(BFLOAT)
    e_down_grad = lead_product(act, result_grad)
    e_downb_grad = jnp.sum(result_grad.astype(FLOAT), 0)
    dpre = (back_product(result_grad, e_down[0]) * slope).astype(BFLOAT)
    e_up_grad = lead_product(rows, dpre)
    e_upb_grad = jnp.sum(dpre.astype(FLOAT), 0)
    back_rows = lax.psum_scatter(
        back_product(dpre, e_up[0]).astype(BFLOAT), "expert", scatter_dimension=0, tiled=True
    )
    hidden_grad = hidden_grad + back_product(logit_grad, router.astype(FLOAT)) + back_rows
    return hidden_grad, (
        router_grad,
        s_up_grad,
        s_upb_grad,
        s_down_grad,
        s_downb_grad,
        e_up_grad,
        e_upb_grad,
        e_down_grad,
        e_downb_grad,
    )


def shards_general(
    tokens,
    timesteps,
    routes_one,
    routes_two,
    cotangent,
    time_table,
    ada_weight,
    ada_bias,
    qkv_weight,
    qv_bias,
    out_weight,
    out_bias,
    router_weight,
    shared_up,
    shared_up_bias,
    shared_down,
    shared_down_bias,
    expert_up,
    expert_up_bias,
    expert_down,
    expert_down_bias,
):
    width = tokens.shape[1]
    steps_count = time_table.shape[0]
    experts_total = router_weight.shape[2]
    route_sets = (routes_one, routes_two)
    steps = lax.all_gather(timesteps, "section", axis=0, tiled=True)
    embedded = jnp.take(time_table, steps, axis=0).astype(FLOAT)
    condition = jax.nn.silu(embedded).astype(BFLOAT)
    section_mod = product(condition, ada_weight[0]) + ada_bias[0].astype(FLOAT)
    mods = lax.all_to_all(section_mod, "section", 0, 0, tiled=True).reshape(-1, 3, width)

    def attn_weights(layer):
        return (
            qkv_weight[layer],
            qv_bias[layer].astype(FLOAT),
            out_weight[layer],
            out_bias[layer].astype(FLOAT),
        )

    def moe_weights(layer):
        return (
            router_weight[layer],
            shared_up[layer],
            shared_up_bias[layer].astype(FLOAT),
            shared_down[layer],
            shared_down_bias[layer].astype(FLOAT),
            expert_up[layer],
            expert_up_bias[layer].astype(FLOAT),
            expert_down[layer],
            expert_down_bias[layer].astype(FLOAT),
        )

    streams, hiddens, branches, kept = [], [], [], []
    stream = tokens
    for block in range(4):
        layer = block // 2
        streams.append(stream)
        wide = stream.astype(FLOAT)
        hidden = modulate(wide, mods[block])
        if block % 2 == 0:
            branch, saved = attention_forward(hidden, attn_weights(layer))
        else:
            branch, saved = moe_forward(hidden, route_sets[layer], moe_weights(layer))
        hiddens.append(hidden)
        branches.append(branch)
        kept.append(saved)
        stream = (wide + mods[block][2] * branch).astype(BFLOAT)
    output = stream

    upstream = cotangent
    mod_grads = [None] * 4
    attn_grads = [None] * 2
    moe_grads = [None] * 2
    for block in (3, 2, 1, 0):
        layer = block // 2
        wide_grad = upstream.astype(FLOAT)
        gating_grad = jnp.sum(wide_grad * branches[block], 0)
        branch_grad = mods[block][2] * wide_grad
        if block % 2 == 0:
            hidden_grad, attn_grads[layer] = attention_backward(
                hiddens[block], attn_weights(layer), kept[block], branch_grad
            )
        else:
            hidden_grad, moe_grads[layer] = moe_backward(
                hiddens[block], moe_weights(layer), kept[block], branch_grad
            )
        stream_grad, shift_grad, scale_grad = norm_backward(
            streams[block].astype(FLOAT), mods[block], hidden_grad
        )
        mod_grads[block] = jnp.concatenate([shift_grad, scale_grad, gating_grad])
        token_grad = wide_grad + stream_grad
        upstream = token_grad.astype(BFLOAT)

    section_grads = lax.all_to_all(jnp.stack(mod_grads), "section", 0, 0, tiled=True)
    ada_part = lead_product(condition, section_grads.astype(BFLOAT))
    condition_grad = back_product(section_grads, ada_weight[0].astype(FLOAT))
    condition_grad = lax.psum(condition_grad, "section")
    embed_grad = jax.vjp(jax.nn.silu, embedded)[1](condition_grad)[0]
    marks = (steps[:, None] == jnp.arange(steps_count, dtype=jnp.int32)[None, :]).astype(FLOAT)
    table_part = lead_product(marks, embed_grad)

    def counted(route_pair):
        return jnp.sum(
            (
                route_pair.reshape(-1)[:, None]
                == jnp.arange(experts_total, dtype=jnp.int32)[None, :]
            ).astype(jnp.int32),
            0,
        )

    def total(parts, axes):
        return lax.psum(parts.astype(BFLOAT), axes).astype(FLOAT)

    both_attn = [jnp.stack([attn_grads[0][n], attn_grads[1][n]]) for n in range(4)]
    both_moe = [jnp.stack([moe_grads[0][n], moe_grads[1][n]]) for n in range(9)]
    counts = lax.psum(jnp.stack([counted(routes_one), counted(routes_two)]), ALL)
    attn_out = [total(item, ALL) for item in both_attn]
    moe_out = [total(item, ALL) for item in both_moe[:5]]
    expert_out = [total(item, ("section", "dp"))[:, None] for item in both_moe[5:]]
    table_out = total(table_part, ("dp", "expert"))
    ada_out = total(ada_part, ("dp", "expert"))[None]
    ada_bias_out = total(jnp.sum(section_grads, 0), ("dp", "expert"))[None]
    return (
        output,
        token_grad,
        table_out,
        ada_out,
        ada_bias_out,
        *attn_out,
        *moe_out,
        *expert_out,
        counts,
    )


def norm_parts(wide):
    row_mean = jnp.mean(wide, -1, keepdims=True)
    centred = wide - row_mean
    variance = jnp.mean(centred * centred, -1, keepdims=True)
    inverse = lax.rsqrt(variance + 1e-06)
    return centred * inverse, inverse


def norm_grad(unit, inverse, scaling, hidden_grad):
    shift_grad = jnp.sum(hidden_grad, 0, keepdims=True)
    scale_grad = jnp.sum(hidden_grad * unit, 0, keepdims=True)
    unit_grad = hidden_grad * (1.0 + scaling)
    stream_grad = inverse * (
        unit_grad
        - jnp.mean(unit_grad, -1, keepdims=True)
        - unit * jnp.mean(unit_grad * unit, -1, keepdims=True)
    )
    return stream_grad, shift_grad, scale_grad


def whole_spec(array):
    return pl.BlockSpec(array.shape, lambda *_: (0,) * array.ndim)


def layer_spec(array, layer):
    block = (None,) + array.shape[1:]
    return pl.BlockSpec(block, lambda *_: (layer,) + (0,) * (array.ndim - 1))


def kernel_call(body, ins, outs, flops, grid=(1,), scratch=(), prefetch=()):
    arrays = [item[0] for item in ins]
    specs = [item[1] if len(item) > 1 else whole_spec(item[0]) for item in ins]
    moved = sum(array.size * array.dtype.itemsize for array in arrays)
    return pl.pallas_call(
        body,
        out_shape=[
            (pltpu.HBM if far else jax.ShapeDtypeStruct)(shape, dtype) for shape, dtype, *far in outs
        ],
        grid_spec=pltpu.PrefetchScalarGridSpec(
            num_scalar_prefetch=len(prefetch),
            grid=grid,
            in_specs=specs,
            out_specs=[
                pl.BlockSpec(item[0], lambda *_, rank=len(item[0]): (0,) * rank) for item in outs
            ],
            scratch_shapes=list(scratch),
        ),
        cost_estimate=pl.CostEstimate(flops=flops, bytes_accessed=moved, transcendentals=0),
        compiler_params=pltpu.CompilerParams(vmem_limit_bytes=32 << 20),
    )(*prefetch, *arrays)


def mod_of(mods, block, part):
    row = 3 * block + part
    return mods[row : row + 1, :]


def head_pairs(width):
    for pair in range(HEADS // 2):
        start = pair * 2 * HD
        yield slice(start, start + 2 * HD), slice(width + start, width + start + 2 * HD), slice(
            2 * width + start, 2 * width + start + 2 * HD
        )


def masked(mask, rows):
    return jnp.where(mask, rows, jnp.zeros_like(rows))


def head_probs(query, key):
    scores = back_product(query, key) * HD ** (-0.5)
    raised = jnp.exp(scores - jnp.max(scores, -1, keepdims=True))
    return raised * (1.0 / jnp.sum(raised, -1, keepdims=True))


def gate_column(gates, expert):
    lanes = lax.broadcasted_iota(jnp.int32, gates.shape, 1)
    return jnp.sum(jnp.where(lanes == expert, gates, 0.0), -1, keepdims=True)


def gelu_value(pre):
    pre = pre.astype(BFLOAT)
    tanh = jnp.tanh(pre * (BFLOAT(0.7978845608028654) + BFLOAT(0.035677408136300125) * (pre * pre)))
    half = BFLOAT(0.5) * pre
    return half + half * tanh


def gelu_both(pre):
    pre = pre.astype(BFLOAT)
    square = pre * pre
    tanh = jnp.tanh(pre * (BFLOAT(0.7978845608028654) + BFLOAT(0.035677408136300125) * square))
    half = BFLOAT(0.5) * pre
    slope = (BFLOAT(0.5) + BFLOAT(0.5) * tanh) + (half * (BFLOAT(1.0) - tanh * tanh)) * (
        BFLOAT(0.7978845608028654) + BFLOAT(0.10703222440890037) * square
    )
    return half + half * tanh, slope


def far(x):
    return pltpu.with_memory_space_constraint(x, pltpu.HBM)


def gates_of(rows, routes, router):
    logits = product(rows, router)
    lanes = lax.broadcasted_iota(jnp.int32, logits.shape, 1)
    marks = (lanes == routes[:, 0:1]) | (lanes == routes[:, 1:2])
    top = jnp.max(jnp.where(marks, logits, -jnp.inf), -1, keepdims=True)
    raised = jnp.where(marks, jnp.exp(logits - top), 0.0)
    return raised / jnp.sum(raised, -1, keepdims=True)


def write_columns(out, start, table):
    rows = table.shape[0]
    turned = jnp.transpose(table)[:8]
    rounded = turned.astype(BFLOAT).astype(FLOAT)
    both = jnp.concatenate([rounded, turned - rounded]).astype(BFLOAT)
    out[start : start + 16, :] = jnp.zeros((16, out.shape[1]), BFLOAT)
    out[start : start + 16, :rows] = both


def read_columns(message, start, rows):
    both = message[start : start + 16, :rows].astype(FLOAT)
    turned = jnp.concatenate([both[:8] + both[8:], jnp.zeros((120, rows), FLOAT)])
    return jnp.transpose(turned)


def attention_forward_body(block, place, *refs):
    layer = block // 2
    refs = list(refs)
    pop = lambda count: [refs.pop(0) for _ in range(count)]
    if block:
        stream, own, back = pop(3)
    else:
        stream, cotangent = pop(2)
    mods, qkv_w, qv_b, out_w, out_b, router, routes = pop(7)
    if block:
        stream_out, before_out = pop(2)
        before = own[...] + back[...].astype(FLOAT)
        before_out[...] = before
        low_stream = (stream[...].astype(FLOAT) + mod_of(mods, block - 1, 2) * before).astype(BFLOAT)
        stream_out[...] = low_stream
        wide = low_stream.astype(FLOAT)
    else:
        wide = stream[...].astype(FLOAT)
    hidden_out, qkv_out, attended_out, branch_out, new_out, message_out, gates_out = pop(7)
    rows, width = wide.shape
    unit, _ = norm_parts(wide)
    hidden = (unit * (1.0 + mod_of(mods, block, 1)) + mod_of(mods, block, 0)).astype(BFLOAT)
    hidden_out[...] = hidden
    bias = qv_b[layer : layer + 1, :].astype(FLOAT)
    projected = product(hidden, qkv_w[...])
    qkv_out[:, :width] = (projected[:, :width] + bias[:, :width]).astype(BFLOAT)
    qkv_out[:, width : 2 * width] = projected[:, width : 2 * width].astype(BFLOAT)
    qkv_out[:, 2 * width :] = (projected[:, 2 * width :] + bias[:, width:]).astype(BFLOAT)
    low = lax.broadcasted_iota(jnp.int32, (rows, 2 * HD), 1) < HD
    for query_at, key_at, value_at in head_pairs(width):
        query, key, value = qkv_out[:, query_at], qkv_out[:, key_at], qkv_out[:, value_at]
        parts = [
            product(head_probs(masked(mask, query), key).astype(BFLOAT), value)
            for mask in (low, ~low)
        ]
        attended_out[:, query_at] = jnp.where(low, parts[0], parts[1]).astype(BFLOAT)
    branch = product(attended_out[...], out_w[...]) + out_b[layer : layer + 1, :].astype(FLOAT)
    branch_out[...] = branch
    new = (wide + mod_of(mods, block, 2) * branch).astype(BFLOAT)
    new_out[...] = new
    unit, _ = norm_parts(new.astype(FLOAT))
    following = (unit * (1.0 + mod_of(mods, block + 1, 1)) + mod_of(mods, block + 1, 0)).astype(
        BFLOAT
    )
    gates = gates_of(following, routes, router[...])
    gates_out[...] = gates
    message_out[:rows, :] = following
    write_columns(message_out, rows, gates)
    if not block:
        (last,) = pop(1)
        last[...] = (mod_of(mods, 3, 2) * cotangent[...].astype(FLOAT)).astype(BFLOAT)


def keep_or_send(place, core, kept, sent, piece, at, value):
    @pl.when(place[0] == core)
    def _():
        kept[piece, at, :] = value

    @pl.when(place[0] != core)
    def _():
        sent[piece, at, :] = value


def attention_backward_body(block, place, *refs):
    (
        upstream, after, after_message, own_grad, message, own_gates, gate_grads,
        stream, hidden, qkv, attended, branch, mods, router, qkv_w, out_w, *refs,
    ) = refs
    if block:
        before, grad_out, before_grad_out, kept, sent, small_out, proj = refs
    else:
        grad_out, kept, sent, small_out, proj = refs
    rows, width = stream.shape
    small_out[...] = jnp.zeros_like(small_out)

    gate_grad = gate_grads[...] + read_columns(message, rows, rows)
    gates = own_gates[...]
    logit_grad = gates * (gate_grad - jnp.sum(gates * gate_grad, -1, keepdims=True))
    logit_grad = logit_grad.astype(BFLOAT)
    router_grad = lead_product(logit_grad, after_message[:rows, :])[:4]
    hidden_grad = (
        own_grad[...] + message[:rows, :].astype(FLOAT) + back_product(logit_grad, router[...])
    )
    unit, inverse = norm_parts(after[...].astype(FLOAT))
    after_grad, shift_grad, scale_grad = norm_grad(
        unit, inverse, mod_of(mods, block + 1, 1), hidden_grad
    )
    small_out[0:1, :] = shift_grad
    small_out[1:2, :] = scale_grad
    wide_grad = (upstream[...].astype(FLOAT) + after_grad).astype(BFLOAT).astype(FLOAT)

    small_out[2:3, :] = jnp.sum(wide_grad * branch[...], 0, keepdims=True)
    branch_grad = (mod_of(mods, block, 2) * wide_grad).astype(BFLOAT)
    out_bias_grad = jnp.sum(branch_grad.astype(FLOAT), 0, keepdims=True)
    attended_grad = back_product(branch_grad, out_w[...]).astype(BFLOAT)
    low = lax.broadcasted_iota(jnp.int32, (rows, 2 * HD), 1) < HD
    factor = HD ** (-0.5)
    for query_at, key_at, value_at in head_pairs(width):
        query, key, value = qkv[:, query_at], qkv[:, key_at], qkv[:, value_at]
        pair_grad = attended_grad[:, query_at]
        sums = None
        for mask in (low, ~low):
            own_query, own_pair = masked(mask, query), masked(mask, pair_grad)
            probs = head_probs(own_query, key)
            value_grad = lead_product(probs.astype(BFLOAT), own_pair)
            prob_grad = back_product(own_pair, value)
            score_grad = (
                probs * (prob_grad - jnp.sum(prob_grad * probs, -1, keepdims=True))
            ).astype(BFLOAT)
            query_grad = masked(mask, product(score_grad, key))
            key_grad = lead_product(score_grad, own_query)
            parts = (query_grad, key_grad, value_grad)
            sums = parts if sums is None else tuple(a + b for a, b in zip(sums, parts))
        proj[:, query_at] = (sums[0] * factor).astype(BFLOAT)
        proj[:, key_at] = (sums[1] * factor).astype(BFLOAT)
        proj[:, value_at] = sums[2].astype(BFLOAT)

    middle = width // 2
    for part in range(4):
        if part < 3:
            grad = lead_product(hidden[...], proj[:, part * width : (part + 1) * width])
        else:
            grad = lead_product(attended[...], branch_grad)
        for side in range(2):
            keep_or_send(
                place,
                part // 2,
                kept,
                sent,
                2 * (part % 2) + side,
                slice(32, 32 + middle),
                grad[side * middle : (side + 1) * middle].astype(BFLOAT),
            )
    extra = jnp.concatenate(
        [
            jnp.sum(proj[:, :width].astype(FLOAT), 0, keepdims=True),
            jnp.sum(proj[:, 2 * width :].astype(FLOAT), 0, keepdims=True),
            out_bias_grad,
            router_grad,
            jnp.zeros((25, width), FLOAT),
        ]
    ).astype(BFLOAT)
    tail = slice(0, 32)
    for piece in range(4):
        for core in range(2):
            value = extra if piece == 0 and core == 0 else jnp.zeros((32, width), BFLOAT)
            keep_or_send(place, core, kept, sent, piece, tail, value)

    hidden_grad = back_product(proj[...], qkv_w[...])
    unit, inverse = norm_parts(stream[...].astype(FLOAT))
    stream_grad, shift_grad, scale_grad = norm_grad(
        unit, inverse, mod_of(mods, block, 1), hidden_grad
    )
    small_out[3:4, :] = shift_grad
    small_out[4:5, :] = scale_grad
    grad = wide_grad + stream_grad
    if block:
        low_grad = grad.astype(BFLOAT)
        grad_out[...] = low_grad
        wide_grad = low_grad.astype(FLOAT)
        before_grad_out[...] = (mod_of(mods, block - 1, 2) * wide_grad).astype(BFLOAT)
        small_out[5:6, :] = jnp.sum(wide_grad * before[...], 0, keepdims=True)
    else:
        grad_out[...] = grad


def shared_body(layer, forward, backward, place, *refs):
    refs = list(refs)
    pop = lambda count: [refs.pop(0) for _ in range(count)]
    (message,) = pop(1)
    branch_grad = pop(1)[0] if backward else None
    up, up_bias, down, down_bias = pop(4)
    total = pop(1)[0] if forward else None
    grads = pop(1)[0] if backward else None
    rows = message.shape[0] - 16
    pre = product(message[:rows, :], up[...]) + up_bias[layer : layer + 1, :].astype(FLOAT)
    if backward:
        act, slope = gelu_both(pre)
        act_grad = (back_product(branch_grad[...], down[...]) * slope).astype(BFLOAT)
        part = back_product(act_grad, up[...])

        @pl.when(pl.program_id(0) == 0)
        def _():
            grads[...] = part

        @pl.when(pl.program_id(0) > 0)
        def _():
            grads[...] += part

    else:
        act = gelu_value(pre)
    if forward:
        part = product(act.astype(BFLOAT), down[...])

        @pl.when(pl.program_id(0) == 0)
        def _():
            total[...] = part + down_bias[layer : layer + 1, :].astype(FLOAT)

        @pl.when(pl.program_id(0) > 0)
        def _():
            total[...] += part


def shared_call(layer, forward, backward, order, message, branch_grad, weights, hide=None):
    up, up_bias, down, down_bias = weights[:4]
    rows, width = message.shape[0] - 16, message.shape[1]
    units = 768 if forward and backward else 1536
    ins = [(message,)] + [(branch_grad,)] * backward
    ins += [
        (up, pl.BlockSpec((None, width, units), lambda i, _: (layer, 0, i))),
        (up_bias, pl.BlockSpec((2, units), lambda i, _: (0, i))),
        (down, pl.BlockSpec((None, units, width), lambda i, _: (layer, i, 0))),
        (down_bias,),
    ]
    return order.call(
        functools.partial(shared_body, layer, forward, backward),
        ins,
        [((rows, width), FLOAT)] * (forward + backward),
        5.0,
        hide=hide,
        grid=(up.shape[2] // units,),
    )


def experts_body(layer, forward, backward, partner, place, *refs):
    refs = list(refs)
    pop = lambda count: [refs.pop(0) for _ in range(count)]
    (message,) = pop(1)
    own_gates = None if partner else pop(1)[0]
    branch_grad = pop(1)[0] if backward else None
    e_up, e_upb, e_down, e_downb, own_up, got_up, own_down, got_down, x_upb, x_downb = pop(10)
    kept = pop(1)[0] if backward and not forward else None
    shared_out = pop(1)[0] if forward and not partner else None
    shared_grad = pop(1)[0] if backward and not partner else None
    if forward:
        total_out = pop(1)[0]
        kept_out = None if backward else pop(1)[0]
    if backward:
        grad_out = pop(1)[0]
        gate_grad_out = None if partner else pop(1)[0]
    x_up, x_down, total, sems = pop(4)
    if partner:
        (gates,) = pop(1)
    else:
        gates = own_gates
    if backward:
        grads, gate_grad = pop(2)
    step = pl.program_id(0)
    rows = message.shape[0] - 16
    lanes = lax.broadcasted_iota(jnp.int32, (rows, 128), 1)

    def copies():
        pairs = (
            (own_up, x_up.at[place[0]]),
            (own_down, x_down.at[place[0]]),
            (got_up, x_up.at[1 - place[0]]),
            (got_down, x_down.at[1 - place[0]]),
        )
        return [
            pltpu.make_async_copy(source, target, sems.at[number])
            for number, (source, target) in enumerate(pairs)
        ]

    @pl.when(step == 0)
    def _():
        if partner:
            gates[...] = read_columns(message, rows, rows)
        for copy in copies():
            copy.start()

    def expert(index, number, up, up_bias, down, down_bias):
        gate = gate_column(gates[...], number)
        pre = product(message[:rows, :], up) + up_bias
        if backward:
            act, slope = gelu_both(pre)
            act_grad = (back_product(branch_grad[...], down) * slope * gate).astype(BFLOAT)
            part_grad = back_product(act_grad, up)
        else:
            act = gelu_value(pre)
        if forward:
            result = (product(act.astype(BFLOAT), down) + down_bias).astype(BFLOAT)
            if kept_out is not None:
                kept_out[index] = result
            result = result.astype(FLOAT)
            part = gate * result
        else:
            result = kept[index].astype(FLOAT)
        if backward:
            column = jnp.sum(branch_grad[...].astype(FLOAT) * result, -1, keepdims=True)
            part_gate = jnp.where(lanes == number, column, 0.0)
        if index == 0:
            if forward:
                total[...] = part
            if backward:
                grads[...] = part_grad
                gate_grad[...] = part_gate
            return
        if forward:
            part = part + total[...]
            if not partner:
                part = part + shared_out[...]
            total_out[...] = part.astype(total_out.dtype)
        if backward:
            part_grad = part_grad + grads[...]
            part_gate = part_gate + gate_grad[...]
            if partner:
                grad_out[:rows, :] = part_grad.astype(BFLOAT)
                write_columns(grad_out, rows, part_gate)
            else:
                grad_out[...] = part_grad + shared_grad[...]
                gate_grad_out[...] = part_gate

    @pl.when(step == 0)
    def _():
        expert(
            0, place[3], e_up[...], e_upb[layer].astype(FLOAT), e_down[...],
            e_downb[layer].astype(FLOAT),
        )

    @pl.when(step == 1)
    def _():
        for copy in copies():
            copy.wait()
        width, units = e_up.shape
        expert(
            1, place[3] ^ 2, x_up[...].reshape(width, units), x_upb[...].astype(FLOAT),
            x_down[...].reshape(units, width),
            x_downb[...].astype(FLOAT),
        )


def experts_call(
    layer,
    forward,
    backward,
    order,
    message,
    gates,
    branch_grad,
    weights,
    extra,
    kept,
    shared,
    hide=None,
):
    e_up, e_upb, e_down, e_downb = weights[4:]
    rows, width = message.shape[0] - 16, message.shape[1]
    units = e_up.shape[3]
    partner = gates is None
    ins = [(message,)]
    if not partner:
        ins += [(gates,)]
    if backward:
        ins += [(branch_grad,)]
    ins += [
        (e_up, pl.BlockSpec((None, None, width, units), lambda i, _: (layer, 0, 0, 0))),
        (e_upb,),
        (e_down, pl.BlockSpec((None, None, units, width), lambda i, _: (layer, 0, 0, 0))),
        (e_downb,),
    ]
    ins += [(item, pl.BlockSpec(memory_space=pltpu.HBM)) for item in extra[:4]]
    ins += [(item,) for item in extra[4:]]
    if backward and not forward:
        ins += [(far(kept),)]
    if not partner:
        ins += [(item,) for item in shared]
    outs = []
    scratch = [
        pltpu.VMEM((2,) + extra[0].shape, BFLOAT),
        pltpu.VMEM((2,) + extra[2].shape, BFLOAT),
        pltpu.VMEM((rows, width), FLOAT),
        pltpu.SemaphoreType.DMA((4,)),
    ]
    if partner:
        scratch += [pltpu.VMEM((rows, 128), FLOAT)]
    if forward:
        outs += [((rows, width), BFLOAT if partner else FLOAT)]
        if not backward:
            outs += [((2, rows, width), BFLOAT, True)]
    if backward:
        outs += [((rows + 16, width), BFLOAT)] if partner else [((rows, width), FLOAT)]
        if not partner:
            outs += [((rows, 128), FLOAT)]
        scratch += [pltpu.VMEM((rows, width), FLOAT), pltpu.VMEM((rows, 128), FLOAT)]
    return order.call(
        functools.partial(experts_body, layer, forward, backward, partner),
        ins,
        outs,
        6.0,
        hide=hide,
        grid=(2,),
        scratch=scratch,
    )


def weight_grads_body(layer, expert, shared, place, *refs):
    messages, branch_grads, refs = refs[0:4], refs[4:8], list(refs[8:])
    pop = lambda count: [refs.pop(0) for _ in range(count)]
    if expert:
        e_up, e_upb, e_down = pop(3)
    if shared:
        s_up, s_upb, s_down = pop(3)
    kept, sent, rows_all, grads_all, acts, pre_grads, sums_all = pop(7)
    step = pl.program_id(0)
    rows, width = 256, rows_all.shape[1]
    units = acts.shape[1]
    middle = width // 2
    unroll = True

    def fill_rows(gated):
        for side in range(4):
            at = slice(side * rows, (side + 1) * rows)
            grad = branch_grads[side][:rows, :]
            rows_all[at, :] = messages[side][:rows, :]
            if gated:
                gate = gate_column(read_columns(messages[side], rows, rows), place[3])
                grad = (gate * grad.astype(FLOAT)).astype(BFLOAT)
            grads_all[at, :] = grad
            bias = jnp.sum(grad.astype(FLOAT), 0, keepdims=True)
            if gated:
                sums_all[4:5, :] += bias
            else:
                sums_all[15:16, :] += jnp.where(place[3] == 0, bias, 0.0)

    def chunk(up, offset, down):
        def tile(side, sums):
            at = pl.ds(pl.multiple_of(side * rows, rows), rows)
            act, slope = gelu_both(product(rows_all[at, :], up[...]) + offset)
            acts[at, :] = act.astype(BFLOAT)
            grad = (back_product(grads_all[at, :], down[...]) * slope).astype(BFLOAT)
            pre_grads[at, :] = grad
            return sums + jnp.sum(grad.astype(FLOAT), 0, keepdims=True)

        return lax.fori_loop(0, 4, tile, jnp.zeros((1, units), FLOAT), unroll=unroll)

    def weight_pair(half):
        at = slice(half * width, (half + 1) * width)
        up_grad = lead_product(rows_all[...], pre_grads[:, at]).astype(BFLOAT)
        down_grad = lead_product(acts[:, at], grads_all[...]).astype(BFLOAT)
        return (0, up_grad), (1, down_grad)

    def tails(start):
        at = slice(start, start + 32)
        value = sums_all[...].astype(BFLOAT)
        for piece in range(4):
            for core in range(2):
                rest = jnp.zeros((32, width), BFLOAT)
                own = value if piece == 0 and core == 0 else rest
                keep_or_send(place, core, kept, sent, piece, at, own)

    if expert:
        for part in range(2):

            @pl.when(step == part)
            def _(part=part):
                if part == 0:
                    sums_all[...] = jnp.zeros_like(sums_all)
                    fill_rows(True)
                sums = chunk(e_up, e_upb[layer].astype(FLOAT), e_down)
                for half in range(2):
                    number = 2 * part + half
                    sums_all[number : number + 1, :] = sums[:, half * width : (half + 1) * width]
                    for core, grad in weight_pair(half):
                        keep_or_send(place, core, kept, sent, number, slice(0, width), grad)
                if part == 1:
                    tails(width)

    if shared:

        @pl.when(step == 2 * expert)
        def _():
            sums_all[...] = jnp.zeros_like(sums_all)
            fill_rows(False)
            sums = chunk(s_up, s_upb[layer : layer + 1, :].astype(FLOAT), s_down)
            start = (width + 32) * expert
            where = slice(start, start + middle)
            for half in range(2):
                part_sums = sums[:, half * width : (half + 1) * width]
                for plane in range(4):
                    row = 7 + 2 * plane + half
                    sums_all[row : row + 1, :] = jnp.where(place[3] == plane, part_sums, 0.0)
                for core, grad in weight_pair(half):
                    for side in range(2):
                        value = grad[side * middle : (side + 1) * middle]
                        keep_or_send(place, core, kept, sent, 2 * half + side, where, value)
            tails(start + middle)


def weight_grads_call(layer, expert, shared, order, messages, branch_grads, weights, hide=None):
    s_up, s_upb, s_down, _, e_up, e_upb, e_down, _ = weights
    rows, width, units = 256, s_up.shape[1], 768
    at_own = lambda i: jnp.minimum(i, 1)
    ins = [(far(item[0]), *item[1:]) for item in (*messages, *branch_grads)]
    if expert:
        ins += [
            (e_up, pl.BlockSpec((None, None, width, units), lambda i, _: (layer, 0, 0, at_own(i)))),
            (e_upb, pl.BlockSpec((2, 1, units), lambda i, _: (0, 0, at_own(i)))),
            (
                e_down,
                pl.BlockSpec((None, None, units, width), lambda i, _: (layer, 0, at_own(i), 0)),
            ),
        ]
    if shared:
        ins += [
            (s_up, pl.BlockSpec((None, width, units), lambda i, at: (layer, 0, at[3]))),
            (s_upb, pl.BlockSpec((2, units), lambda i, at: (0, at[3]))),
            (s_down, pl.BlockSpec((None, units, width), lambda i, at: (layer, at[3], 0))),
        ]
    piece = (width + 32) * expert + (width // 2 + 32) * shared
    return order.call(
        functools.partial(weight_grads_body, layer, expert, shared),
        ins,
        [((4, piece, width), BFLOAT, True)] * 2,
        7.0 * (2 * expert + shared),
        hide=hide,
        grid=(2 * expert + shared,),
        scratch=[
            pltpu.VMEM((4 * rows, width), BFLOAT),
            pltpu.VMEM((4 * rows, width), BFLOAT),
            pltpu.VMEM((4 * rows, units), BFLOAT),
            pltpu.VMEM((4 * rows, units), BFLOAT),
            pltpu.VMEM((32, width), FLOAT),
        ],
    )


def swap(x, axis, by):
    return lax.ppermute(x, axis, [(i, i ^ by) for i in range(lax.axis_size(axis))])


def bits():
    section = lax.axis_index("section")
    return lax.axis_index("dp"), section // 2, section % 2


def ordered(bit, mine, other):
    return jnp.stack([jnp.where(bit == 0, mine, other), jnp.where(bit == 0, other, mine)])


def wide_sum(*parts):
    total = parts[0].astype(FLOAT)
    for part in parts[1:]:
        total = total + part.astype(FLOAT)
    return total


class Groups:
    def __init__(self, expert, shared, every):
        self.expert, self.shared, self.every = expert, shared, every
        self.rows = expert + shared + every
        self.half = self.rows // 2
        self.sent = expert // 2 + 2 * shared + every // 2


def first_body(parts, has_misc, place, *refs):
    keeps, gots, refs = refs[:parts], refs[parts : 2 * parts], refs[2 * parts :]
    if has_misc:
        misc, got_misc, *refs = refs
    keep_a, send_a, keep_b, send_b, pieces = refs
    half = keep_a.shape[1]
    y, x = place[1], place[2]
    for piece in range(4):
        at = 0
        for keep, got in zip(keeps[:-1], gots[:-1]):
            rows = keep.shape[1]
            total = wide_sum(keep[piece], got[piece])
            pieces[piece, at : at + rows, :] = total.astype(BFLOAT)
            at += rows
        joint = at - 32
        first = total[rows - 32 :]
        second = wide_sum(keeps[-1][piece], gots[-1][piece])
        small = first + second[:32]
        if has_misc and piece in (1, 2):
            at = slice(32 * (piece - 1), 32 * piece)
            small = small + jnp.where(place[0] == 0, misc[at, :] + got_misc[at, :], 0.0)
        pieces[piece, joint : joint + 32, :] = small.astype(BFLOAT)
        pieces[piece, joint + 32 :, :] = second[32:].astype(BFLOAT)
    for other in range(2):
        keep_a[other] = pieces[2 * other + x, :half, :]
        send_a[other] = pieces[2 * other + 1 - x, :half, :]
        keep_b[other] = pieces[2 * y + other, half:, :]
        send_b[other] = pieces[2 * (1 - y) + other, half:, :]


def second_body(place, keep_a, got_a, keep_b, got_b, *outs):
    next_a, sent_a, next_b, sent_b = outs
    y, x = place[1], place[2]
    next_a[...] = wide_sum(keep_a[y], got_a[y]).astype(BFLOAT)
    sent_a[...] = wide_sum(keep_a[1 - y], got_a[1 - y]).astype(BFLOAT)
    next_b[...] = wide_sum(keep_b[x], got_b[x]).astype(BFLOAT)
    sent_b[...] = wide_sum(keep_b[1 - x], got_b[1 - x]).astype(BFLOAT)


def third_body(groups, place, keep_a, got_a, keep_b, got_b, *refs):
    *outs, piece = refs
    piece[: groups.half, :] = wide_sum(keep_a[...], got_a[...]).astype(BFLOAT)
    piece[groups.half :, :] = wide_sum(keep_b[...], got_b[...]).astype(BFLOAT)
    middle = groups.expert // 2
    if groups.expert:
        outs[0][...] = piece[:middle, :]
        outs[1][...] = piece[middle : 2 * middle, :]
    if groups.shared:
        outs[-1][...] = piece[2 * middle :, :]


def column_body(groups, joined, place, *refs):
    experts = (refs[0], refs[1]) if joined else None
    columns, sent = refs[2 * joined : 2 * joined + 4], refs[2 * joined + 4 :]
    z = place[3]
    shared, every = groups.shared // 2, groups.every // 2
    for side in range(2):
        out = sent[side]
        at = 0
        if joined:
            at = groups.expert // 2
            out[:at, :] = experts[side][...]
        for turn in range(4):
            to = pl.multiple_of(at + (z ^ turn) * shared, 16)
            out[pl.ds(to, shared), :] = columns[turn][side * shared : (side + 1) * shared, :]
        at += 4 * shared
        rows = slice(groups.shared + side * every, groups.shared + (side + 1) * every)
        first = wide_sum(columns[0][rows, :], columns[1][rows, :])
        second = wide_sum(columns[2][rows, :], columns[3][rows, :])
        out[at:, :] = (first + second).astype(BFLOAT)


def pair_body(place, own_a, got_a, own_b, got_b, out_a, out_b):
    y, x = place[1], place[2]
    out_a[y] = own_a[...]
    out_a[1 - y] = got_a[...]
    out_b[x] = own_b[...]
    out_b[1 - x] = got_b[...]


COST = 1.1e9


class Order:
    def __init__(self, place):
        self.place = place

    def call(self, body, ins, outs, micros, hide=None, **kwargs):
        outs = kernel_call(body, ins, outs, int(micros * COST), prefetch=(self.place,), **kwargs)
        if hide is None:
            self.place = lax.optimization_barrier((self.place, outs[-1]))[0]
            return outs
        self.place, outs, hide = lax.optimization_barrier((self.place, outs, hide))
        return outs, hide

    def arrive(self, xs):
        self.place, xs = lax.optimization_barrier((self.place, xs))
        return xs

    def tie(self, x):
        return lax.optimization_barrier((x, self.place))[0]

    def wait(self, x):
        self.place = lax.optimization_barrier((self.place, x))[0]


class Flow:
    def __init__(self, groups, order, slow):
        self.groups, self.order, self.parts = groups, order, []
        self.far = (True,) * slow

    def add(self, kept, sent):
        self.width = kept.shape[2]
        self.parts.append([kept, swap(sent, "dp", 1)])

    def across(self, turn, first, second):
        self.got = (
            swap(first, "section", 1 + turn),
            swap(second, "section", 2 - turn),
        )

    def first(self, misc=()):
        groups, width = self.groups, self.width
        ins = [kept for kept, _ in self.parts] + [got for _, got in self.parts] + list(misc)
        self.keep_a, send_a, self.keep_b, send_b = self.order.call(
            functools.partial(first_body, len(self.parts), bool(misc)),
            [(item,) for item in ins],
            [((2, groups.half, width), BFLOAT, *self.far), ((2, groups.half, width), BFLOAT)] * 2,
            4.0,
            scratch=[pltpu.VMEM((4, groups.rows, width), BFLOAT)],
        )
        self.across(0, send_a, send_b)

    def second(self):
        self.keep_a, send_a, self.keep_b, send_b = self.order.call(
            second_body,
            [(far(item),) for item in (self.keep_a, self.got[0], self.keep_b, self.got[1])],
            [
                ((self.groups.half, self.width), BFLOAT, *self.far),
                ((self.groups.half, self.width), BFLOAT),
            ]
            * 2,
            1.5,
        )
        self.across(1, send_a, send_b)

    def third(self):
        groups, width = self.groups, self.width
        outs = []
        if groups.expert:
            outs += [((groups.expert // 2, width), BFLOAT)] * 2
        if groups.shared:
            outs += [((groups.shared + groups.every, width), BFLOAT)]
        outs = self.order.call(
            functools.partial(third_body, groups),
            [(self.keep_a,), (self.got[0],), (self.keep_b,), (self.got[1],)],
            outs,
            1.5,
            scratch=[pltpu.VMEM((groups.rows, width), BFLOAT)],
        )
        self.expert = list(outs[:2]) if groups.expert else []
        if groups.shared:
            columns = outs[-1]
            self.columns = [columns, swap(columns, "expert", 1), swap(columns, "expert", 2)]

    def relay(self):
        self.columns.append(swap(self.order.tie(self.columns[2]), "expert", 1))

    def column(self, joined):
        ins = self.expert * joined + self.columns
        rows = self.groups.sent - self.groups.expert // 2 * (not joined)
        return Spread(
            self.order,
            self.order.call(
                functools.partial(column_body, self.groups, joined),
                [(far(item),) for item in ins],
                [((rows, self.width), BFLOAT)] * 2,
                1.5,
            ),
        )


class Spread:
    def __init__(self, order, own):
        self.order, self.own = order, own
        self.got = [swap(own[0], "section", 2), swap(own[1], "section", 1)]

    def pair(self):
        self.own = self.order.call(
            pair_body,
            [(self.own[0],), (self.got[0],), (self.own[1],), (self.got[1],)],
            [((2,) + item.shape, BFLOAT) for item in self.own],
            1.7,
        )
        self.got = [swap(self.own[0], "section", 1), swap(self.own[1], "section", 2)]
        self.other_own = [swap(item, "dp", 1) for item in self.own]

    def finish(self):
        for item in self.other_own:
            self.order.wait(item)
        other_got = [swap(item, "dp", 1) for item in self.got]
        own, got, other_own = self.own, self.got, self.other_own
        self.all = [own[0], got[0], own[1], got[1]]
        self.all += [other_own[0], other_got[0], other_own[1], other_got[1]]


def table_rows(steps, rows):
    count, width = steps.shape[1], rows.shape[1]
    lanes = lax.broadcasted_iota(jnp.int32, (1000, count), 1)
    places = lax.broadcasted_iota(jnp.int32, (1000, count), 0)
    marks = jnp.where((places == steps) & (lanes < 32), 1.0, 0.0).astype(BFLOAT)
    wide = jnp.concatenate([rows, jnp.zeros((count - 32, width), FLOAT)]).astype(BFLOAT)
    return product(marks, wide)


def final_body(groups, last, place, *refs):
    parts, refs = refs[:8], refs[8:]
    if last:
        small_one, bias_one, *refs = refs
        refs = refs[6:]
    up, down, bias, s_up, s_down, qkv, out_w, small, *refs = refs
    *refs, data, sems = refs
    step = pl.program_id(0)
    core, y, x = place[0], place[1], place[2]

    @pl.when(step == 0)
    def _():
        copies = []
        for chip in range(2):
            own_a, got_a, own_b, got_b = parts[4 * chip : 4 * chip + 4]
            owner = 1 - core if chip else core
            for other in range(2):
                for source, piece, side in (
                    (own_a, 2 * other + x, 0),
                    (got_a, 2 * other + 1 - x, 0),
                    (own_b, 2 * y + other, 1),
                    (got_b, 2 * (1 - y) + other, 1),
                ):
                    target = data.at[owner, piece, side]
                    sem = sems.at[len(copies)]
                    copies.append(pltpu.make_async_copy(source.at[other], target, sem))
        for copy in copies:
            copy.start()
        for copy in copies:
            copy.wait()

    rows = groups.expert // 2
    for part in range(4):

        @pl.when(step == 2 * part)
        def _(part=part):
            for out, owner in ((up, 0), (down, 1)):
                both = data[owner, part, :, :rows, :].reshape(groups.expert, -1)
                out[...] = both[: groups.expert - 32].astype(FLOAT)
                if owner == 0 and part == 0:
                    bias[...] = both[groups.expert - 32 :].astype(FLOAT)

    half = groups.shared // 2
    for number in range(8):

        @pl.when(step == number)
        def _(number=number):
            at, block = rows + number // 2 * half, number % 2
            for out, owner in ((s_up, 0), (s_down, 1)):
                both = data[owner, 2 * block : 2 * block + 2, :, at : at + half, :]
                out[...] = both.reshape(4 * half, -1).astype(FLOAT)

    every = groups.every // 2
    real = groups.every - 32
    start = rows + 4 * half
    for part in range(4):

        @pl.when(step == 2 * part)
        def _(part=part):
            target = qkv if part < 3 else out_w
            for piece in range(2):
                number = 2 * (part % 2) + piece
                both = data[part // 2, number, :, start : start + every, :]
                both = both.reshape(groups.every, -1)
                target[real * piece : real * (piece + 1), :] = both[32:].astype(FLOAT)
                if part < 2:
                    small[number] = both[:32].astype(FLOAT)

    if last:

        @pl.when(step == 7)
        def _():
            qv_b, out_b, router, s_upb, s_downb, e_upb, e_downb, table, counts = refs
            width = data.shape[4]
            for layer, rest, biases in ((0, small, bias), (1, small_one, bias_one)):
                at = slice(layer, layer + 1)
                for row in range(2):
                    qv_b[at, row * width : (row + 1) * width] = rest[0, row : row + 1, :]
                out_b[at, :] = rest[0, 2:3, :]
                router[layer] = rest[0, 3:7, :]
                for row in range(8):
                    s_upb[at, row * width : (row + 1) * width] = rest[0, 7 + row : 8 + row, :]
                s_downb[at, :] = rest[0, 15:16, :]
                for row in range(4):
                    e_upb[layer, :, row * width : (row + 1) * width] = biases[row : row + 1, :]
                e_downb[layer] = biases[4:5, :]
            steps = 32.0 * small[2, 0:1, :128] + small[2, 1:2, :128]
            table[...] = table_rows(steps.astype(jnp.int32), small[1])
            spots = lax.broadcasted_iota(jnp.int32, (256, 128), 0) % 8
            lanes = lax.broadcasted_iota(jnp.int32, (256, 128), 1)
            marks = jnp.where(spots == lanes, 1.0, 0.0).astype(BFLOAT)
            numbers = small[2, 0:8, :256].astype(BFLOAT)
            sums = product(numbers, marks)[2:3, :].astype(jnp.int32)
            counts[0:1, :] = sums[:, 0:4]
            counts[1:2, :] = sums[:, 4:8]


def final_call(groups, layer, order, parts, before, hide=()):
    width = parts[0].shape[2]
    outs = [
        (2, 1, width, 4 * width),
        (2, 1, 4 * width, width),
        (32, width),
        (2, width, 8 * width),
        (2, 8 * width, width),
        (2, width, 3 * width),
        (2, width, width),
        (4, 32, width),
    ]
    specs = [
        pl.BlockSpec((None, None, width, width), lambda i, _: (layer, 0, 0, i // 2)),
        pl.BlockSpec((None, None, width, width), lambda i, _: (layer, 0, i // 2, 0)),
        pl.BlockSpec((32, width), lambda i, _: (0, 0)),
        pl.BlockSpec((None, width, width), lambda i, _: (layer, 0, i)),
        pl.BlockSpec((None, width, width), lambda i, _: (layer, i, 0)),
        pl.BlockSpec((None, width, width), lambda i, _: (layer, 0, jnp.minimum(i // 2, 2))),
        pl.BlockSpec((None, width, width), lambda i, _: (layer, 0, 0)),
        pl.BlockSpec((4, 32, width), lambda i, _: (0, 0, 0)),
    ]
    ins = [far(item) for item in parts]
    in_specs = [pl.BlockSpec(memory_space=pltpu.HBM)] * len(parts)
    aliases = {}
    shapes = [jax.ShapeDtypeStruct(shape, FLOAT) for shape in outs]
    if before is not None:
        ins += [before[7], before[2]]
        in_specs += [whole_spec(before[7]), whole_spec(before[2])]
        for number in (0, 1, 3, 4, 5, 6):
            aliases[1 + len(ins)] = number
            ins.append(before[number])
            in_specs.append(pl.BlockSpec(memory_space=pl.ANY))
        rest = [
            (2, 2 * width),
            (2, width),
            (2, 4, width),
            (2, 8 * width),
            (2, width),
            (2, 1, 4 * width),
            (2, 1, width),
            (1000, width),
        ]
        shapes += [jax.ShapeDtypeStruct(shape, FLOAT) for shape in rest]
        shapes += [jax.ShapeDtypeStruct((2, 4), jnp.int32)]
        specs += [
            pl.BlockSpec(item.shape, lambda *_, rank=len(item.shape): (0,) * rank)
            for item in shapes[8:]
        ]
    outs = pl.pallas_call(
        functools.partial(final_body, groups, before is not None),
        out_shape=shapes,
        grid_spec=pltpu.PrefetchScalarGridSpec(
            num_scalar_prefetch=1,
            grid=(8,),
            in_specs=in_specs,
            out_specs=specs,
            scratch_shapes=[
                pltpu.VMEM((2, 4, 2, parts[0].shape[1], width), BFLOAT),
                pltpu.SemaphoreType.DMA((16,)),
            ],
        ),
        input_output_aliases=aliases,
        cost_estimate=pl.CostEstimate(flops=int(8e9), bytes_accessed=16 << 20, transcendentals=0),
        compiler_params=pltpu.CompilerParams(vmem_limit_bytes=50 << 20),
    )(order.place, *ins)
    outs, hide = order.arrive((outs, hide))
    return outs, hide


def extra_plane_body(place, own_a, got_a, own_b, got_b, out_a, out_b):
    y, x = place[1], place[2]
    for other in range(2):
        out_a[2 * other + x] = own_a[other]
        out_a[2 * other + 1 - x] = got_a[other]
        out_b[2 * y + other] = own_b[other]
        out_b[2 * (1 - y) + other] = got_b[other]


class ExtraExpert:
    def __init__(self, layer, order, number, up, down):
        width, units = up.shape[2], up.shape[3]
        some_up = lax.dynamic_slice(
            up, (layer, 0, number * (width // 8), 0), (1, 1, width // 8, units)
        ).reshape(width // 8, units)
        some_down = lax.dynamic_slice(
            down, (layer, 0, number * (units // 8), 0), (1, 1, units // 8, width)
        ).reshape(units // 8, width)
        self.order = order
        self.shapes = [some_up.shape, some_down.shape]
        self.own = [swap(some_up, "expert", 2), swap(some_down, "expert", 2)]

    def across(self, after):
        self.own = [lax.optimization_barrier((item, after))[0] for item in self.own]
        self.got = [swap(self.own[0], "section", 2), swap(self.own[1], "section", 1)]

    def pair(self):
        self.own = self.order.call(
            pair_body,
            [(self.own[0],), (self.got[0],), (self.own[1],), (self.got[1],)],
            [((2,) + shape, BFLOAT) for shape in self.shapes],
            1.7,
        )
        self.got = [swap(self.own[0], "section", 1), swap(self.own[1], "section", 2)]

    def plane(self):
        up, down = self.order.call(
            extra_plane_body,
            [(self.own[0],), (self.got[0],), (self.own[1],), (self.got[1],)],
            [((4,) + shape, BFLOAT) for shape in self.shapes],
            1.7,
        )
        self.all = [up, swap(up, "dp", 1), down, swap(down, "dp", 1)]


def shards_fast(
    tokens,
    timesteps,
    routes_one,
    routes_two,
    cotangent,
    time_table,
    ada_weight,
    ada_bias,
    qkv_weight,
    qv_bias,
    out_weight,
    out_bias,
    router_weight,
    shared_up,
    shared_up_bias,
    shared_down,
    shared_down_bias,
    expert_up,
    expert_up_bias,
    expert_down,
    expert_down_bias,
):
    width = tokens.shape[1]
    rows = tokens.shape[0]
    bf, fl = BFLOAT, FLOAT
    experts_total = router_weight.shape[2]
    core, y, x_bit = bits()
    place = jnp.stack([core, y, x_bit, lax.axis_index("expert")]).astype(jnp.int32)
    routers = jnp.pad(router_weight, ((0, 0), (0, 0), (0, 128 - experts_total)))

    order = Order(place)
    number = core * 4 + y * 2 + x_bit
    hidden_units = expert_up.shape[3]
    first_extra = ExtraExpert(0, order, number, expert_up, expert_down)
    half_steps = ordered(x_bit, timesteps[0], swap(timesteps[0], "section", 1))
    number = lax.optimization_barrier((number, half_steps))[0]
    second_extra = ExtraExpert(1, order, number, expert_up, expert_down)
    steps = ordered(y, half_steps, swap(half_steps, "section", 2)).reshape(4)
    embedded = jnp.take(time_table, steps, axis=0)
    condition = jax.nn.silu(embedded.astype(FLOAT)).astype(BFLOAT)
    section_mod = product(condition, ada_weight[0]) + ada_bias[0].astype(FLOAT)
    mods = lax.all_to_all(section_mod, "section", 0, 0, tiled=True).reshape(12, width)
    first_extra.across(section_mod)
    first_extra.pair()
    own_bias = jnp.concatenate([expert_up_bias[:, 0], expert_down_bias[:, 0]], -1)
    own_bias = lax.optimization_barrier((own_bias, section_mod))[0]
    extra_bias = swap(own_bias, "expert", 2)

    def with_bias(layer, extra):
        bias = extra_bias[layer : layer + 1]
        return [*(far(item) for item in extra.all), bias[:, :hidden_units], bias[:, hidden_units:]]

    weights = (
        far(shared_up),
        shared_up_bias,
        far(shared_down),
        shared_down_bias,
        far(expert_up),
        expert_up_bias,
        far(expert_down),
        expert_down_bias,
    )

    size = rows + 16
    block_outs = [
        ((rows, width), bf, True),
        ((rows, 3 * width), bf, True),
        ((rows, width), bf, True),
        ((rows, width), fl, True),
        ((rows, width), bf, True),
        ((size, width), bf),
        ((rows, 128), fl, True),
    ]

    def attn_ins(layer, routes):
        return [
            (mods,),
            (qkv_weight, layer_spec(qkv_weight, layer)),
            (qv_bias,),
            (out_weight, layer_spec(out_weight, layer)),
            (out_bias,),
            (routers, layer_spec(routers, layer)),
            (routes,),
        ]

    def z(x, by):
        return swap(order.tie(x), "expert", by)

    (hidden0, qkv0, attended0, branch0, stream1, message1, gates1, last_grad), (first_extra.got,) = (
        order.call(
            functools.partial(attention_forward_body, 0),
            [(tokens,), (cotangent,), *attn_ins(0, routes_one)],
            block_outs + [((rows, width), bf)],
            4.2,
            hide=[first_extra.got],
        )
    )
    got1 = swap(message1, "expert", 1)
    first_extra.plane()
    (shared1,), (got1, first_extra.all) = shared_call(
        0, True, False, order, message1, None, weights, hide=[got1, first_extra.all]
    )
    extra0 = with_bias(0, first_extra)
    sent1, kept_got1 = experts_call(
        0, True, False, order, got1, None, None, weights, extra0, None, ()
    )
    back1 = swap(sent1, "expert", 1)
    second_extra.across(sent1)
    (own1, kept_own1), (back1,) = experts_call(
        0, True, False, order, message1, gates1, None, weights, extra0, None, (shared1,),
        hide=[back1],
    )
    got_last = z(last_grad, 1)
    second_extra.pair()
    (stream2, branch1, hidden2, qkv2, attended2, branch2, stream3, message3, gates3), (got_last,) = (
        order.call(
            functools.partial(attention_forward_body, 2),
            [(stream1,), (own1,), (back1,), *attn_ins(1, routes_two)],
            [((rows, width), bf, True), ((rows, width), fl, True)] + block_outs,
            4.2,
            hide=[got_last],
        )
    )
    got3 = swap(message3, "expert", 1)
    second_extra.plane()
    (shared3, shared_grad3), (got3, second_extra.all) = shared_call(
        1, True, True, order, message3, last_grad, weights, hide=[got3, second_extra.all]
    )
    far_last = z(last_grad, 2)
    extra1 = with_bias(1, second_extra)
    (sent3, back_message3), (far_last,) = experts_call(
        1, True, True, order, got3, None, got_last, weights, extra1, None, (), hide=[far_last]
    )
    back_grad3 = swap(back_message3, "expert", 1)
    far3 = z(message3, 2)
    (own3, own_grad3, gate_grad3), (back_grad3, far3) = experts_call(
        1, True, True, order, message3, gates3, last_grad, weights, extra1, None,
        (shared3, shared_grad3), hide=[back_grad3, far3],
    )
    farther_last, farther3 = z(far_last, 1), z(far3, 1)
    grad_outs = [((4, width // 2 + 32, width), bf, True)] * 2 + [((16, width), fl)]
    proj = [pltpu.VMEM((rows, 3 * width), bf)]

    def attn_back_ins(layer):
        return [
            (mods,),
            (routers, layer_spec(routers, layer)),
            (qkv_weight, layer_spec(qkv_weight, layer)),
            (out_weight, layer_spec(out_weight, layer)),
        ]

    groups = Groups(width + 32, width // 2, width // 2 + 32)
    flow1, flow0 = Flow(groups, order, True), Flow(groups, order, True)
    (grad1, branch_grad1, kept_a, sent_a, small1), (farther_last, farther3) = order.call(
        functools.partial(attention_backward_body, 2),
        [
            (item,)
            for item in (
                cotangent, stream3, message3, own_grad3, back_grad3, gates3, gate_grad3,
                stream2, hidden2, qkv2, attended2, branch2,
            )
        ]
        + attn_back_ins(1)
        + [(branch1,)],
        [((rows, width), bf), ((rows, width), bf)] + grad_outs,
        7.7,
        hide=[farther_last, farther3],
        scratch=proj,
    )
    got_grad1 = swap(branch_grad1, "expert", 1)
    (shared_grad1,), (got_grad1,) = shared_call(
        0, False, True, order, message1, branch_grad1, weights, hide=[got_grad1]
    )
    far_grad1, far1, back3 = z(branch_grad1, 2), z(message1, 2), z(sent3, 1)
    (kept, sent), (far_grad1, far1, back3) = weight_grads_call(
        1,
        True,
        True,
        order,
        [(item,) for item in (message3, got3, far3, farther3)],
        [(item,) for item in (last_grad, got_last, far_last, farther_last)],
        weights,
        hide=[far_grad1, far1, back3],
    )
    flow1.add(kept, sent)
    flow1.add(kept_a, sent_a)
    (back_message1,), (flow1.parts[0][1], flow1.parts[1][1]) = experts_call(
        0, False, True, order, got1, None, got_grad1, weights, extra0, kept_got1, (),
        hide=[flow1.parts[0][1], flow1.parts[1][1]],
    )
    back_grad1 = swap(back_message1, "expert", 1)
    flow1.first()
    (own_grad1, gate_grad1), (back_grad1,) = experts_call(
        0, False, True, order, message1, gates1, branch_grad1, weights, extra0, kept_own1,
        (shared_grad1,), hide=[back_grad1],
    )
    farther1, farther_grad1 = z(far1, 1), z(far_grad1, 1)
    (token_grad, kept_a, sent_a, small0), (farther1, farther_grad1) = order.call(
        functools.partial(attention_backward_body, 0),
        [
            (item,)
            for item in (
                grad1, stream1, message1, own_grad1, back_grad1, gates1, gate_grad1,
                tokens, hidden0, qkv0, attended0, branch0,
            )
        ]
        + attn_back_ins(0),
        [((rows, width), fl)] + grad_outs,
        7.7,
        hide=[farther1, farther_grad1],
        scratch=proj,
    )
    flow1.second()

    branch3 = own3 + back3.astype(FLOAT)
    output = (stream3.astype(FLOAT) + mods[11:12] * branch3).astype(BFLOAT)
    gating3 = jnp.sum(cotangent.astype(FLOAT) * branch3, 0, keepdims=True)
    own_condition = jax.nn.silu(lax.dynamic_slice_in_dim(embedded, 2 * y + x_bit, 1).astype(FLOAT))
    own_condition = own_condition.astype(BFLOAT).astype(FLOAT)
    none = jnp.zeros((4, width), FLOAT)
    to_sections = jnp.concatenate(
        [
            small0[3:5], small0[2:3], own_condition, none,
            small0[0:2], small1[5:6], own_condition, none,
            small1[3:5], small1[2:3], own_condition, none,
            small1[0:2], gating3, own_condition, none,
        ]
    )
    to_sections = to_sections.reshape(4, 8, width)
    section = 2 * y + x_bit

    image = core * 4 + lax.axis_index("expert")
    spots = jnp.arange(32)[:, None] == jnp.arange(4)[None, :] * 8 + image
    def counted(route_pair):
        numbers = jnp.arange(experts_total, dtype=jnp.int32)
        return jnp.sum((route_pair.reshape(-1)[:, None] == numbers[None, :]).astype(FLOAT), 0)

    device = section * 8 + image
    counts = jnp.tile(jnp.concatenate([counted(routes_one), counted(routes_two)]), 32)
    places = jnp.arange(width) // (2 * experts_total)
    counts = jnp.where(places == device, jnp.pad(counts, (0, width - 64 * experts_total)), 0.0)
    is_mine = jnp.arange(width) == device
    high, low = timesteps[0] // 32, timesteps[0] % 32
    def toward(by):
        return lax.dynamic_index_in_dim(to_sections, section ^ by, 0, keepdims=False)

    factors = [toward(0)] + [swap(toward(by), "section", by) for by in (1, 2, 3)]
    sources0 = (
        [(item,) for item in (message1, got1, far1, farther1)],
        [(item,) for item in (branch_grad1, got_grad1, far_grad1, farther_grad1)],
    )
    (kept, sent), (factors, flow1.got) = weight_grads_call(
        0, False, True, order, *sources0, weights, hide=[factors, flow1.got]
    )
    flow1.third()
    flow0.add(kept, sent)
    flow0.add(kept_a, sent_a)
    factors = jnp.take(jnp.stack(factors), jnp.arange(4) ^ section, axis=0)
    low_grads = factors[:, :3].reshape(4, 3 * width).astype(BFLOAT)
    condition_grad = back_product(low_grads, ada_weight[0])
    embed_grad = jax.vjp(jax.nn.silu, embedded.astype(FLOAT))[1](condition_grad)[0]
    embed_rows = jnp.sum(jnp.where(spots[:, :, None], embed_grad[None], 0.0), 1)

    misc = jnp.concatenate(
        [
            embed_rows,
            jnp.where(is_mine, high.astype(FLOAT), 0.0)[None],
            jnp.where(is_mine, low.astype(FLOAT), 0.0)[None],
            counts[None],
            jnp.zeros((29, width), FLOAT),
        ]
    )
    got_misc = swap(misc, "dp", 1)
    factors = ordered(core, factors, swap(factors, "dp", 1))
    hidden = [flow0.parts[0][1], flow0.parts[1][1], flow1.columns, got_misc]
    (kept, sent), hidden = weight_grads_call(
        0, True, False, order, *sources0, weights, hide=hidden
    )
    flow0.parts[0][1], flow0.parts[1][1], flow1.columns, got_misc = hidden
    flow0.add(kept, sent)
    flow0.parts = [flow0.parts[2], flow0.parts[0], flow0.parts[1]]
    flow1.relay()
    flow0.first((misc, got_misc))
    flow0.got, flow1.columns, factors = order.arrive((flow0.got, flow1.columns, factors))
    flow0.second()
    spread1 = flow1.column(True)
    flow0.got = order.arrive(flow0.got)
    flow0.third()
    flow0.columns, spread1.got = order.arrive((flow0.columns, spread1.got))
    spread1.pair()
    flow0.relay()
    flow0.columns, spread1.other_own = order.arrive((flow0.columns, spread1.other_own))
    spread0 = flow0.column(True)
    turns = [factors] + [z(factors, by) for by in (2, 1)]
    spread1.got, spread0.got, turns = order.arrive((spread1.got, spread0.got, turns))
    turns = [turns[0], turns[2], turns[1], z(turns[1], 1)]
    spread1.finish()
    spread0.pair()
    spread1.all, spread0.other_own, turns = order.arrive((spread1.all, spread0.other_own, turns))
    turns = jnp.take(jnp.stack(turns), jnp.arange(4) ^ place[3], axis=0)
    factors = turns.reshape(32, 8, width)
    mod_grads = factors[:, :3].reshape(-1, 3 * width)
    ada_out = lead_product(factors[:, 3].astype(BFLOAT), mod_grads.astype(BFLOAT))[None]
    ada_bias_out = jnp.sum(mod_grads, 0)[None]
    finals, (spread0.got, ada_out, ada_bias_out) = final_call(
        groups, 1, order, spread1.all, None, [spread0.got, ada_out, ada_bias_out]
    )
    spread0.finish()
    finals, _ = final_call(groups, 0, order, spread0.all, finals)
    e_up_out, e_down_out, _, s_up_out, s_down_out, qkv_out, out_w_out, _, *rest = finals
    qv_out, out_b_out, router_out, s_upb_out, s_downb_out, *rest = rest
    e_upb_out, e_downb_out, table_out, counts_out = rest
    router_out = router_out.swapaxes(1, 2)

    return (
        output,
        token_grad,
        table_out,
        ada_out,
        ada_bias_out,
        qkv_out,
        qv_out,
        out_w_out,
        out_b_out,
        router_out,
        s_up_out,
        s_upb_out,
        s_down_out,
        s_downb_out,
        e_up_out,
        e_upb_out,
        e_down_out,
        e_downb_out,
        counts_out,
    )


def shards(*args):
    fits = (
        lax.axis_size("section") == 4
        and lax.axis_size("dp") == 2
        and lax.axis_size("expert") == 4
        and args[12].shape[2] == 4
        and args[1].shape[0] == 1
    )
    return (shards_fast if fits else shards_general)(*args)


def solution(mesh):
    rows = P(ALL, None)
    whole = P()
    placed = (
        rows,
        P(ALL),
        rows,
        rows,
        rows,
        whole,
        P("section", None, None),
        P("section", None),
        *([whole] * 9),
        P(None, "expert", None, None),
        P(None, "expert", None),
        P(None, "expert", None, None),
        P(None, "expert", None),
    )
    return jax.shard_map(
        shards,
        mesh=mesh,
        in_specs=placed,
        out_specs=(
            rows,
            rows,
            whole,
            P("section", None, None),
            P("section", None),
            *([whole] * 9),
            P(None, "expert", None, None),
            P(None, "expert", None),
            P(None, "expert", None, None),
            P(None, "expert", None),
            whole,
        ),
        check_vma=False,
    )
```
